32 devices in a mesh: row: 4 (over y, x), col: 8 (over z, core).
Axes of the slice: x: 2, y: 2, z: 4, core: 2. Of those that a mesh axis runs over, the one named last changes fastest.
Arguments:
- features: bfloat16 [16, 1024, 2048], P(None, 'row', 'col'), may hold values from -6 to 6
- conv_weight: bfloat16 [3, 16, 3, 3], replicated, may hold values from -0.5 to 0.5
- bias: float32 [3], replicated, may hold values from -3 to 3
- inv_wavelength: float32 [3], replicated, may hold values from 12 to 18
- distance: float32 [1], replicated, may hold values from 16000 to 32000
Outputs:
- propagated: bfloat16 [3, 2, 1024, 2048], P(None, None, ('row', 'col'))
The draws below stay inside these ranges and needn't reach their ends.
All inputs are finite; a program needn't handle non-finite values.
Results may differ from the reference program's by a relative error of at most 0.0025.
Values may be sent and summed in bfloat16 or wider, within the bound.
No kernel may reach another device: no remote copies, remote signals or barrier semaphores. Data moves between devices by JAX's collectives and lax.ppermute only.
A program may use at most 128 MiB of HBM per device.

```python
import math
import jax
import jax.numpy as jnp
from jax import lax

CH = 16
COLORS = 3
NX = 1024
NY = 2048


def levels(rng, shape, shards, smallest, top_value):
    factor_of, own = 1.0, jax.random.fold_in(rng, 6)
    for dim, blocks in shards:
        steps = jnp.exp(jax.random.uniform(jax.random.fold_in(own, dim), (blocks,), jnp.float32, smallest / len(shards), top_value / len(shards)))
        factor_of = factor_of * jnp.repeat(steps, shape[dim] // blocks).reshape([-1 if axis == dim else 1 for axis in range(len(shape))])
    return factor_of


def gaussian(stream_key, shape, spread, most, cuts=(), kind=jnp.bfloat16):
    array = spread * jax.random.normal(stream_key, shape, jnp.float32)
    if cuts:
        array = array * levels(stream_key, shape, cuts, -0.22, 0.18)
    return jnp.clip(array, -most, most).astype(kind)


def setup_inputs(seed: int = 0) -> dict:
    key_list = jax.random.split(jax.random.key(seed), 6)
    features = gaussian(key_list[0], (CH, NX, NY), 1.0, 6.0, ((1, 4), (2, 8)))
    conv_weight = gaussian(key_list[1], (COLORS, CH, 3, 3), (CH * 9) ** -0.5, 0.5)
    bias = gaussian(key_list[2], (COLORS,), 0.5, 3.0, (), jnp.float32)
    inv_wavelength = jnp.clip(jnp.exp(jax.random.uniform(key_list[3], (COLORS,), jnp.float32, math.log(12.0), math.log(18.0))), 12.0, 18.0)
    distance = jnp.clip(jax.random.uniform(key_list[4], (1,), jnp.float32, 16000.0, 32000.0), 16000.0, 32000.0)
    return {"features": features, "conv_weight": conv_weight, "bias": bias, "inv_wavelength": inv_wavelength, "distance": distance}


def phase_delay(freq_x, freq_y, grid_height, grid_width, wave_inv, travel):
    signed_x = jnp.where(freq_x < grid_height // 2, freq_x, freq_x - grid_height).astype(jnp.float32) / grid_height
    signed_y = jnp.where(freq_y < grid_width // 2, freq_y, freq_y - grid_width).astype(jnp.float32) / grid_width
    squared = signed_x * signed_x + signed_y * signed_y
    factor = 2.0 * math.pi * travel
    return factor * squared / (wave_inv + jnp.sqrt(wave_inv * wave_inv - squared))

def reference(features, conv_weight, bias, inv_wavelength, distance):
    score = lax.conv_general_dilated(features[None], conv_weight, (1, 1), 'SAME', dimension_numbers=('NCHW', 'OIHW', 'NCHW'), preferred_element_type=jnp.float32)[0]
    phase = math.pi * jnp.tanh(score + bias[:, None, None])
    grid_height = phase.shape[1]
    grid_width = phase.shape[2]
    freq_x = jnp.arange(grid_height, dtype=jnp.int32)[:, None]
    freq_y = jnp.arange(grid_width, dtype=jnp.int32)[None, :]
    results = []
    for color_index in range(phase.shape[0]):
        field = lax.complex(jnp.cos(phase[color_index]), jnp.sin(phase[color_index]))
        delay = phase_delay(freq_x, freq_y, grid_height, grid_width, inv_wavelength[color_index], distance[0])
        transfer = lax.complex(jnp.cos(delay), -jnp.sin(delay))
        propagated_field = jnp.fft.ifft2(jnp.fft.fft2(field) * transfer)
        results.append(jnp.stack((jnp.real(propagated_field), jnp.imag(propagated_field)), 0).astype(jnp.bfloat16))
    return jnp.stack(results, 0)
```

```python
from functools import partial
import math

import numpy as np
import jax
import jax.numpy as jnp
from jax import lax
from jax.experimental import pallas as pl
from jax.experimental.pallas import tpu as pltpu
from jax.sharding import PartitionSpec as P

F32 = jnp.float32
BF16 = jnp.bfloat16
TILE = 256
CODE = 124.0
TINY = 1.2e-38
VMEM_LIMIT = 56 * 1024 * 1024


def split_np(table):
    high = table.astype(jnp.bfloat16)
    low = (table - high.astype(np.float64)).astype(jnp.bfloat16)
    return high, low


def dft_np(rows, cols, length):
    product = np.outer(np.arange(rows), np.arange(cols)) % length
    angle = 2.0 * np.pi * product / length
    return np.cos(angle), np.sin(angle)


def interleaved(table, parts):
    rows = table.shape[0]
    return table.reshape(rows, 2, parts, TILE // parts).transpose(0, 2, 1, 3).reshape(rows, 2 * TILE)


def forward_y_np(parts):
    c, s = dft_np(TILE, TILE, TILE)
    full = np.block([[c, -s], [s, c]])
    return split_np(interleaved(full, parts))


def inverse_y_np(parts):
    c, s = dft_np(TILE, TILE, TILE)
    full = np.block([[c, s], [-s, c]])
    return split_np(np.ascontiguousarray(interleaved(full.T.copy(), parts).T))


def stacked_x_np():
    c, s = dft_np(TILE, TILE, TILE)
    return split_np(np.concatenate([c, s], 0))


def sincos_half(t):
    u = t * t
    h = np.pi / 2
    sp = [(-1) ** k * h ** (2 * k + 1) / math.factorial(2 * k + 1) for k in range(6)]
    cp = [(-1) ** k * h ** (2 * k) / math.factorial(2 * k) for k in range(7)]
    s = jnp.full_like(u, sp[-1])
    for coef in sp[-2::-1]:
        s = s * u + coef
    s = s * t
    c = jnp.full_like(u, cp[-1])
    for coef in cp[-2::-1]:
        c = c * u + coef
    return 1.0 - 2.0 * s * s, 2.0 * s * c


def encode(v):
    v2 = v * v
    v4 = v2 * v2
    return (v4 * (v2 * v)).astype(BF16)


def decode(w):
    w = w.astype(F32)
    mag = jnp.exp2(jnp.log2(jnp.maximum(jnp.abs(w), TINY)) * (1.0 / 7.0))
    return jnp.where(w < 0, -mag, mag)


def split(x):
    high = x.astype(BF16)
    return high, (x - high.astype(F32)).astype(BF16)


def dot(a, b):
    return lax.dot_general(a, b, (((1,), (0,)), ((), ())), preferred_element_type=F32)


def lane_shift(x, shift):
    width = x.shape[-1]
    shift = shift % width
    if shift == 0:
        return x
    if width % 128 == 0:
        return pltpu.roll(x, shift, x.ndim - 1)
    return jnp.concatenate([x[..., width - shift :], x[..., : width - shift]], -1)


class Pair:
    def __init__(self, re, im):
        self.re, self.im = re, im

    def __add__(self, o):
        return Pair(self.re + o.re, self.im + o.im)

    def __sub__(self, o):
        return Pair(self.re - o.re, self.im - o.im)

    def turn(self, sign):
        return Pair(-self.im, self.re) if sign > 0 else Pair(self.im, -self.re)

    def times(self, c, s):
        return Pair(self.re * c - self.im * s, self.re * s + self.im * c)


class Lanes:
    def __init__(self, x, sign_row):
        self.x, self.sign_row = x, sign_row

    def __add__(self, o):
        return Lanes(self.x + o.x, self.sign_row)

    def __sub__(self, o):
        return Lanes(self.x - o.x, self.sign_row)

    def turn(self, sign):
        half = lane_shift(self.x, self.x.shape[-1] // 2) * self.sign_row
        return Lanes(half if sign > 0 else -half, self.sign_row)

    def times(self, c, s):
        return Lanes(self.x * c + self.turn(1).x * s, self.sign_row)


def small_dft(items, sign):
    n = len(items)
    if n == 1:
        return items
    even = small_dft(items[0::2], sign)
    odd = small_dft(items[1::2], sign)
    out = [None] * n
    for k in range(n // 2):
        if k == 0:
            o = odd[k]
        elif 4 * k == n:
            o = odd[k].turn(sign)
        else:
            angle = sign * 2.0 * math.pi * k / n
            o = odd[k].times(math.cos(angle), math.sin(angle))
        out[k] = even[k] + o
        out[k + n // 2] = even[k] - o
    return out


def edge_slot(color, part):
    return 8 * (2 * color + part) + 4


def head_kernel(colors, chans, band, feat, halo, taps, expand, spread, masks, bias, out, table):
    step = 16
    rows = feat.shape[1]
    chunks = rows // step
    groups = 3 * colors
    total = None
    for u in range(3):
        wide = dot(expand[...], taps[u]).astype(BF16)
        wide = dot(wide, spread[...]) * masks[u]
        total = wide if total is None else total + wide
    table[...] = total.astype(BF16)
    halo_table = dot(expand[groups * step :, :], taps[2]).astype(BF16)
    lower = dot(expand[groups * step :, :], taps[0]).astype(BF16)

    lane = lax.broadcasted_iota(jnp.int32, (1, TILE), 1)
    keep_left = (lane != 0).astype(F32)
    keep_right = (lane != TILE - 1).astype(F32)
    lane_half = lax.broadcasted_iota(jnp.int32, (1, TILE // 2), 1)
    outer = (lane_half == 0) | (lane_half == TILE // 2 - 1)
    row16 = lax.broadcasted_iota(jnp.int32, (step, 1), 0)

    def combine(q0, q1, q2):
        r0 = pltpu.roll(q0, 1, 1)
        r2 = pltpu.roll(q2, TILE - 1, 1)
        own = q1 + r0 * keep_left + r2 * keep_right
        cross = jnp.where(lane_half == 0, r0[:, : TILE // 2], r2[:, TILE // 2 :])
        return own, cross

    def ring(block, base):
        res = []
        for o in range(colors):
            q = [block[base + v * colors + o : base + v * colors + o + 1] for v in range(3)]
            q = [jnp.broadcast_to(x, (8, TILE)) for x in q]
            own, cross = combine(*q)
            res.append((own[:1], cross[:1]))
        return res

    above = ring(dot(lower, halo[0]), 16)
    below = ring(dot(halo_table, halo[1]), 0)

    def chunk(i):
        block = feat[:, step * i : step * (i + 1), :].reshape(chans * step, TILE)
        prod = dot(table[...], block)
        main = []
        for o in range(colors):
            q = [prod[(v * colors + o) * step : (v * colors + o + 1) * step] for v in range(3)]
            main.append(combine(*q))
        base = groups * step
        return main, ring(prod, base), ring(prod, base + 16)

    def finish(i, main, from_above, from_below):
        extra = jnp.zeros((step, TILE // 2), F32)
        j, r = divmod(step * i, band)
        for o in range(colors):
            own, cross = main[o]
            own = own + jnp.where(row16 == 0, from_above[o][0], 0.0) + jnp.where(row16 == step - 1, from_below[o][0], 0.0)
            cross = cross + jnp.where(row16 == 0, from_above[o][1], 0.0) + jnp.where(row16 == step - 1, from_below[o][1], 0.0)
            own = own + bias[o]
            code = jnp.exp2(CODE * jnp.tanh(own))
            out[j, o * band + r : o * band + r + step, :] = code.astype(BF16)
            edges = jnp.where(lane_half == 0, own[:, : TILE // 2], own[:, TILE // 2 :])
            edges = jnp.where(outer, edges, 0.0) + pltpu.roll(jnp.where(outer, cross, 0.0), 2, 1)
            high = edges.astype(BF16).astype(F32)
            extra = extra + pltpu.roll(high, edge_slot(o, 0), 1) + pltpu.roll(edges - high, edge_slot(o, 1), 1)
        base = colors * band
        if band >= 2 * step:
            half = r // step
            row = base + (half // 2) * step
            start = (half % 2) * (TILE // 2)
            out[j, row : row + step, start : start + TILE // 2] = extra.astype(BF16)
        else:
            out[j, base + r : base + r + step, : TILE // 2] = extra.astype(BF16)
            out[j, base + r : base + r + step, TILE // 2 :] = jnp.zeros((step, TILE // 2), BF16)

    held = chunk(0)
    from_above = above
    for i in range(chunks):
        after = chunk(i + 1) if i + 1 < chunks else None
        from_below = after[1] if after is not None else below
        finish(i, held[0], from_above, from_below)
        from_above = held[2]
        held = after


def head_tables(colors, chans):
    step = 16
    groups = 3 * colors
    rows = groups * step + 32
    expand = np.zeros((rows, 16), np.float32)
    masks = np.zeros((3, rows, chans * step), np.float32)
    spread = np.zeros((chans, chans * step), np.float32)
    x_in = np.tile(np.arange(step), chans)
    for c in range(chans):
        spread[c, c * step : (c + 1) * step] = 1
    for g in range(groups):
        for xo in range(step):
            row = g * step + xo
            expand[row, g] = 1
            for u in range(3):
                masks[u, row] = x_in - xo + 1 == u
        top, bottom = groups * step + g, groups * step + 16 + g
        expand[top, g] = 1
        expand[bottom, g] = 1
        masks[2, top] = x_in == 0
        masks[0, bottom] = x_in == step - 1
    return expand.astype(jnp.bfloat16), spread.astype(jnp.bfloat16), masks


def head(features, halo, conv_weight, bias, band, peers):
    chans, rows, cols = features.shape
    colors = conv_weight.shape[0]
    expand, spread, masks = head_tables(colors, chans)
    taps = conv_weight.transpose(2, 3, 0, 1).reshape(3, 3 * colors, chans)
    taps = jnp.pad(taps, ((0, 0), (0, 16 - 3 * colors), (0, 0)))
    extra = max(16, band // 2)
    vm = pl.BlockSpec(memory_space=pltpu.VMEM)
    return pl.pallas_call(
        partial(head_kernel, colors, chans, band),
        out_shape=jax.ShapeDtypeStruct((peers, colors * band + extra, cols), BF16),
        in_specs=[vm] * 6 + [pl.BlockSpec(memory_space=pltpu.SMEM)],
        out_specs=vm,
        scratch_shapes=[pltpu.VMEM((3 * colors * 16 + 32, chans * 16), BF16)],
        compiler_params=pltpu.CompilerParams(vmem_limit_bytes=VMEM_LIMIT),
        name="conv_head",
    )(features, halo, taps, jnp.asarray(expand), jnp.asarray(spread), jnp.asarray(masks), bias)


def forward_y_kernel(colors, band, parts, coded, m_hi, m_lo, tw_c, tw_s, out, hi, lo):
    peers = coded.shape[0]
    step = 16
    half_lanes = TILE // 2
    lane = lax.broadcasted_iota(jnp.int32, (1, half_lanes), 1)
    for o in range(colors):
        for r in range(0, band, step):
            edge = []
            for p in range(peers):
                base = colors * band
                if band >= 2 * step:
                    half = r // step
                    row = base + (half // 2) * step
                    start = (half % 2) * half_lanes
                else:
                    row, start = base + r, 0
                block = coded[p, row : row + step, start : start + half_lanes].astype(F32)
                edge.append(
                    pltpu.roll(block, half_lanes - edge_slot(o, 0), 1) + pltpu.roll(block, half_lanes - edge_slot(o, 1), 1)
                )
            cross = [pltpu.roll(x, half_lanes - 2, 1) for x in edge]
            zero = jnp.zeros_like(cross[0])
            rows = slice(o * band + r, o * band + r + step)
            fixed = []
            for p in range(peers):
                before = cross[p - 1] if p > 0 else zero
                after = cross[p + 1] if p + 1 < peers else zero
                fixed.append(jnp.tanh(edge[p] + jnp.where(lane < half_lanes // 2, before, after)))
            for h in range(2):
                at = slice(h * half_lanes, (h + 1) * half_lanes)
                items = []
                for p in range(peers):
                    t = jnp.log2(coded[p, rows, at].astype(F32)) * (1.0 / CODE)
                    t = jnp.where(lane == (half_lanes - 1) * h, fixed[p], t)
                    items.append(Pair(*sincos_half(t)))
                items = small_dft(items, -1)
                for k, z in enumerate(items):
                    if k:
                        z = z.times(tw_c[k : k + 1, at], -tw_s[k : k + 1, at])
                    for part, x in enumerate((z.re, z.im)):
                        x_hi, x_lo = split(x)
                        to = slice(part * TILE + h * half_lanes, part * TILE + (h + 1) * half_lanes)
                        hi[k, rows, to] = x_hi
                        lo[k, rows, to] = x_lo
    width = 2 * TILE // parts
    for k in range(peers):
        acc = dot(hi[k], m_hi[...]) + dot(lo[k], m_hi[...]) + dot(hi[k], m_lo[...])
        code = encode(acc)
        for q in range(parts):
            out[parts * k + q] = code[:, q * width : (q + 1) * width]


def forward_y(coded, colors, band, parts):
    peers = coded.shape[0]
    m_hi, m_lo = forward_y_np(parts)
    tw_c, tw_s = dft_np(peers, TILE, peers * TILE)
    vm = pl.BlockSpec(memory_space=pltpu.VMEM)
    return pl.pallas_call(
        partial(forward_y_kernel, colors, band, parts),
        out_shape=jax.ShapeDtypeStruct((peers * parts, colors * band, 2 * TILE // parts), BF16),
        in_specs=[vm] * 5,
        out_specs=vm,
        scratch_shapes=[pltpu.VMEM((peers, colors * band, 2 * TILE), BF16)] * 2,
        compiler_params=pltpu.CompilerParams(vmem_limit_bytes=VMEM_LIMIT),
        name="forward_y",
    )(coded, jnp.asarray(m_hi), jnp.asarray(m_lo), jnp.asarray(tw_c, F32), jnp.asarray(tw_s, F32))


def transfer_kernel(sizes, position, wave, travel, out):
    height, width, parts, peers, block = sizes
    color, k = pl.program_id(0), pl.program_id(1)
    k0 = position[0] // parts
    q = position[0] % parts
    shape = out.shape[2:]
    m = lax.broadcasted_iota(jnp.int32, shape, 0)
    lane = lax.broadcasted_iota(jnp.int32, shape, 1)
    kx = k + (height // TILE) * m
    ky = k0 + peers * (block * q + lane % block)
    sx = jnp.where(kx < height // 2, kx, kx - height).astype(F32) / height
    sy = jnp.where(ky < width // 2, ky, ky - width).astype(F32) / width
    f2 = sx * sx + sy * sy
    a = wave[color]
    turns = travel[0] * f2 / (a + jnp.sqrt(a * a - f2))
    turns = turns - jnp.round(turns)
    turns = jnp.where(lane < block, turns, turns - 0.25)
    turns = turns - jnp.round(turns)
    c, _ = sincos_half(2.0 * turns)
    out[0, 0] = c * (1.0 / height)


def transfer(position, inv_wavelength, distance, sizes):
    height, width, parts, peers, block = sizes
    colors = inv_wavelength.shape[0]
    sm = pl.BlockSpec(memory_space=pltpu.SMEM)
    n = height // TILE
    return pl.pallas_call(
        partial(transfer_kernel, sizes),
        grid=(colors, n),
        out_shape=jax.ShapeDtypeStruct((colors, n, TILE, 2 * block), F32),
        in_specs=[sm] * 3,
        out_specs=pl.BlockSpec((1, 1, TILE, 2 * block), lambda c, k: (c, k, 0, 0)),
        compiler_params=pltpu.CompilerParams(vmem_limit_bytes=VMEM_LIMIT),
        name="transfer",
    )(position, inv_wavelength, distance)


def middle_kernel(coded, table, d_hi, d_lo, tw_c, tw_s, out, f_hi, f_lo):
    n = table.shape[1]
    width = coded.shape[-1]
    block = width // 2
    per = coded.shape[0] // n
    band = coded.shape[2]
    lane = lax.broadcasted_iota(jnp.int32, (1, width), 1)
    sign_row = jnp.where(lane < block, -1.0, 1.0)
    step = 16
    pieces = TILE // step
    for i in range(pieces):
        s, r = divmod(i * step, band)
        items = [Lanes(decode(coded[per * a + s, 0, r : r + step, :]), sign_row) for a in range(n)]
        items = small_dft(items, -1)
        rows = slice(i * step, (i + 1) * step)
        for k, z in enumerate(items):
            if k:
                z = z.times(tw_c[k, rows, :], -tw_s[k, rows, :])
            x_hi, x_lo = split(z.x)
            f_hi[rows, k * width : (k + 1) * width] = x_hi
            f_lo[rows, k * width : (k + 1) * width] = x_lo
    group = max(1, min(n, 256 // width))
    values = [None] * n
    for g in range(0, n, group):
        cols = slice(g * width, (g + group) * width)
        acc = dot(d_hi[...], f_hi[:, cols]) + dot(d_lo[...], f_hi[:, cols]) + dot(d_hi[...], f_lo[:, cols])
        for j in range(group):
            k = g + j
            re = acc[:TILE, j * width : (j + 1) * width]
            im = acc[TILE:, j * width : (j + 1) * width]
            z = Lanes(re, sign_row) + Lanes(im, sign_row).turn(-1)
            t = table[0, k]
            swapped = lane_shift(t, block)
            c = jnp.where(lane < block, t, swapped)
            s = jnp.where(lane < block, swapped, t)
            z = z.times(c, -s)
            x_hi, x_lo = split(z.x)
            f_hi[:, k * width : (k + 1) * width] = x_hi
            f_lo[:, k * width : (k + 1) * width] = x_lo
        acc = dot(d_hi[...], f_hi[:, cols]) + dot(d_lo[...], f_hi[:, cols]) + dot(d_hi[...], f_lo[:, cols])
        for j in range(group):
            k = g + j
            re = acc[:TILE, j * width : (j + 1) * width]
            im = acc[TILE:, j * width : (j + 1) * width]
            z = Lanes(re, sign_row) + Lanes(im, sign_row).turn(1)
            if k:
                z = z.times(tw_c[k], tw_s[k])
            values[k] = z
    for a, z in enumerate(small_dft(values, 1)):
        code = encode(z.x)
        for s in range(per):
            out[per * a + s, 0] = code[s * band : (s + 1) * band]


def middle(coded, table):
    groups, colors, band, width = coded.shape
    n = table.shape[1]
    d_hi, d_lo = stacked_x_np()
    tw_c, tw_s = dft_np(n, TILE, n * TILE)
    tw_c = np.repeat(tw_c[:, :, None], width, 2)
    tw_s = np.repeat(tw_s[:, :, None], width, 2)
    vm = pl.BlockSpec(memory_space=pltpu.VMEM)
    return pl.pallas_call(
        middle_kernel,
        grid=(colors,),
        out_shape=jax.ShapeDtypeStruct(coded.shape, BF16),
        in_specs=[
            pl.BlockSpec((groups, 1, band, width), lambda c: (0, c, 0, 0)),
            pl.BlockSpec((1, n, TILE, width), lambda c: (c, 0, 0, 0)),
            vm,
            vm,
            vm,
            vm,
        ],
        out_specs=pl.BlockSpec((groups, 1, band, width), lambda c: (0, c, 0, 0)),
        scratch_shapes=[pltpu.VMEM((TILE, n * width), BF16)] * 2,
        compiler_params=pltpu.CompilerParams(vmem_limit_bytes=VMEM_LIMIT),
        name="middle_x",
    )(coded, table, jnp.asarray(d_hi), jnp.asarray(d_lo), jnp.asarray(tw_c, F32), jnp.asarray(tw_s, F32))


def inverse_y_kernel(parts, coded, m_hi, m_lo, tw_c, tw_s, out, field):
    peers = tw_c.shape[0]
    colors, band = coded.shape[1], coded.shape[2]
    width = coded.shape[3]
    rows = colors * band
    for k in range(peers):
        z = [decode(coded[parts * k + q].reshape(rows, width)) for q in range(parts)]
        z = jnp.concatenate(z, -1)
        hi, lo = split(z)
        acc = dot(hi, m_hi[...]) + dot(lo, m_hi[...]) + dot(hi, m_lo[...])
        field[k] = acc
    step = 8
    half_lanes = TILE // 2
    scale = 1.0 / (peers * TILE)
    for o in range(colors):
        for r in range(0, band, 16):
            for h in range(2):
                at = slice(h * half_lanes, (h + 1) * half_lanes)
                at_im = slice(TILE + h * half_lanes, TILE + (h + 1) * half_lanes)
                got = slice(o * band + r, o * band + r + 16)
                items = []
                for k in range(peers):
                    z = Pair(field[k, got, at], field[k, got, at_im])
                    items.append(z.times(tw_c[k : k + 1, at] * scale, tw_s[k : k + 1, at] * scale))
                for p, z in enumerate(small_dft(items, 1)):
                    to = slice(p * TILE + h * half_lanes, p * TILE + (h + 1) * half_lanes)
                    out[o, 0, r : r + 16, to] = z.re.astype(BF16)
                    out[o, 1, r : r + 16, to] = z.im.astype(BF16)


def inverse_y(coded, parts):
    groups, colors, band, width = coded.shape
    peers = groups // parts
    m_hi, m_lo = inverse_y_np(parts)
    tw_c, tw_s = dft_np(peers, TILE, peers * TILE)
    vm = pl.BlockSpec(memory_space=pltpu.VMEM)
    return pl.pallas_call(
        partial(inverse_y_kernel, parts),
        out_shape=jax.ShapeDtypeStruct((colors, 2, band, peers * TILE), BF16),
        in_specs=[vm] * 5,
        out_specs=vm,
        scratch_shapes=[pltpu.VMEM((peers, colors * band, 2 * TILE), F32)],
        compiler_params=pltpu.CompilerParams(vmem_limit_bytes=VMEM_LIMIT),
        name="inverse_y",
    )(coded, jnp.asarray(m_hi), jnp.asarray(m_lo), jnp.asarray(tw_c, F32), jnp.asarray(tw_s, F32))


def per_device(features, conv_weight, bias, inv_wavelength, distance):
    mesh_rows = lax.axis_size("row")
    mesh_cols = lax.axis_size("col")
    groups = mesh_rows * mesh_cols
    chans, tile_rows, tile_cols = features.shape
    colors = conv_weight.shape[0]
    band = tile_rows // mesh_cols
    height = tile_rows * mesh_rows
    width = tile_cols * mesh_cols
    block = width // groups
    position = (lax.axis_index("row") * mesh_cols + lax.axis_index("col")).astype(jnp.int32)
    up = [(i, i + 1) for i in range(mesh_rows - 1)]
    down = [(j, i) for i, j in up]
    above = lax.ppermute(features[:, tile_rows - 1, :], "row", up)
    below = lax.ppermute(features[:, 0, :], "row", down)
    coded = head(features, jnp.stack((above, below)), conv_weight, bias, band, mesh_cols)
    coded = lax.all_to_all(coded, "col", split_axis=0, concat_axis=0, tiled=True)
    spectrum = forward_y(coded, colors, band, mesh_rows)
    table = transfer(position[None], inv_wavelength, distance, (height, width, mesh_rows, mesh_cols, block))
    spectrum = lax.all_to_all(spectrum, ("row", "col"), split_axis=0, concat_axis=0, tiled=True)
    back = middle(spectrum.reshape(groups, colors, band, 2 * block), table)
    back = lax.all_to_all(back, ("row", "col"), split_axis=0, concat_axis=0, tiled=True)
    return inverse_y(back, mesh_rows)


def solution(mesh):
    in_specs = (P(None, "row", "col"), P(), P(), P(), P())
    out_specs = P(None, None, ("row", "col"), None)
    return jax.shard_map(
        per_device, mesh=mesh, in_specs=in_specs, out_specs=out_specs, check_vma=False
    )
```

```python
from functools import partial
import math

import numpy as np
import jax
import jax.numpy as jnp
from jax import lax
from jax.experimental import pallas as pl
from jax.experimental.pallas import tpu as pltpu
from jax.sharding import PartitionSpec as P

F32 = jnp.float32
BF16 = jnp.bfloat16
TILE = 256
HALF = 128
CODE = 124.0
TINY = 1.2e-38
VMEM_LIMIT = 20 * 1024 * 1024


def split_np(table):
    high = table.astype(jnp.bfloat16)
    low = (table - high.astype(np.float64)).astype(jnp.bfloat16)
    return high, low


def dft_np(rows, cols, length):
    product = np.outer(np.arange(rows), np.arange(cols)) % length
    angle = 2.0 * np.pi * product / length
    return np.cos(angle), np.sin(angle)


def interleaved(table, parts):
    rows = table.shape[0]
    return table.reshape(rows, 2, parts, HALF // parts).transpose(0, 2, 1, 3).reshape(rows, 2 * HALF)


def complex_np(sign):
    c, s = dft_np(HALF, HALF, HALF)
    return np.block([[c, sign * s], [-sign * s, c]])


def tall(table):
    high, low = split_np(table)
    return np.concatenate([high, high, low], 0)


def wide(table):
    high, low = split_np(table)
    return np.concatenate([high, low, high], 1)


def fitted(func, terms, odd):
    t = np.cos(np.pi * (np.arange(400) + 0.5) / 800)
    powers = np.stack([t ** (2 * k + odd) for k in range(terms)], 1)
    return [float(v) for v in np.linalg.lstsq(powers, func(np.pi / 2 * t), rcond=None)[0]]


def sincos_half(t, terms=5, scale=1.0):
    u = t * t
    sines = [v * scale ** (2 * k + 1) for k, v in enumerate(fitted(np.sin, terms, 1))]
    cosines = [v * scale ** (2 * k) for k, v in enumerate(fitted(np.cos, terms, 0))]
    s = sines[-1]
    for coef in sines[-2::-1]:
        s = s * u + coef
    s = s * t
    c = cosines[-1]
    for coef in cosines[-2::-1]:
        c = c * u + coef
    s2 = s + s
    return 1.0 - s2 * s, s2 * c


def log2(x):
    return lax.log(x) * (1.0 / math.log(2.0))


def encode(v):
    v2 = v * v
    return (v2 * v2 * v).astype(BF16)


def decode(w):
    w = w.astype(F32)
    return w * jnp.exp2(lax.log(jnp.maximum(jnp.abs(w), TINY)) * (-0.8 / math.log(2.0)))


def fetch(copies):
    for copy in copies:
        copy.start()
    return copies


def split(x):
    high = x.astype(BF16)
    return high, (x - high.astype(F32)).astype(BF16)


def dot(a, b):
    return lax.dot_general(a, b, (((1,), (0,)), ((), ())), preferred_element_type=F32)


def lane_shift(x, shift):
    width = x.shape[-1]
    shift = shift % width
    if shift == 0:
        return x
    if width % 128 == 0:
        return pltpu.roll(x, shift, x.ndim - 1)
    return jnp.concatenate([x[..., width - shift :], x[..., : width - shift]], -1)


class Pair:
    def __init__(self, re, im):
        self.re, self.im = re, im

    def __add__(self, o):
        return Pair(self.re + o.re, self.im + o.im)

    def __sub__(self, o):
        return Pair(self.re - o.re, self.im - o.im)

    def times(self, c, s):
        return Pair(self.re * c - self.im * s, self.re * s + self.im * c)


def butterfly(even, odd, k, n, sign):
    if k == 0:
        return even + odd, even - odd
    if 4 * k == n:
        plus = Pair(even.re - odd.im, even.im + odd.re)
        minus = Pair(even.re + odd.im, even.im - odd.re)
        return (plus, minus) if sign > 0 else (minus, plus)
    if 8 * k in (n, 3 * n):
        h = math.sqrt(0.5)
        a, b = (odd.re - odd.im) * h, (odd.re + odd.im) * h
        if sign > 0 and 8 * k == n:
            return Pair(even.re + a, even.im + b), Pair(even.re - a, even.im - b)
        if sign > 0:
            return Pair(even.re - b, even.im + a), Pair(even.re + b, even.im - a)
        if 8 * k == n:
            return Pair(even.re + b, even.im - a), Pair(even.re - b, even.im + a)
        return Pair(even.re - a, even.im - b), Pair(even.re + a, even.im + b)
    angle = sign * 2.0 * math.pi * k / n
    o = odd.times(math.cos(angle), math.sin(angle))
    return even + o, even - o


def small_dft(items, sign):
    n = len(items)
    if n == 1:
        return items
    even = small_dft(items[0::2], sign)
    odd = small_dft(items[1::2], sign)
    out = [None] * n
    for k in range(n // 2):
        out[k], out[k + n // 2] = butterfly(even[k], odd[k], k, n, sign)
    return out


def edge_slot(color, part):
    return 16 * color + 8 * part


def head_kernel(colors, chans, band, place, feat, above, below, taps, expand, spread, masks, bias, *rest):
    out, table = rest
    peers = out.shape[0]
    step = 16
    per = band // step
    groups = 3 * colors
    main_rows = groups * step
    me = place[0]
    for v in range(3):
        total = None
        for u in range(3):
            tall_taps = dot(expand[...], taps[u, v]).astype(BF16)
            part = dot(tall_taps, spread[...]) * masks[u].astype(F32)
            total = part if total is None else total + part
        main = colors * step
        table[v * main : (v + 1) * main, :] = total[:main].astype(BF16)
        ring = colors * 8
        start = main_rows + v * ring
        table[start : start + ring, :] = total[main:].astype(BF16)

    lane = lax.broadcasted_iota(jnp.int32, (1, TILE), 1)
    lane_half = lax.broadcasted_iota(jnp.int32, (1, HALF), 1)
    outer = (lane_half == 0) | (lane_half == HALF - 1)
    sub = lax.broadcasted_iota(jnp.int32, (8, 1), 0)

    first, last = sub == 0, sub == 7

    def outside(u, source):
        pieces = [dot(expand[colors * step :, :], taps[u, v]).astype(BF16) for v in range(3)]
        return [dot(piece, source) for piece in pieces]

    def ring_of(block):
        return [block[v * 8 * colors : (v + 1) * 8 * colors] for v in range(3)]

    def chunk(i):
        return feat[:, i * step : (i + 1) * step, :].reshape(chans * step, TILE)

    prods = [None] * (peers * per)
    rings = [None] * (peers * per + 2)
    rings[0] = outside(0, above[...])
    rings[-1] = outside(2, below[...])

    def multiply(j):
        for i in range(j * per, (j + 1) * per):
            prods[i] = dot(table[...], chunk(i))
            rings[i + 1] = ring_of(prods[i][main_rows:])

    def finish(j):
        slot = me ^ j
        total = None
        for i in range(per):
            at = j * per + i
            extra = None
            for o in range(colors):
                q = []
                for v in range(3):
                    g = v * colors + o
                    main = prods[at][g * step : (g + 1) * step]
                    top = main[:8] + jnp.where(first, rings[at][v][8 * o : 8 * o + 8], 0.0)
                    bottom = main[8:] + jnp.where(last, rings[at + 2][v][8 * o : 8 * o + 8], 0.0)
                    q.append(jnp.concatenate([top, bottom], 0))
                r0 = pltpu.roll(q[0], 1, 1)
                r2 = pltpu.roll(q[2], TILE - 1, 1)
                own = q[1] + jnp.where(lane == 0, 0.0, r0) + jnp.where(lane == TILE - 1, 0.0, r2) + bias[o]
                code = jnp.exp2(CODE * jnp.tanh(own)).astype(BF16)
                row = o * band + i * step
                for h in range(2):
                    start = h * colors * band + row
                    out[slot, start : start + step, :] = code[:, h * HALF : (h + 1) * HALF]
                cross = jnp.where(lane_half == 0, r0[:, :HALF], r2[:, HALF:])
                cross = pltpu.roll(jnp.where(outer, cross, 0.0), 2, 1)
                edges = jnp.where(lane_half == 0, own[:, :HALF], own[:, HALF:])
                edges = jnp.where(outer, edges, cross)
                high = edges.astype(BF16).astype(F32)
                both = high + pltpu.roll(edges - high, edge_slot(0, 1), 1)
                shift = edge_slot(o, 0) + 64 * i
                if shift:
                    both = pltpu.roll(both, shift, 1)
                extra = both if extra is None else extra + both
            total = extra if total is None else total + extra
        base = 2 * colors * band
        out[slot, base : base + step, :] = total.astype(BF16)

    multiply(0)
    for j in range(peers):
        if j + 1 < peers:
            multiply(j + 1)
        finish(j)


def head_tables(colors, chans):
    step = 16
    rows = colors * (step + 8)
    expand = np.zeros((rows, colors), np.float32)
    masks = np.zeros((3, rows, chans * step), np.float32)
    spread = np.zeros((chans, chans * step), np.float32)
    x_in = np.tile(np.arange(step), chans)
    for c in range(chans):
        spread[c, c * step : (c + 1) * step] = 1
    for o in range(colors):
        for xo in range(step):
            row = o * step + xo
            expand[row, o] = 1
            for u in range(3):
                masks[u, row] = x_in - xo + 1 == u
        base = colors * step + 8 * o
        expand[base, o] = 1
        expand[base + 7, o] = 1
        masks[0, base] = x_in == step - 1
        masks[2, base + 7] = x_in == 0
    return tuple(x.astype(jnp.bfloat16) for x in (expand, spread, masks))


def head(features, above, below, taps, bias, place, band, peers):
    chans, rows, cols = features.shape
    colors = bias.shape[0]
    expand, spread, masks = head_tables(colors, chans)
    vm = pl.BlockSpec(memory_space=pltpu.VMEM)
    sm = pl.BlockSpec(memory_space=pltpu.SMEM)
    return pl.pallas_call(
        partial(head_kernel, colors, chans, band),
        out_shape=jax.ShapeDtypeStruct((peers, 2 * colors * band + 16, HALF), BF16),
        in_specs=[sm] + [vm] * 7 + [sm],
        out_specs=vm,
        scratch_shapes=[pltpu.VMEM((3 * colors * 24, chans * 16), BF16)],
        compiler_params=pltpu.CompilerParams(vmem_limit_bytes=VMEM_LIMIT),
        name="conv_head",
    )(place, features, above, below, taps, jnp.asarray(expand), jnp.asarray(spread), jnp.asarray(masks), bias)


def forward_y_kernel(colors, band, parts, place, *refs):
    peers = len(refs) - 6
    matrix, tw_c, tw_s, out, coded, left = refs[peers:]
    for k in range(peers):
        coded[place[0] ^ k] = refs[k][...]
    step = 16
    lane = lax.broadcasted_iota(jnp.int32, (1, HALF), 1)
    for o in range(colors):
        for r in range(0, band, step):
            edge = []
            for p in range(peers):
                base = 2 * colors * band
                block = coded[p, base : base + step, :].astype(F32)
                shift = edge_slot(o, 0) + 64 * (r // step)
                if shift:
                    block = pltpu.roll(block, HALF - shift, 1)
                edge.append(block + pltpu.roll(block, HALF - edge_slot(0, 1), 1))
            cross = [pltpu.roll(x, HALF - 2, 1) for x in edge]
            zero = jnp.zeros_like(cross[0])
            fixed = []
            for p in range(peers):
                before = cross[p - 1] if p > 0 else zero
                after = cross[p + 1] if p + 1 < peers else zero
                fixed.append(CODE * jnp.tanh(edge[p] + jnp.where(lane < HALF // 2, before, after)))
            items = []
            for p in range(peers):
                for h in range(2):
                    start = (h * colors + o) * band + r
                    t = log2(coded[p, start : start + step, :].astype(F32))
                    t = jnp.where(lane == (HALF - 1) * h, fixed[p], t)
                    items.append(Pair(*sincos_half(t, 4, 1.0 / CODE)))
            for k, z in enumerate(small_dft(items, -1)):
                if k:
                    z = z.times(tw_c[k : k + 1, :], -tw_s[k : k + 1, :])
                for part, x in enumerate((z.re, z.im)):
                    high, low = split(x)
                    for j, value in enumerate((high, low, high)):
                        to = slice((2 * j + part) * HALF, (2 * j + part + 1) * HALF)
                        left[o, k, r : r + step, to] = value
        width = TILE // parts
        acc = dot(left[o].reshape(2 * peers * band, 3 * TILE), matrix[...])
        code = encode(acc)
        for k in range(2 * peers):
            for q in range(parts):
                out[parts * k + q, o * band : (o + 1) * band, :] = code[k * band : (k + 1) * band, q * width : (q + 1) * width]


def forward_y(blocks, place, colors, band, parts):
    peers = len(blocks)
    tw_c, tw_s = dft_np(2 * peers, HALF, peers * TILE)
    vm = pl.BlockSpec(memory_space=pltpu.VMEM)
    sm = pl.BlockSpec(memory_space=pltpu.SMEM)
    matrix = tall(interleaved(complex_np(-1), parts))
    return pl.pallas_call(
        partial(forward_y_kernel, colors, band, parts),
        out_shape=jax.ShapeDtypeStruct((2 * peers * parts, colors * band, TILE // parts), BF16),
        in_specs=[sm] + [vm] * (peers + 3),
        out_specs=vm,
        scratch_shapes=[
            pltpu.VMEM((peers,) + blocks[0].shape, BF16),
            pltpu.VMEM((colors, 2 * peers, band, 3 * TILE), BF16),
        ],
        compiler_params=pltpu.CompilerParams(vmem_limit_bytes=VMEM_LIMIT),
        name="forward_y",
    )(place, *blocks, jnp.asarray(matrix), jnp.asarray(tw_c, F32), jnp.asarray(tw_s, F32))


def transfer_kernel(sizes, position, wave, travel, out):
    height, width, parts, inner, block = sizes
    color, k = pl.program_id(0), pl.program_id(1)
    k0 = position[0] // parts
    q = position[0] % parts
    shape = out.shape[3:]
    m = lax.broadcasted_iota(jnp.int32, shape, 0)
    lane = lax.broadcasted_iota(jnp.int32, shape, 1)
    kx = 2 * k + lane // block + (height // HALF) * m
    ky = k0 + inner * (block * q + lane % block)
    sx = jnp.where(kx < height // 2, kx, kx - height).astype(F32) / height
    sy = jnp.where(ky < width // 2, ky, ky - width).astype(F32) / width
    f2 = sx * sx + sy * sy
    a = wave[color]
    turns = travel[0] * f2 / (a + jnp.sqrt(a * a - f2))
    turns = turns - jnp.round(turns)
    c, s = sincos_half(2.0 * turns)
    out[0, 0, 0] = c * (1.0 / height)
    out[0, 0, 1] = s * (1.0 / height)


def transfer(position, inv_wavelength, distance, sizes):
    height, width, parts, inner, block = sizes
    colors = inv_wavelength.shape[0]
    sm = pl.BlockSpec(memory_space=pltpu.SMEM)
    n = height // TILE
    return pl.pallas_call(
        partial(transfer_kernel, sizes),
        grid=(colors, n),
        out_shape=jax.ShapeDtypeStruct((colors, n, 2, HALF, 2 * block), F32),
        in_specs=[sm] * 3,
        out_specs=pl.BlockSpec((1, 1, 2, HALF, 2 * block), lambda c, k: (c, k, 0, 0, 0)),
        compiler_params=pltpu.CompilerParams(vmem_limit_bytes=VMEM_LIMIT),
        name="transfer",
    )(position, inv_wavelength, distance)


def middle_kernel(coded, tables, forward, inverse, tw_c, tw_s, out, right):
    for color in range(tables.shape[0]):
        middle_color(coded.at[:, color], tables.at[color], forward, inverse, tw_c, tw_s, out.at[:, color], right.at[color])


def middle_color(coded, table, forward, inverse, tw_c, tw_s, out, right):
    n = table.shape[0]
    width = coded.shape[-1]
    block = width // 2
    per = coded.shape[0] // (2 * n)
    band = coded.shape[1]
    lane = lax.broadcasted_iota(jnp.int32, (1, width), 1)
    left = lane < block
    step = 16
    turn_c = [jnp.where(left, 1.0, math.cos(math.pi * a / n)) for a in range(n)]
    turn_s = [jnp.where(left, 0.0, math.sin(math.pi * a / n)) for a in range(n)]

    def put(k, rows, z):
        for part, x in enumerate((z.re, z.im)):
            high, low = split(x)
            for j, value in enumerate((high, high, low)):
                to = (2 * j + part) * HALF
                right[to + rows.start : to + rows.stop, k * width : (k + 1) * width] = value

    for i in range(HALF // step):
        s, r = divmod(i * step, band)
        rows = slice(i * step, (i + 1) * step)
        items = []
        for a in range(n):
            x = decode(coded[per * a + s, r : r + step, :])
            y = decode(coded[per * (a + n) + s, r : r + step, :])
            u, v = x + y, x - y
            z = Pair(jnp.where(left, u, lane_shift(v, block)), jnp.where(left, lane_shift(u, block), v))
            if a:
                z = z.times(turn_c[a], -turn_s[a])
            items.append(z)
        for k, z in enumerate(small_dft(items, -1)):
            put(k, rows, z.times(tw_c[k, rows, :], -tw_s[k, rows, :]))
    acc = dot(forward[...], right[...])
    for k in range(n):
        cols = slice(k * width, (k + 1) * width)
        z = Pair(acc[:HALF, cols], acc[HALF:, cols])
        put(k, slice(0, HALF), z.times(table[k, 0], -table[k, 1]))
    acc = dot(inverse[...], right[...])
    for i in range(HALF // step):
        s, r = divmod(i * step, band)
        rows = slice(i * step, (i + 1) * step)
        items = []
        for k in range(n):
            cols = slice(k * width, (k + 1) * width)
            z = Pair(acc[rows, cols], acc[HALF + rows.start : HALF + rows.stop, cols])
            items.append(z.times(tw_c[k, rows, :], tw_s[k, rows, :]))
        for a, z in enumerate(small_dft(items, 1)):
            if a:
                z = z.times(turn_c[a], turn_s[a])
            u = jnp.where(left, z.re, lane_shift(z.im, block))
            v = jnp.where(left, lane_shift(z.re, block), z.im)
            out[per * a + s, r : r + step, :] = encode(u + v)
            out[per * (a + n) + s, r : r + step, :] = encode(u - v)


def middle(coded, table):
    groups, colors, band, width = coded.shape
    n = table.shape[1]
    tw_c, tw_s = dft_np(2 * n, HALF, 2 * n * HALF)
    tw_c, tw_s = (np.repeat(x.reshape(n, 2, HALF).transpose(0, 2, 1), width // 2, 2) for x in (tw_c, tw_s))
    vm = pl.BlockSpec(memory_space=pltpu.VMEM)
    forward = wide(complex_np(-1).T)
    inverse = wide(complex_np(1).T)
    return pl.pallas_call(
        middle_kernel,
        out_shape=jax.ShapeDtypeStruct(coded.shape, BF16),
        in_specs=[vm] * 6,
        out_specs=vm,
        scratch_shapes=[pltpu.VMEM((colors, 3 * TILE, n * width), BF16)],
        compiler_params=pltpu.CompilerParams(vmem_limit_bytes=VMEM_LIMIT),
        name="middle_x",
    )(coded, table, jnp.asarray(forward), jnp.asarray(inverse), jnp.asarray(tw_c, F32), jnp.asarray(tw_s, F32))


def inverse_y_kernel(parts, coded, matrix, tw_c, tw_s, target, left, out, sems):
    inner = tw_c.shape[0]
    colors, band, width = coded.shape[1], coded.shape[2], coded.shape[3]
    outs = []
    step = 16
    scale = 1.0 / (inner * HALF)
    for o in range(colors):
        for k in range(inner):
            for q in range(parts):
                high, low = split(decode(coded[parts * k + q, o]))
                for j, value in enumerate((high, low, high)):
                    left[o, k, :, j * TILE + q * width : j * TILE + (q + 1) * width] = value
        acc = dot(left[o].reshape(inner * band, 3 * TILE), matrix[...])
        for r in range(0, band, step):
            items = []
            for k in range(inner):
                z = acc[k * band + r : k * band + r + step]
                items.append(Pair(z[:, :HALF], z[:, HALF:]).times(tw_c[k : k + 1, :] * scale, tw_s[k : k + 1, :] * scale))
            for a, z in enumerate(small_dft(items, 1)):
                out[o, 0, r : r + step, a * HALF : (a + 1) * HALF] = z.re.astype(BF16)
                out[o, 1, r : r + step, a * HALF : (a + 1) * HALF] = z.im.astype(BF16)
        outs += fetch([pltpu.make_async_copy(out.at[o], target.at[o], sems.at[o])])
    for copy in outs:
        copy.wait()


def inverse_y(coded, parts):
    groups, colors, band, width = coded.shape
    inner = groups // parts
    tw_c, tw_s = dft_np(inner, HALF, inner * HALF)
    matrix = tall(np.ascontiguousarray(interleaved(complex_np(1).T.copy(), parts).T))
    hbm = pl.BlockSpec(memory_space=pltpu.HBM)
    vm = pl.BlockSpec(memory_space=pltpu.VMEM)
    return pl.pallas_call(
        partial(inverse_y_kernel, parts),
        out_shape=jax.ShapeDtypeStruct((colors, 2, band, inner * HALF), BF16),
        in_specs=[vm] * 4,
        out_specs=hbm,
        scratch_shapes=[
            pltpu.VMEM((colors, inner, band, 3 * TILE), BF16),
            pltpu.VMEM((colors, 2, band, inner * HALF), BF16),
            pltpu.SemaphoreType.DMA((colors,)),
        ],
        compiler_params=pltpu.CompilerParams(vmem_limit_bytes=VMEM_LIMIT),
        name="inverse_y",
    )(coded, jnp.asarray(matrix), jnp.asarray(tw_c, F32), jnp.asarray(tw_s, F32))


def per_device(features, conv_weight, bias, inv_wavelength, distance):
    mesh_rows = lax.axis_size("row")
    mesh_cols = lax.axis_size("col")
    groups = mesh_rows * mesh_cols
    chans, tile_rows, tile_cols = features.shape
    colors = conv_weight.shape[0]
    band = tile_rows // mesh_cols
    height = tile_rows * mesh_rows
    width = tile_cols * mesh_cols
    block = width // groups
    parts = mesh_rows // 2
    position = (lax.axis_index("row") * mesh_cols + lax.axis_index("col")).astype(jnp.int32)
    up = [(i, i + 1) for i in range(mesh_rows - 1)]
    down = [(j, i) for i, j in up]
    above = lax.ppermute(features[:, tile_rows - 1, :], "row", up)
    below = lax.ppermute(features[:, 0, :], "row", down)
    taps = conv_weight.transpose(2, 3, 0, 1)
    place = lax.axis_index("col").astype(jnp.int32)[None]
    bands = head(features, above, below, taps, bias, place, band, mesh_cols)
    blocks = [bands[0]]
    for k in range(1, mesh_cols):
        blocks.append(lax.ppermute(bands[k], "col", [(i, i ^ k) for i in range(mesh_cols)]))
    spectrum = forward_y(blocks, place, colors, band, parts)
    table = transfer(position[None], inv_wavelength, distance, (height, width, parts, 2 * mesh_cols, block))
    spectrum = lax.all_to_all(spectrum, ("row", "col"), split_axis=0, concat_axis=0, tiled=True)
    back = middle(spectrum.reshape(groups, colors, band, 2 * block), table)
    back = lax.all_to_all(back, ("row", "col"), split_axis=0, concat_axis=0, tiled=True)
    return inverse_y(back, parts)


def solution(mesh):
    in_specs = (P(None, "row", "col"), P(), P(), P(), P())
    out_specs = P(None, None, ("row", "col"), None)
    return jax.shard_map(
        per_device, mesh=mesh, in_specs=in_specs, out_specs=out_specs, check_vma=False
    )
```

```python
from functools import partial
import math

import numpy as np
import jax
import jax.numpy as jnp
from jax import lax
from jax.experimental import pallas as pl
from jax.experimental.pallas import tpu as pltpu
from jax.sharding import PartitionSpec as P

F32 = jnp.float32
BF16 = jnp.bfloat16
TILE = 256
HALF = 128
CODE = 124.0
TINY = 1.2e-38
VMEM_LIMIT = 10 * 1024 * 1024


def split_np(table):
    high = table.astype(jnp.bfloat16)
    low = (table - high.astype(np.float64)).astype(jnp.bfloat16)
    return high, low


def dft_np(rows, cols, length):
    product = np.outer(np.arange(rows), np.arange(cols)) % length
    angle = 2.0 * np.pi * product / length
    return np.cos(angle), np.sin(angle)


def interleaved(table, parts):
    rows = table.shape[0]
    return table.reshape(rows, 2, parts, HALF // parts).transpose(0, 2, 1, 3).reshape(rows, 2 * HALF)


def complex_np(sign):
    c, s = dft_np(HALF, HALF, HALF)
    return np.block([[c, sign * s], [-sign * s, c]])


def tall(table):
    high, low = split_np(table)
    return np.concatenate([high, high, low], 0)


def wide(table):
    high, low = split_np(table)
    return np.concatenate([high, low, high], 1)


def fitted(func, terms, odd):
    t = np.cos(np.pi * (np.arange(400) + 0.5) / 800)
    powers = np.stack([t ** (2 * k + odd) for k in range(terms)], 1)
    return [float(v) for v in np.linalg.lstsq(powers, func(np.pi / 2 * t), rcond=None)[0]]


def sincos_half(t, terms=5, scale=1.0):
    u = t * t
    sines = [v * scale ** (2 * k + 1) for k, v in enumerate(fitted(np.sin, terms, 1))]
    cosines = [v * scale ** (2 * k) for k, v in enumerate(fitted(np.cos, terms, 0))]
    s = sines[-1]
    for coef in sines[-2::-1]:
        s = s * u + coef
    s = s * t
    c = cosines[-1]
    for coef in cosines[-2::-1]:
        c = c * u + coef
    s2 = s + s
    return 1.0 - s2 * s, s2 * c


def log2(x):
    return lax.log(x) * (1.0 / math.log(2.0))


def encode(v):
    v2 = v * v
    return (v2 * v2 * v).astype(BF16)


def decode(w):
    w = w.astype(F32)
    return w * jnp.exp2(lax.log(jnp.maximum(jnp.abs(w), TINY)) * (-0.8 / math.log(2.0)))


def fetch(copies):
    for copy in copies:
        copy.start()
    return copies


def split(x):
    high = x.astype(BF16)
    return high, (x - high.astype(F32)).astype(BF16)


def dot(a, b):
    return lax.dot_general(a, b, (((1,), (0,)), ((), ())), preferred_element_type=F32)


def lane_shift(x, shift):
    width = x.shape[-1]
    shift = shift % width
    if shift == 0:
        return x
    if width % 128 == 0:
        return pltpu.roll(x, shift, x.ndim - 1)
    return jnp.concatenate([x[..., width - shift :], x[..., : width - shift]], -1)


class Pair:
    def __init__(self, re, im):
        self.re, self.im = re, im

    def __add__(self, o):
        return Pair(self.re + o.re, self.im + o.im)

    def __sub__(self, o):
        return Pair(self.re - o.re, self.im - o.im)

    def times(self, c, s):
        return Pair(self.re * c - self.im * s, self.re * s + self.im * c)


def butterfly(even, odd, k, n, sign):
    if k == 0:
        return even + odd, even - odd
    if 4 * k == n:
        plus = Pair(even.re - odd.im, even.im + odd.re)
        minus = Pair(even.re + odd.im, even.im - odd.re)
        return (plus, minus) if sign > 0 else (minus, plus)
    if 8 * k in (n, 3 * n):
        h = math.sqrt(0.5)
        a, b = (odd.re - odd.im) * h, (odd.re + odd.im) * h
        if sign > 0 and 8 * k == n:
            return Pair(even.re + a, even.im + b), Pair(even.re - a, even.im - b)
        if sign > 0:
            return Pair(even.re - b, even.im + a), Pair(even.re + b, even.im - a)
        if 8 * k == n:
            return Pair(even.re + b, even.im - a), Pair(even.re - b, even.im + a)
        return Pair(even.re - a, even.im - b), Pair(even.re + a, even.im + b)
    angle = sign * 2.0 * math.pi * k / n
    o = odd.times(math.cos(angle), math.sin(angle))
    return even + o, even - o


def small_dft(items, sign):
    n = len(items)
    if n == 1:
        return items
    even = small_dft(items[0::2], sign)
    odd = small_dft(items[1::2], sign)
    out = [None] * n
    for k in range(n // 2):
        out[k], out[k + n // 2] = butterfly(even[k], odd[k], k, n, sign)
    return out


def edge_slot(color, part):
    return 16 * color + 8 * part


def prepare_kernel(colors, chans, feat, weight, bias, tile, first_edge, second_edge, table, ring_table, bias_rows, edge, taps, bias_in, sems):
    step = 16
    rows = feat.shape[1]
    copies = fetch(
        [
            pltpu.make_async_copy(weight, taps, sems.at[0]),
            pltpu.make_async_copy(bias, bias_in, sems.at[1]),
            pltpu.make_async_copy(feat.at[:, pl.ds(0, step), :], edge.at[0], sems.at[2]),
            pltpu.make_async_copy(feat.at[:, pl.ds(rows - step, step), :], edge.at[1], sems.at[3]),
        ]
        + [
            pltpu.make_async_copy(feat.at[pl.ds(i * (chans // 8), chans // 8)], tile.at[pl.ds(i * (chans // 8), chans // 8)], sems.at[4 + i])
            for i in range(8)
        ]
    )
    copies[0].wait()
    wide = chans * step
    c_of = lax.broadcasted_iota(jnp.int32, (chans, wide), 1) // step
    spread = (c_of == lax.broadcasted_iota(jnp.int32, (chans, wide), 0)).astype(F32).astype(BF16)
    x_in = lax.broadcasted_iota(jnp.int32, (step + 8, wide), 1) % step
    row = lax.broadcasted_iota(jnp.int32, (step + 8, wide), 0)
    masks = []
    for u in range(3):
        main = (row < step) & (x_in - row + 1 == u)
        if u == 0:
            main = main | ((row == step) & (x_in == step - 1))
        if u == 2:
            main = main | ((row == step + 7) & (x_in == 0))
        masks.append(main)
    sub = lax.broadcasted_iota(jnp.int32, (8, chans), 0)
    for o in range(colors):
        spreads = [dot(taps[o, u], spread) for u in range(3)]
        small = [taps[o, u].astype(F32) for u in range(3)]
        for v in range(3):
            total = jnp.zeros((step + 8, wide), F32)
            for u in range(3):
                total = total + jnp.where(masks[u], spreads[u][v : v + 1], 0.0)
            g = v * colors + o
            table[g * step : (g + 1) * step, :] = total[:step].astype(BF16)
            start = 3 * colors * step + 8 * g
            table[start : start + 8, :] = total[step:].astype(BF16)
            ring_table[0, 8 * g : 8 * g + 8, :] = jnp.where(sub == 0, small[0][v : v + 1], 0.0).astype(BF16)
            ring_table[1, 8 * g : 8 * g + 8, :] = jnp.where(sub == 7, small[2][v : v + 1], 0.0).astype(BF16)
    copies[1].wait()
    for o in range(colors):
        bias_rows[o : o + 1, :] = jnp.full((1, TILE), bias_in[o], F32)
    copies[2].wait()
    copies[3].wait()
    top = edge[0].astype(F32)[:, 0, :]
    bottom = edge[1].astype(F32)[:, step - 1, :]
    even = lax.axis_index("row") % 2 == 0
    first_edge[...] = jnp.where(even, bottom, top).astype(BF16)
    second_edge[...] = jnp.where(even, top, bottom).astype(BF16)
    for copy in copies[4:]:
        copy.wait()


def prepare(features, conv_weight, bias):
    chans, rows, cols = features.shape
    colors = bias.shape[0]
    weight = conv_weight.transpose(0, 2, 3, 1)
    hbm = pl.BlockSpec(memory_space=pltpu.HBM)
    vm = pl.BlockSpec(memory_space=pltpu.VMEM)
    return pl.pallas_call(
        partial(prepare_kernel, colors, chans),
        out_shape=[
            pltpu.VMEM(features.shape, BF16),
            pltpu.VMEM((chans, cols), BF16),
            pltpu.VMEM((chans, cols), BF16),
            pltpu.VMEM((3 * colors * 24, chans * 16), BF16),
            pltpu.VMEM((2, 3 * colors * 8, chans), BF16),
            pltpu.VMEM((colors, TILE), F32),
        ],
        in_specs=[hbm] * 3,
        out_specs=[vm] * 6,
        scratch_shapes=[
            pltpu.VMEM((2, chans, 16, cols), BF16),
            pltpu.VMEM(weight.shape, BF16),
            pltpu.SMEM(bias.shape, F32),
            pltpu.SemaphoreType.DMA((12,)),
        ],
        compiler_params=pltpu.CompilerParams(vmem_limit_bytes=VMEM_LIMIT),
        name="prepare",
    )(*(pltpu.with_memory_space_constraint(x, pltpu.HBM) for x in (features, weight, bias)))


def head_kernel(colors, chans, band, feat, first_halo, second_halo, table, ring_table, bias, out):
    peers = out.shape[0]
    step = 16
    per = band // step
    groups = 3 * colors
    main_rows = groups * step
    me = lax.axis_index("col")

    lane = lax.broadcasted_iota(jnp.int32, (1, TILE), 1)
    lane_half = lax.broadcasted_iota(jnp.int32, (1, HALF), 1)
    outer = (lane_half == 0) | (lane_half == HALF - 1)
    sub = lax.broadcasted_iota(jnp.int32, (8, 1), 0)

    first, last = sub == 0, sub == 7

    def ring_of(block):
        return [block[v * 8 * colors : (v + 1) * 8 * colors] for v in range(3)]

    def chunk(i):
        return feat[:, i * step : (i + 1) * step, :].reshape(chans * step, TILE)

    prods = [None] * (peers * per)
    rings = [None] * (peers * per + 2)
    even = lax.axis_index("row") % 2 == 0
    one, two = first_halo[...].astype(F32), second_halo[...].astype(F32)
    above = jnp.where(even, two, one).astype(BF16)
    below = jnp.where(even, one, two).astype(BF16)
    rings[0] = ring_of(dot(ring_table[0], above))
    rings[-1] = ring_of(dot(ring_table[1], below))

    def multiply(j):
        for i in range(j * per, (j + 1) * per):
            prods[i] = dot(table[...], chunk(i))
            rings[i + 1] = ring_of(prods[i][main_rows:])

    def finish(j):
        slot = me ^ j
        total = None
        for i in range(per):
            at = j * per + i
            extra = None
            for o in range(colors):
                q = []
                for v in range(3):
                    g = v * colors + o
                    main = prods[at][g * step : (g + 1) * step]
                    top = main[:8] + jnp.where(first, rings[at][v][8 * o : 8 * o + 8], 0.0)
                    bottom = main[8:] + jnp.where(last, rings[at + 2][v][8 * o : 8 * o + 8], 0.0)
                    q.append(jnp.concatenate([top, bottom], 0))
                r0 = pltpu.roll(q[0], 1, 1)
                r2 = pltpu.roll(q[2], TILE - 1, 1)
                own = q[1] + jnp.where(lane == 0, 0.0, r0) + jnp.where(lane == TILE - 1, 0.0, r2) + bias[o : o + 1, :]
                code = jnp.exp2(CODE * jnp.tanh(own)).astype(BF16)
                row = o * band + i * step
                for h in range(2):
                    start = h * colors * band + row
                    out[slot, start : start + step, :] = code[:, h * HALF : (h + 1) * HALF]
                cross = jnp.where(lane_half == 0, r0[:, :HALF], r2[:, HALF:])
                cross = pltpu.roll(jnp.where(outer, cross, 0.0), 2, 1)
                edges = jnp.where(lane_half == 0, own[:, :HALF], own[:, HALF:])
                edges = jnp.where(outer, edges, cross)
                high = edges.astype(BF16).astype(F32)
                both = high + pltpu.roll(edges - high, edge_slot(0, 1), 1)
                shift = edge_slot(o, 0) + 64 * i
                if shift:
                    both = pltpu.roll(both, shift, 1)
                extra = both if extra is None else extra + both
            total = extra if total is None else total + extra
        base = 2 * colors * band
        out[slot, base : base + step, :] = total.astype(BF16)

    multiply(0)
    for j in range(peers):
        if j + 1 < peers:
            multiply(j + 1)
        finish(j)


def head(prepared, above, below, band, peers):
    features, table, ring_table, bias = prepared
    chans, rows, cols = features.shape
    colors = bias.shape[0]
    vm = pl.BlockSpec(memory_space=pltpu.VMEM)
    return pl.pallas_call(
        partial(head_kernel, colors, chans, band),
        out_shape=pltpu.VMEM((peers, 2 * colors * band + 16, HALF), BF16),
        in_specs=[vm] * 6,
        out_specs=vm,
        compiler_params=pltpu.CompilerParams(vmem_limit_bytes=VMEM_LIMIT),
        name="conv_head",
    )(features, above, below, table, ring_table, bias)


def forward_y_kernel(colors, band, parts, *refs):
    peers = len(refs) - 6
    matrix, tw_c, tw_s, out, coded, left = refs[peers:]
    for k in range(peers):
        coded[lax.axis_index("col") ^ k] = refs[k][...]
    step = 16
    lane = lax.broadcasted_iota(jnp.int32, (1, HALF), 1)
    for o in range(colors):
        for r in range(0, band, step):
            edge = []
            for p in range(peers):
                base = 2 * colors * band
                block = coded[p, base : base + step, :].astype(F32)
                shift = edge_slot(o, 0) + 64 * (r // step)
                if shift:
                    block = pltpu.roll(block, HALF - shift, 1)
                edge.append(block + pltpu.roll(block, HALF - edge_slot(0, 1), 1))
            cross = [pltpu.roll(x, HALF - 2, 1) for x in edge]
            zero = jnp.zeros_like(cross[0])
            fixed = []
            for p in range(peers):
                before = cross[p - 1] if p > 0 else zero
                after = cross[p + 1] if p + 1 < peers else zero
                fixed.append(CODE * jnp.tanh(edge[p] + jnp.where(lane < HALF // 2, before, after)))
            items = []
            for p in range(peers):
                for h in range(2):
                    start = (h * colors + o) * band + r
                    t = log2(coded[p, start : start + step, :].astype(F32))
                    t = jnp.where(lane == (HALF - 1) * h, fixed[p], t)
                    items.append(Pair(*sincos_half(t, 4, 1.0 / CODE)))
            for k, z in enumerate(small_dft(items, -1)):
                if k:
                    z = z.times(tw_c[k : k + 1, :], -tw_s[k : k + 1, :])
                for part, x in enumerate((z.re, z.im)):
                    high, low = split(x)
                    for j, value in enumerate((high, low, high)):
                        to = slice((2 * j + part) * HALF, (2 * j + part + 1) * HALF)
                        left[o, k, r : r + step, to] = value
        width = TILE // parts
        acc = dot(left[o].reshape(2 * peers * band, 3 * TILE), matrix[...])
        code = encode(acc)
        for k in range(2 * peers):
            for q in range(parts):
                out[parts * k + q, o * band : (o + 1) * band, :] = code[k * band : (k + 1) * band, q * width : (q + 1) * width]


def forward_y(blocks, colors, band, parts):
    peers = len(blocks)
    tw_c, tw_s = dft_np(2 * peers, HALF, peers * TILE)
    vm = pl.BlockSpec(memory_space=pltpu.VMEM)
    sm = pl.BlockSpec(memory_space=pltpu.SMEM)
    matrix = tall(interleaved(complex_np(-1), parts))
    return pl.pallas_call(
        partial(forward_y_kernel, colors, band, parts),
        out_shape=pltpu.VMEM((2 * peers * parts, colors * band, TILE // parts), BF16),
        in_specs=[vm] * (peers + 3),
        out_specs=vm,
        scratch_shapes=[
            pltpu.VMEM((peers,) + blocks[0].shape, BF16),
            pltpu.VMEM((colors, 2 * peers, band, 3 * TILE), BF16),
        ],
        compiler_params=pltpu.CompilerParams(vmem_limit_bytes=VMEM_LIMIT),
        name="forward_y",
    )(*blocks, jnp.asarray(matrix), jnp.asarray(tw_c, F32), jnp.asarray(tw_s, F32))


def transfer_kernel(sizes, wave, travel, out):
    height, width, parts, inner, block = sizes
    color, k = pl.program_id(0), pl.program_id(1)
    position = lax.axis_index("row") * lax.axis_size("col") + lax.axis_index("col")
    k0 = position // parts
    q = position % parts
    shape = out.shape[3:]
    m = lax.broadcasted_iota(jnp.int32, shape, 0)
    lane = lax.broadcasted_iota(jnp.int32, shape, 1)
    kx = 2 * k + lane // block + (height // HALF) * m
    ky = k0 + inner * (block * q + lane % block)

    @pl.when(color < wave.shape[0])
    def _():
        sx = jnp.where(kx < height // 2, kx, kx - height).astype(F32) / height
        sy = jnp.where(ky < width // 2, ky, ky - width).astype(F32) / width
        f2 = sx * sx + sy * sy
        a = wave[jnp.minimum(color, wave.shape[0] - 1)]
        turns = travel[0] * f2 / (a + jnp.sqrt(a * a - f2))
        turns = turns - jnp.round(turns)
        c, s = sincos_half(2.0 * turns)
        out[0, 0, 0] = c * (1.0 / height)
        out[0, 0, 1] = s * (1.0 / height)

    @pl.when(color == wave.shape[0])
    def _():
        turns = ((2 * k + lane // block) * m).astype(F32) * (1.0 / height)
        c, s = sincos_half(2.0 * (turns - jnp.round(turns)))
        out[0, 0, 0] = c
        out[0, 0, 1] = s


def transfer(inv_wavelength, distance, sizes):
    height, width, parts, inner, block = sizes
    colors = inv_wavelength.shape[0]
    sm = pl.BlockSpec(memory_space=pltpu.SMEM)
    n = height // TILE
    return pl.pallas_call(
        partial(transfer_kernel, sizes),
        grid=(colors + 1, n),
        out_shape=jax.ShapeDtypeStruct((colors + 1, n, 2, HALF, 2 * block), F32),
        in_specs=[sm] * 2,
        out_specs=pl.BlockSpec((1, 1, 2, HALF, 2 * block), lambda c, k: (c, k, 0, 0, 0)),
        compiler_params=pltpu.CompilerParams(vmem_limit_bytes=VMEM_LIMIT),
        name="transfer",
    )(inv_wavelength, distance)


def middle_kernel(coded, tables, matrix, out, right):
    colors = out.shape[1]
    for color in range(colors):
        middle_color(
            coded.at[:, color], tables.at[color], matrix, tables.at[colors], out.at[:, color], right.at[color]
        )


def middle_color(coded, table, matrix, twiddles, out, right):
    n = table.shape[0]
    width = coded.shape[-1]
    block = width // 2
    per = coded.shape[0] // (2 * n)
    band = coded.shape[1]
    lane = lax.broadcasted_iota(jnp.int32, (1, width), 1)
    left = lane < block
    step = 16
    turn_c = [jnp.where(left, 1.0, math.cos(math.pi * a / n)) for a in range(n)]
    turn_s = [jnp.where(left, 0.0, math.sin(math.pi * a / n)) for a in range(n)]

    def put(k, rows, z, order):
        for part, x in zip(order, (z.re, z.im)):
            high, low = split(x)
            for j, value in enumerate((high, high, low)):
                to = (2 * j + part) * HALF
                right[to + rows.start : to + rows.stop, k * width : (k + 1) * width] = value

    for i in range(HALF // step):
        s, r = divmod(i * step, band)
        rows = slice(i * step, (i + 1) * step)
        items = []
        for a in range(n):
            x = decode(coded[per * a + s, r : r + step, :])
            y = decode(coded[per * (a + n) + s, r : r + step, :])
            u, v = x + y, x - y
            z = Pair(jnp.where(left, u, lane_shift(v, block)), jnp.where(left, lane_shift(u, block), v))
            if a:
                z = z.times(turn_c[a], -turn_s[a])
            items.append(z)
        for k, z in enumerate(small_dft(items, -1)):
            put(k, rows, z.times(twiddles[k, 0, rows, :], -twiddles[k, 1, rows, :]), (0, 1))
    acc = dot(matrix[...], right[...])
    for k in range(n):
        cols = slice(k * width, (k + 1) * width)
        z = Pair(acc[:HALF, cols], acc[HALF:, cols])
        put(k, slice(0, HALF), z.times(table[k, 0], -table[k, 1]), (1, 0))
    acc = dot(matrix[...], right[...])
    for i in range(HALF // step):
        s, r = divmod(i * step, band)
        rows = slice(i * step, (i + 1) * step)
        items = []
        for k in range(n):
            cols = slice(k * width, (k + 1) * width)
            z = Pair(acc[HALF + rows.start : HALF + rows.stop, cols], acc[rows, cols])
            items.append(z.times(twiddles[k, 0, rows, :], twiddles[k, 1, rows, :]))
        for a, z in enumerate(small_dft(items, 1)):
            if a:
                z = z.times(turn_c[a], turn_s[a])
            u = jnp.where(left, z.re, lane_shift(z.im, block))
            v = jnp.where(left, lane_shift(z.re, block), z.im)
            out[per * a + s, r : r + step, :] = encode(u + v)
            out[per * (a + n) + s, r : r + step, :] = encode(u - v)


def middle(coded, table):
    groups, colors, band, width = coded.shape
    n = table.shape[1]
    vm = pl.BlockSpec(memory_space=pltpu.VMEM)
    forward = wide(complex_np(-1).T)
    return pl.pallas_call(
        middle_kernel,
        out_shape=jax.ShapeDtypeStruct(coded.shape, BF16),
        in_specs=[vm] * 3,
        out_specs=vm,
        scratch_shapes=[pltpu.VMEM((colors, 3 * TILE, n * width), BF16)],
        compiler_params=pltpu.CompilerParams(vmem_limit_bytes=VMEM_LIMIT),
        name="middle_x",
    )(*(pltpu.with_memory_space_constraint(x, pltpu.VMEM) for x in (coded, table, jnp.asarray(forward))))


def inverse_y_kernel(parts, coded, matrix, tw_c, tw_s, target, left, out, sems):
    inner = tw_c.shape[0]
    colors, band, width = coded.shape[1], coded.shape[2], coded.shape[3]
    outs = []
    step = 16
    scale = 1.0 / (inner * HALF)
    for o in range(colors):
        for k in range(inner):
            for q in range(parts):
                high, low = split(decode(coded[parts * k + q, o]))
                for j, value in enumerate((high, low, high)):
                    left[o, k, :, j * TILE + q * width : j * TILE + (q + 1) * width] = value
        acc = dot(left[o].reshape(inner * band, 3 * TILE), matrix[...])
        for r in range(0, band, step):
            items = []
            for k in range(inner):
                z = acc[k * band + r : k * band + r + step]
                items.append(Pair(z[:, :HALF], z[:, HALF:]).times(tw_c[k : k + 1, :] * scale, tw_s[k : k + 1, :] * scale))
            for a, z in enumerate(small_dft(items, 1)):
                out[o, 0, r : r + step, a * HALF : (a + 1) * HALF] = z.re.astype(BF16)
                out[o, 1, r : r + step, a * HALF : (a + 1) * HALF] = z.im.astype(BF16)
        outs += fetch([pltpu.make_async_copy(out.at[o], target.at[o], sems.at[o])])
    for copy in outs:
        copy.wait()


def inverse_y(coded, parts):
    groups, colors, band, width = coded.shape
    inner = groups // parts
    tw_c, tw_s = dft_np(inner, HALF, inner * HALF)
    matrix = tall(np.ascontiguousarray(interleaved(complex_np(1).T.copy(), parts).T))
    hbm = pl.BlockSpec(memory_space=pltpu.HBM)
    vm = pl.BlockSpec(memory_space=pltpu.VMEM)
    return pl.pallas_call(
        partial(inverse_y_kernel, parts),
        out_shape=jax.ShapeDtypeStruct((colors, 2, band, inner * HALF), BF16),
        in_specs=[vm] * 4,
        out_specs=hbm,
        scratch_shapes=[
            pltpu.VMEM((colors, inner, band, 3 * TILE), BF16),
            pltpu.VMEM((colors, 2, band, inner * HALF), BF16),
            pltpu.SemaphoreType.DMA((colors,)),
        ],
        compiler_params=pltpu.CompilerParams(vmem_limit_bytes=VMEM_LIMIT),
        name="inverse_y",
    )(coded, jnp.asarray(matrix), jnp.asarray(tw_c, F32), jnp.asarray(tw_s, F32))


def per_device(features, conv_weight, bias, inv_wavelength, distance):
    mesh_rows = lax.axis_size("row")
    mesh_cols = lax.axis_size("col")
    groups = mesh_rows * mesh_cols
    chans, tile_rows, tile_cols = features.shape
    colors = conv_weight.shape[0]
    band = tile_rows // mesh_cols
    height = tile_rows * mesh_rows
    width = tile_cols * mesh_cols
    block = width // groups
    parts = mesh_rows // 2
    tile, edge_one, edge_two, *prepared = prepare(features, conv_weight, bias)
    halos = []
    for start, edge in ((0, edge_one), (1, edge_two)):
        pairs = [(i, i + 1) for i in range(start, mesh_rows - 1, 2)]
        halos.append(lax.ppermute(edge, "row", pairs + [(j, i) for i, j in pairs]))
    bands = head((tile, *prepared), *halos, band, mesh_cols)
    blocks = [bands[0]] * mesh_cols
    for k in range(mesh_cols - 1, 0, -1):
        blocks[k] = lax.ppermute(bands[k], "col", [(i, i ^ k) for i in range(mesh_cols)])
    spectrum = forward_y(blocks, colors, band, parts)
    table = transfer(inv_wavelength, distance, (height, width, parts, 2 * mesh_cols, block))
    spectrum = lax.all_to_all(spectrum, ("row", "col"), split_axis=0, concat_axis=0, tiled=True)
    back = middle(spectrum.reshape(groups, colors, band, 2 * block), table)
    back = lax.all_to_all(back, ("row", "col"), split_axis=0, concat_axis=0, tiled=True)
    return inverse_y(back, parts)


def solution(mesh):
    in_specs = (P(None, "row", "col"), P(), P(), P(), P())
    out_specs = P(None, None, ("row", "col"), None)
    return jax.shard_map(
        per_device, mesh=mesh, in_specs=in_specs, out_specs=out_specs, check_vma=False
    )
```

```python
from functools import partial
import math

import numpy as np
import jax
import jax.numpy as jnp
from jax import lax
from jax.experimental import pallas as pl
from jax.experimental.pallas import tpu as pltpu
from jax.sharding import PartitionSpec as P

F32 = jnp.float32
BF16 = jnp.bfloat16
TILE = 256
HALF = 128
CODE = 124.0
TINY = 1.2e-38
VMEM_LIMIT = 10 * 1024 * 1024


def split_np(table):
    high = table.astype(jnp.bfloat16)
    low = (table - high.astype(np.float64)).astype(jnp.bfloat16)
    return high, low


def dft_np(rows, cols, length):
    product = np.outer(np.arange(rows), np.arange(cols)) % length
    angle = 2.0 * np.pi * product / length
    return np.cos(angle), np.sin(angle)


def interleaved(table, parts):
    rows = table.shape[0]
    return table.reshape(rows, 2, parts, HALF // parts).transpose(0, 2, 1, 3).reshape(rows, 2 * HALF)


def complex_np(sign):
    c, s = dft_np(HALF, HALF, HALF)
    return np.block([[c, sign * s], [-sign * s, c]])


def tall(table):
    high, low = split_np(table)
    return np.concatenate([high, high, low], 0)


def wide(table):
    high, low = split_np(table)
    return np.concatenate([high, low, high], 1)


def fitted(func, terms, odd):
    t = np.cos(np.pi * (np.arange(400) + 0.5) / 800)
    powers = np.stack([t ** (2 * k + odd) for k in range(terms)], 1)
    return [float(v) for v in np.linalg.lstsq(powers, func(np.pi / 2 * t), rcond=None)[0]]


def sincos_half(t, terms=5, scale=1.0):
    u = t * t
    sines = [v * scale ** (2 * k + 1) for k, v in enumerate(fitted(np.sin, terms, 1))]
    cosines = [v * scale ** (2 * k) for k, v in enumerate(fitted(np.cos, terms, 0))]
    s = sines[-1]
    for coef in sines[-2::-1]:
        s = s * u + coef
    s = s * t
    c = cosines[-1]
    for coef in cosines[-2::-1]:
        c = c * u + coef
    s2 = s + s
    return 1.0 - s2 * s, s2 * c


def log2(x):
    return lax.log(x) * (1.0 / math.log(2.0))


def encode(v):
    v2 = v * v
    return (v2 * v2 * v).astype(BF16)


def decode(w):
    w = w.astype(F32)
    return w * jnp.exp2(lax.log(jnp.maximum(jnp.abs(w), TINY)) * (-0.8 / math.log(2.0)))


def fetch(copies):
    for copy in copies:
        copy.start()
    return copies


def split(x):
    high = x.astype(BF16)
    return high, (x - high.astype(F32)).astype(BF16)


def dot(a, b):
    return lax.dot_general(a, b, (((1,), (0,)), ((), ())), preferred_element_type=F32)


def lane_shift(x, shift):
    width = x.shape[-1]
    shift = shift % width
    if shift == 0:
        return x
    if width % 128 == 0:
        return pltpu.roll(x, shift, x.ndim - 1)
    return jnp.concatenate([x[..., width - shift :], x[..., : width - shift]], -1)


class Pair:
    def __init__(self, re, im):
        self.re, self.im = re, im

    def __add__(self, o):
        return Pair(self.re + o.re, self.im + o.im)

    def __sub__(self, o):
        return Pair(self.re - o.re, self.im - o.im)

    def times(self, c, s):
        return Pair(self.re * c - self.im * s, self.re * s + self.im * c)


def butterfly(even, odd, k, n, sign):
    if k == 0:
        return even + odd, even - odd
    if 4 * k == n:
        plus = Pair(even.re - odd.im, even.im + odd.re)
        minus = Pair(even.re + odd.im, even.im - odd.re)
        return (plus, minus) if sign > 0 else (minus, plus)
    if 8 * k in (n, 3 * n):
        h = math.sqrt(0.5)
        a, b = (odd.re - odd.im) * h, (odd.re + odd.im) * h
        if sign > 0 and 8 * k == n:
            return Pair(even.re + a, even.im + b), Pair(even.re - a, even.im - b)
        if sign > 0:
            return Pair(even.re - b, even.im + a), Pair(even.re + b, even.im - a)
        if 8 * k == n:
            return Pair(even.re + b, even.im - a), Pair(even.re - b, even.im + a)
        return Pair(even.re - a, even.im - b), Pair(even.re + a, even.im + b)
    angle = sign * 2.0 * math.pi * k / n
    o = odd.times(math.cos(angle), math.sin(angle))
    return even + o, even - o


def small_dft(items, sign):
    n = len(items)
    if n == 1:
        return items
    even = small_dft(items[0::2], sign)
    odd = small_dft(items[1::2], sign)
    out = [None] * n
    for k in range(n // 2):
        out[k], out[k + n // 2] = butterfly(even[k], odd[k], k, n, sign)
    return out


def edge_slot(color, part):
    return 16 * color + 8 * part


def prepare_kernel(colors, chans, feat, weight, bias, tile, first_edge, second_edge, table, ring_table, bias_rows, edge, taps, bias_in, sems):
    step = 16
    rows = feat.shape[1]
    copies = fetch(
        [
            pltpu.make_async_copy(weight, taps, sems.at[0]),
            pltpu.make_async_copy(bias, bias_in, sems.at[1]),
            pltpu.make_async_copy(feat.at[:, pl.ds(0, step), :], edge.at[0], sems.at[2]),
            pltpu.make_async_copy(feat.at[:, pl.ds(rows - step, step), :], edge.at[1], sems.at[3]),
        ]
        + [
            pltpu.make_async_copy(feat.at[pl.ds(i * (chans // 8), chans // 8)], tile.at[pl.ds(i * (chans // 8), chans // 8)], sems.at[4 + i])
            for i in range(8)
        ]
    )
    copies[0].wait()
    wide = chans * step
    c_of = lax.broadcasted_iota(jnp.int32, (chans, wide), 1) // step
    spread = (c_of == lax.broadcasted_iota(jnp.int32, (chans, wide), 0)).astype(F32).astype(BF16)
    x_in = lax.broadcasted_iota(jnp.int32, (step + 8, wide), 1) % step
    row = lax.broadcasted_iota(jnp.int32, (step + 8, wide), 0)
    masks = []
    for u in range(3):
        main = (row < step) & (x_in - row + 1 == u)
        if u == 0:
            main = main | ((row == step) & (x_in == step - 1))
        if u == 2:
            main = main | ((row == step + 7) & (x_in == 0))
        masks.append(main)
    sub = lax.broadcasted_iota(jnp.int32, (8, chans), 0)
    for o in range(colors):
        spreads = [dot(taps[o, u], spread) for u in range(3)]
        small = [taps[o, u].astype(F32) for u in range(3)]
        for v in range(3):
            total = jnp.zeros((step + 8, wide), F32)
            for u in range(3):
                total = total + jnp.where(masks[u], spreads[u][v : v + 1], 0.0)
            g = v * colors + o
            table[g * step : (g + 1) * step, :] = total[:step].astype(BF16)
            start = 3 * colors * step + 8 * g
            table[start : start + 8, :] = total[step:].astype(BF16)
            ring_table[0, 8 * g : 8 * g + 8, :] = jnp.where(sub == 0, small[0][v : v + 1], 0.0).astype(BF16)
            ring_table[1, 8 * g : 8 * g + 8, :] = jnp.where(sub == 7, small[2][v : v + 1], 0.0).astype(BF16)
    copies[1].wait()
    for o in range(colors):
        bias_rows[o : o + 1, :] = jnp.full((1, TILE), bias_in[o], F32)
    copies[2].wait()
    copies[3].wait()
    top = edge[0].astype(F32)[:, 0, :]
    bottom = edge[1].astype(F32)[:, step - 1, :]
    even = lax.axis_index("row") % 2 == 0
    first_edge[...] = jnp.where(even, bottom, top).astype(BF16)
    second_edge[...] = jnp.where(even, top, bottom).astype(BF16)
    for copy in copies[4:]:
        copy.wait()


def prepare(features, conv_weight, bias):
    chans, rows, cols = features.shape
    colors = bias.shape[0]
    weight = conv_weight.transpose(0, 2, 3, 1)
    hbm = pl.BlockSpec(memory_space=pltpu.HBM)
    vm = pl.BlockSpec(memory_space=pltpu.VMEM)
    return pl.pallas_call(
        partial(prepare_kernel, colors, chans),
        out_shape=[
            pltpu.VMEM(features.shape, BF16),
            pltpu.VMEM((chans, cols), BF16),
            pltpu.VMEM((chans, cols), BF16),
            pltpu.VMEM((3 * colors * 24, chans * 16), BF16),
            pltpu.VMEM((2, 3 * colors * 8, chans), BF16),
            pltpu.VMEM((colors, TILE), F32),
        ],
        in_specs=[hbm] * 3,
        out_specs=[vm] * 6,
        scratch_shapes=[
            pltpu.VMEM((2, chans, 16, cols), BF16),
            pltpu.VMEM(weight.shape, BF16),
            pltpu.SMEM(bias.shape, F32),
            pltpu.SemaphoreType.DMA((12,)),
        ],
        compiler_params=pltpu.CompilerParams(vmem_limit_bytes=VMEM_LIMIT),
        name="prepare",
    )(*(pltpu.with_memory_space_constraint(x, pltpu.HBM) for x in (features, weight, bias)))


def head_kernel(colors, chans, band, second_halo, first_halo, feat, table, ring_table, bias, out):
    peers = out.shape[0]
    step = 16
    per = band // step
    groups = 3 * colors
    main_rows = groups * step
    me = lax.axis_index("col")

    lane = lax.broadcasted_iota(jnp.int32, (1, TILE), 1)
    lane_half = lax.broadcasted_iota(jnp.int32, (1, HALF), 1)
    outer = (lane_half == 0) | (lane_half == HALF - 1)
    sub = lax.broadcasted_iota(jnp.int32, (8, 1), 0)

    first, last = sub == 0, sub == 7

    def ring_of(block):
        return [block[v * 8 * colors : (v + 1) * 8 * colors] for v in range(3)]

    def chunk(i):
        return feat[:, i * step : (i + 1) * step, :].reshape(chans * step, TILE)

    prods = [None] * (peers * per)
    rings = [None] * (peers * per + 2)
    even = lax.axis_index("row") % 2 == 0
    one, two = first_halo[...].astype(F32), second_halo[...].astype(F32)
    above = jnp.where(even, two, one).astype(BF16)
    below = jnp.where(even, one, two).astype(BF16)
    rings[0] = ring_of(dot(ring_table[0], above))
    rings[-1] = ring_of(dot(ring_table[1], below))

    def multiply(j):
        for i in range(j * per, (j + 1) * per):
            prods[i] = dot(table[...], chunk(i))
            rings[i + 1] = ring_of(prods[i][main_rows:])

    def finish(j):
        slot = me ^ j
        total = None
        for i in range(per):
            at = j * per + i
            extra = None
            for o in range(colors):
                q = []
                for v in range(3):
                    g = v * colors + o
                    main = prods[at][g * step : (g + 1) * step]
                    top = main[:8] + jnp.where(first, rings[at][v][8 * o : 8 * o + 8], 0.0)
                    bottom = main[8:] + jnp.where(last, rings[at + 2][v][8 * o : 8 * o + 8], 0.0)
                    q.append(jnp.concatenate([top, bottom], 0))
                r0 = pltpu.roll(q[0], 1, 1)
                r2 = pltpu.roll(q[2], TILE - 1, 1)
                own = q[1] + jnp.where(lane == 0, 0.0, r0) + jnp.where(lane == TILE - 1, 0.0, r2) + bias[o : o + 1, :]
                code = jnp.exp2(CODE * jnp.tanh(own)).astype(BF16)
                row = o * band + i * step
                for h in range(2):
                    start = h * colors * band + row
                    out[slot, start : start + step, :] = code[:, h * HALF : (h + 1) * HALF]
                cross = jnp.where(lane_half == 0, r0[:, :HALF], r2[:, HALF:])
                cross = pltpu.roll(jnp.where(outer, cross, 0.0), 2, 1)
                edges = jnp.where(lane_half == 0, own[:, :HALF], own[:, HALF:])
                edges = jnp.where(outer, edges, cross)
                high = edges.astype(BF16).astype(F32)
                both = high + pltpu.roll(edges - high, edge_slot(0, 1), 1)
                shift = edge_slot(o, 0) + 64 * i
                if shift:
                    both = pltpu.roll(both, shift, 1)
                extra = both if extra is None else extra + both
            total = extra if total is None else total + extra
        base = 2 * colors * band
        out[slot, base : base + step, :] = total.astype(BF16)

    multiply(0)
    for j in range(peers):
        if j + 1 < peers:
            multiply(j + 1)
        finish(j)


def head(prepared, second_halo, first_halo, band, peers):
    features, table, ring_table, bias = prepared
    chans, rows, cols = features.shape
    colors = bias.shape[0]
    vm = pl.BlockSpec(memory_space=pltpu.VMEM)
    return pl.pallas_call(
        partial(head_kernel, colors, chans, band),
        out_shape=pltpu.VMEM((peers, 2 * colors * band + 16, HALF), BF16),
        in_specs=[vm] * 6,
        out_specs=vm,
        compiler_params=pltpu.CompilerParams(vmem_limit_bytes=VMEM_LIMIT),
        name="conv_head",
    )(second_halo, first_halo, features, table, ring_table, bias)


def sending_order(peers):
    return [*range(peers - 2, 0, -2), *range(peers - 1, 0, -2), 0]


def forward_y_kernel(colors, band, parts, *refs):
    peers = len(refs) - 6
    matrix, tw_c, tw_s, out, coded, left = refs[peers:]
    for i, k in enumerate(sending_order(peers)):
        coded[lax.axis_index("col") ^ k] = refs[i][...]
    step = 16
    lane = lax.broadcasted_iota(jnp.int32, (1, HALF), 1)
    for o in range(colors):
        for r in range(0, band, step):
            edge = []
            for p in range(peers):
                base = 2 * colors * band
                block = coded[p, base : base + step, :].astype(F32)
                shift = edge_slot(o, 0) + 64 * (r // step)
                if shift:
                    block = pltpu.roll(block, HALF - shift, 1)
                edge.append(block + pltpu.roll(block, HALF - edge_slot(0, 1), 1))
            cross = [pltpu.roll(x, HALF - 2, 1) for x in edge]
            zero = jnp.zeros_like(cross[0])
            fixed = []
            for p in range(peers):
                before = cross[p - 1] if p > 0 else zero
                after = cross[p + 1] if p + 1 < peers else zero
                fixed.append(CODE * jnp.tanh(edge[p] + jnp.where(lane < HALF // 2, before, after)))
            items = []
            for p in range(peers):
                for h in range(2):
                    start = (h * colors + o) * band + r
                    t = log2(coded[p, start : start + step, :].astype(F32))
                    t = jnp.where(lane == (HALF - 1) * h, fixed[p], t)
                    items.append(Pair(*sincos_half(t, 4, 1.0 / CODE)))
            for k, z in enumerate(small_dft(items, -1)):
                if k:
                    z = z.times(tw_c[k : k + 1, :], -tw_s[k : k + 1, :])
                for part, x in enumerate((z.re, z.im)):
                    high, low = split(x)
                    for j, value in enumerate((high, low, high)):
                        to = slice((2 * j + part) * HALF, (2 * j + part + 1) * HALF)
                        left[o, k, r : r + step, to] = value
        width = TILE // parts
        acc = dot(left[o].reshape(2 * peers * band, 3 * TILE), matrix[...])
        code = encode(acc)
        for k in range(2 * peers):
            for q in range(parts):
                out[parts * k + q, o * band : (o + 1) * band, :] = code[k * band : (k + 1) * band, q * width : (q + 1) * width]


def forward_y(blocks, colors, band, parts):
    peers = len(blocks)
    tw_c, tw_s = dft_np(2 * peers, HALF, peers * TILE)
    vm = pl.BlockSpec(memory_space=pltpu.VMEM)
    sm = pl.BlockSpec(memory_space=pltpu.SMEM)
    matrix = tall(interleaved(complex_np(-1), parts))
    return pl.pallas_call(
        partial(forward_y_kernel, colors, band, parts),
        out_shape=pltpu.VMEM((2 * peers * parts, colors * band, TILE // parts), BF16),
        in_specs=[vm] * (peers + 3),
        out_specs=vm,
        scratch_shapes=[
            pltpu.VMEM((peers,) + blocks[0].shape, BF16),
            pltpu.VMEM((colors, 2 * peers, band, 3 * TILE), BF16),
        ],
        compiler_params=pltpu.CompilerParams(vmem_limit_bytes=VMEM_LIMIT),
        name="forward_y",
    )(*(blocks[k] for k in sending_order(peers)), jnp.asarray(matrix), jnp.asarray(tw_c, F32), jnp.asarray(tw_s, F32))


def transfer_kernel(sizes, wave, travel, out):
    height, width, parts, inner, block = sizes
    color, k = pl.program_id(0), pl.program_id(1)
    position = lax.axis_index("row") * lax.axis_size("col") + lax.axis_index("col")
    k0 = position // parts
    q = position % parts
    shape = out.shape[3:]
    m = lax.broadcasted_iota(jnp.int32, shape, 0)
    lane = lax.broadcasted_iota(jnp.int32, shape, 1)
    kx = 2 * k + lane // block + (height // HALF) * m
    ky = k0 + inner * (block * q + lane % block)

    @pl.when(color < wave.shape[0])
    def _():
        sx = jnp.where(kx < height // 2, kx, kx - height).astype(F32) / height
        sy = jnp.where(ky < width // 2, ky, ky - width).astype(F32) / width
        f2 = sx * sx + sy * sy
        a = wave[jnp.minimum(color, wave.shape[0] - 1)]
        turns = travel[0] * f2 / (a + jnp.sqrt(a * a - f2))
        turns = turns - jnp.round(turns)
        c, s = sincos_half(2.0 * turns)
        out[0, 0, 0] = c * (1.0 / height)
        out[0, 0, 1] = s * (1.0 / height)

    @pl.when(color == wave.shape[0])
    def _():
        turns = ((2 * k + lane // block) * m).astype(F32) * (1.0 / height)
        c, s = sincos_half(2.0 * (turns - jnp.round(turns)))
        out[0, 0, 0] = c
        out[0, 0, 1] = s


def transfer(inv_wavelength, distance, sizes):
    height, width, parts, inner, block = sizes
    colors = inv_wavelength.shape[0]
    sm = pl.BlockSpec(memory_space=pltpu.SMEM)
    n = height // TILE
    return pl.pallas_call(
        partial(transfer_kernel, sizes),
        grid=(colors + 1, n),
        out_shape=jax.ShapeDtypeStruct((colors + 1, n, 2, HALF, 2 * block), F32),
        in_specs=[sm] * 2,
        out_specs=pl.BlockSpec((1, 1, 2, HALF, 2 * block), lambda c, k: (c, k, 0, 0, 0)),
        compiler_params=pltpu.CompilerParams(vmem_limit_bytes=VMEM_LIMIT),
        name="transfer",
    )(inv_wavelength, distance)


def middle_kernel(coded, tables, matrix, out, right):
    colors = out.shape[1]
    for color in range(colors):
        middle_color(
            coded.at[:, color], tables.at[color], matrix, tables.at[colors], out.at[:, color], right.at[color]
        )


def middle_color(coded, table, matrix, twiddles, out, right):
    n = table.shape[0]
    width = coded.shape[-1]
    block = width // 2
    per = coded.shape[0] // (2 * n)
    band = coded.shape[1]
    lane = lax.broadcasted_iota(jnp.int32, (1, width), 1)
    left = lane < block
    step = 16
    turn_c = [jnp.where(left, 1.0, math.cos(math.pi * a / n)) for a in range(n)]
    turn_s = [jnp.where(left, 0.0, math.sin(math.pi * a / n)) for a in range(n)]

    def put(k, rows, z, order):
        for part, x in zip(order, (z.re, z.im)):
            high, low = split(x)
            for j, value in enumerate((high, high, low)):
                to = (2 * j + part) * HALF
                right[to + rows.start : to + rows.stop, k * width : (k + 1) * width] = value

    for i in range(HALF // step):
        s, r = divmod(i * step, band)
        rows = slice(i * step, (i + 1) * step)
        items = []
        for a in range(n):
            x = decode(coded[per * a + s, r : r + step, :])
            y = decode(coded[per * (a + n) + s, r : r + step, :])
            u, v = x + y, x - y
            z = Pair(jnp.where(left, u, lane_shift(v, block)), jnp.where(left, lane_shift(u, block), v))
            if a:
                z = z.times(turn_c[a], -turn_s[a])
            items.append(z)
        for k, z in enumerate(small_dft(items, -1)):
            put(k, rows, z.times(twiddles[k, 0, rows, :], -twiddles[k, 1, rows, :]), (0, 1))
    acc = dot(matrix[...], right[...])
    for k in range(n):
        cols = slice(k * width, (k + 1) * width)
        z = Pair(acc[:HALF, cols], acc[HALF:, cols])
        put(k, slice(0, HALF), z.times(table[k, 0], -table[k, 1]), (1, 0))
    acc = dot(matrix[...], right[...])
    for i in range(HALF // step):
        s, r = divmod(i * step, band)
        rows = slice(i * step, (i + 1) * step)
        items = []
        for k in range(n):
            cols = slice(k * width, (k + 1) * width)
            z = Pair(acc[HALF + rows.start : HALF + rows.stop, cols], acc[rows, cols])
            items.append(z.times(twiddles[k, 0, rows, :], twiddles[k, 1, rows, :]))
        for a, z in enumerate(small_dft(items, 1)):
            if a:
                z = z.times(turn_c[a], turn_s[a])
            u = jnp.where(left, z.re, lane_shift(z.im, block))
            v = jnp.where(left, lane_shift(z.re, block), z.im)
            out[per * a + s, r : r + step, :] = encode(u + v)
            out[per * (a + n) + s, r : r + step, :] = encode(u - v)


def middle(coded, table):
    groups, colors, band, width = coded.shape
    n = table.shape[1]
    vm = pl.BlockSpec(memory_space=pltpu.VMEM)
    forward = wide(complex_np(-1).T)
    return pl.pallas_call(
        middle_kernel,
        out_shape=jax.ShapeDtypeStruct(coded.shape, BF16),
        in_specs=[vm] * 3,
        out_specs=vm,
        scratch_shapes=[pltpu.VMEM((colors, 3 * TILE, n * width), BF16)],
        compiler_params=pltpu.CompilerParams(vmem_limit_bytes=VMEM_LIMIT),
        name="middle_x",
    )(*(pltpu.with_memory_space_constraint(x, pltpu.VMEM) for x in (coded, table, jnp.asarray(forward))))


def inverse_y_kernel(parts, coded, matrix, tw_c, tw_s, target, left, out, sems):
    inner = tw_c.shape[0]
    colors, band, width = coded.shape[1], coded.shape[2], coded.shape[3]
    outs = []
    step = 16
    scale = 1.0 / (inner * HALF)
    for o in range(colors):
        for k in range(inner):
            for q in range(parts):
                high, low = split(decode(coded[parts * k + q, o]))
                for j, value in enumerate((high, low, high)):
                    left[o, k, :, j * TILE + q * width : j * TILE + (q + 1) * width] = value
        acc = dot(left[o].reshape(inner * band, 3 * TILE), matrix[...])
        for r in range(0, band, step):
            items = []
            for k in range(inner):
                z = acc[k * band + r : k * band + r + step]
                items.append(Pair(z[:, :HALF], z[:, HALF:]).times(tw_c[k : k + 1, :] * scale, tw_s[k : k + 1, :] * scale))
            for a, z in enumerate(small_dft(items, 1)):
                out[o, 0, r : r + step, a * HALF : (a + 1) * HALF] = z.re.astype(BF16)
                out[o, 1, r : r + step, a * HALF : (a + 1) * HALF] = z.im.astype(BF16)
        outs += fetch([pltpu.make_async_copy(out.at[o], target.at[o], sems.at[o])])
    for copy in outs:
        copy.wait()


def inverse_y(coded, parts):
    groups, colors, band, width = coded.shape
    inner = groups // parts
    tw_c, tw_s = dft_np(inner, HALF, inner * HALF)
    matrix = tall(np.ascontiguousarray(interleaved(complex_np(1).T.copy(), parts).T))
    hbm = pl.BlockSpec(memory_space=pltpu.HBM)
    vm = pl.BlockSpec(memory_space=pltpu.VMEM)
    return pl.pallas_call(
        partial(inverse_y_kernel, parts),
        out_shape=jax.ShapeDtypeStruct((colors, 2, band, inner * HALF), BF16),
        in_specs=[vm] * 4,
        out_specs=hbm,
        scratch_shapes=[
            pltpu.VMEM((colors, inner, band, 3 * TILE), BF16),
            pltpu.VMEM((colors, 2, band, inner * HALF), BF16),
            pltpu.SemaphoreType.DMA((colors,)),
        ],
        compiler_params=pltpu.CompilerParams(vmem_limit_bytes=VMEM_LIMIT),
        name="inverse_y",
    )(coded, jnp.asarray(matrix), jnp.asarray(tw_c, F32), jnp.asarray(tw_s, F32))


def per_device(features, conv_weight, bias, inv_wavelength, distance):
    mesh_rows = lax.axis_size("row")
    mesh_cols = lax.axis_size("col")
    groups = mesh_rows * mesh_cols
    chans, tile_rows, tile_cols = features.shape
    colors = conv_weight.shape[0]
    band = tile_rows // mesh_cols
    height = tile_rows * mesh_rows
    width = tile_cols * mesh_cols
    block = width // groups
    parts = mesh_rows // 2
    tile, edge_one, edge_two, *prepared = prepare(features, conv_weight, bias)
    halos = []
    for start, edge in ((1, edge_two), (0, edge_one)):
        pairs = [(i, i + 1) for i in range(start, mesh_rows - 1, 2)]
        halos.append(lax.ppermute(edge, "row", pairs + [(j, i) for i, j in pairs]))
    bands = head((tile, *prepared), *halos, band, mesh_cols)
    blocks = [bands[0]] * mesh_cols
    for k in range(mesh_cols - 1, 0, -1):
        blocks[k] = lax.ppermute(bands[k], "col", [(i, i ^ k) for i in range(mesh_cols)])
    spectrum = forward_y(blocks, colors, band, parts)
    table = transfer(inv_wavelength, distance, (height, width, parts, 2 * mesh_cols, block))
    spectrum = lax.all_to_all(spectrum, ("row", "col"), split_axis=0, concat_axis=0, tiled=True)
    back = middle(spectrum.reshape(groups, colors, band, 2 * block), table)
    back = lax.all_to_all(back, ("row", "col"), split_axis=0, concat_axis=0, tiled=True)
    return inverse_y(back, parts)


def solution(mesh):
    in_specs = (P(None, "row", "col"), P(), P(), P(), P())
    out_specs = P(None, None, ("row", "col"), None)
    return jax.shard_map(
        per_device, mesh=mesh, in_specs=in_specs, out_specs=out_specs, check_vma=False
    )
```

```python
from functools import partial
import math

import numpy as np
import jax
import jax.numpy as jnp
from jax import lax
from jax.experimental import pallas as pl
from jax.experimental.pallas import tpu as pltpu
from jax.sharding import PartitionSpec as P

F32 = jnp.float32
BF16 = jnp.bfloat16
TILE = 256
HALF = 128
CODE = 124.0
TINY = 1.2e-38
VMEM_LIMIT = 10 * 1024 * 1024


def split_np(table):
    high = table.astype(jnp.bfloat16)
    low = (table - high.astype(np.float64)).astype(jnp.bfloat16)
    return high, low


def dft_np(rows, cols, length):
    product = np.outer(np.arange(rows), np.arange(cols)) % length
    angle = 2.0 * np.pi * product / length
    return np.cos(angle), np.sin(angle)


def interleaved(table, parts):
    rows = table.shape[0]
    return table.reshape(rows, 2, parts, HALF // parts).transpose(0, 2, 1, 3).reshape(rows, 2 * HALF)


def complex_np(sign):
    c, s = dft_np(HALF, HALF, HALF)
    return np.block([[c, sign * s], [-sign * s, c]])


def tall(table):
    high, low = split_np(table)
    return np.concatenate([high, high, low], 0)


def wide(table):
    high, low = split_np(table)
    return np.concatenate([high, low, high], 1)


def fitted(func, terms, odd):
    t = np.cos(np.pi * (np.arange(400) + 0.5) / 800)
    powers = np.stack([t ** (2 * k + odd) for k in range(terms)], 1)
    return [float(v) for v in np.linalg.lstsq(powers, func(np.pi / 2 * t), rcond=None)[0]]


def sincos_half(t, terms=5, scale=1.0):
    u = t * t
    sines = [v * scale ** (2 * k + 1) for k, v in enumerate(fitted(np.sin, terms, 1))]
    cosines = [v * scale ** (2 * k) for k, v in enumerate(fitted(np.cos, terms, 0))]
    s = sines[-1]
    for coef in sines[-2::-1]:
        s = s * u + coef
    s = s * t
    c = cosines[-1]
    for coef in cosines[-2::-1]:
        c = c * u + coef
    s2 = s + s
    return 1.0 - s2 * s, s2 * c


def log2(x):
    return lax.log(x) * (1.0 / math.log(2.0))


def encode(v):
    v2 = v * v
    return (v2 * v2 * v).astype(BF16)


def decode(w):
    w = w.astype(F32)
    return w * jnp.exp2(lax.log(jnp.maximum(jnp.abs(w), TINY)) * (-0.8 / math.log(2.0)))


def fetch(copies):
    for copy in copies:
        copy.start()
    return copies


def split(x):
    high = x.astype(BF16)
    return high, (x - high.astype(F32)).astype(BF16)


def dot(a, b):
    return lax.dot_general(a, b, (((1,), (0,)), ((), ())), preferred_element_type=F32)


def lane_shift(x, shift):
    width = x.shape[-1]
    shift = shift % width
    if shift == 0:
        return x
    if width % 128 == 0:
        return pltpu.roll(x, shift, x.ndim - 1)
    return jnp.concatenate([x[..., width - shift :], x[..., : width - shift]], -1)


class Pair:
    def __init__(self, re, im):
        self.re, self.im = re, im

    def __add__(self, o):
        return Pair(self.re + o.re, self.im + o.im)

    def __sub__(self, o):
        return Pair(self.re - o.re, self.im - o.im)

    def times(self, c, s):
        return Pair(self.re * c - self.im * s, self.re * s + self.im * c)


def butterfly(even, odd, k, n, sign):
    if k == 0:
        return even + odd, even - odd
    if 4 * k == n:
        plus = Pair(even.re - odd.im, even.im + odd.re)
        minus = Pair(even.re + odd.im, even.im - odd.re)
        return (plus, minus) if sign > 0 else (minus, plus)
    if 8 * k in (n, 3 * n):
        h = math.sqrt(0.5)
        a, b = (odd.re - odd.im) * h, (odd.re + odd.im) * h
        if sign > 0 and 8 * k == n:
            return Pair(even.re + a, even.im + b), Pair(even.re - a, even.im - b)
        if sign > 0:
            return Pair(even.re - b, even.im + a), Pair(even.re + b, even.im - a)
        if 8 * k == n:
            return Pair(even.re + b, even.im - a), Pair(even.re - b, even.im + a)
        return Pair(even.re - a, even.im - b), Pair(even.re + a, even.im + b)
    angle = sign * 2.0 * math.pi * k / n
    o = odd.times(math.cos(angle), math.sin(angle))
    return even + o, even - o


def small_dft(items, sign):
    n = len(items)
    if n == 1:
        return items
    even = small_dft(items[0::2], sign)
    odd = small_dft(items[1::2], sign)
    out = [None] * n
    for k in range(n // 2):
        out[k], out[k + n // 2] = butterfly(even[k], odd[k], k, n, sign)
    return out


def edge_slot(color, part):
    return 16 * color + 8 * part


def edges_kernel(feat, first_edge, second_edge, edge, sems):
    step = 16
    rows = feat.shape[1]
    copies = fetch(
        [
            pltpu.make_async_copy(feat.at[:, pl.ds(0, step), :], edge.at[0], sems.at[0]),
            pltpu.make_async_copy(feat.at[:, pl.ds(rows - step, step), :], edge.at[1], sems.at[1]),
        ]
    )
    for copy in copies:
        copy.wait()
    top = edge[0].astype(F32)[:, 0, :]
    bottom = edge[1].astype(F32)[:, step - 1, :]
    even = lax.axis_index("row") % 2 == 0
    first_edge[...] = jnp.where(even, bottom, top).astype(BF16)
    second_edge[...] = jnp.where(even, top, bottom).astype(BF16)


def edges(features):
    chans, rows, cols = features.shape
    vm = pl.BlockSpec(memory_space=pltpu.VMEM)
    return pl.pallas_call(
        edges_kernel,
        out_shape=[pltpu.VMEM((chans, cols), BF16)] * 2,
        in_specs=[pl.BlockSpec(memory_space=pltpu.HBM)],
        out_specs=[vm] * 2,
        scratch_shapes=[pltpu.VMEM((2, chans, 16, cols), BF16), pltpu.SemaphoreType.DMA((2,))],
        compiler_params=pltpu.CompilerParams(vmem_limit_bytes=VMEM_LIMIT),
        name="edges",
    )(pltpu.with_memory_space_constraint(features, pltpu.HBM))


def prepare_kernel(colors, chans, feat, weight, bias, tile, table, ring_table, bias_rows, taps, bias_in, sems):
    step = 16
    copies = fetch(
        [
            pltpu.make_async_copy(weight, taps, sems.at[0]),
            pltpu.make_async_copy(bias, bias_in, sems.at[1]),
        ]
        + [
            pltpu.make_async_copy(feat.at[pl.ds(i * (chans // 8), chans // 8)], tile.at[pl.ds(i * (chans // 8), chans // 8)], sems.at[2 + i])
            for i in range(8)
        ]
    )
    copies[0].wait()
    wide = chans * step
    c_of = lax.broadcasted_iota(jnp.int32, (chans, wide), 1) // step
    spread = (c_of == lax.broadcasted_iota(jnp.int32, (chans, wide), 0)).astype(F32).astype(BF16)
    x_in = lax.broadcasted_iota(jnp.int32, (step + 8, wide), 1) % step
    row = lax.broadcasted_iota(jnp.int32, (step + 8, wide), 0)
    masks = []
    for u in range(3):
        main = (row < step) & (x_in - row + 1 == u)
        if u == 0:
            main = main | ((row == step) & (x_in == step - 1))
        if u == 2:
            main = main | ((row == step + 7) & (x_in == 0))
        masks.append(main)
    sub = lax.broadcasted_iota(jnp.int32, (8, chans), 0)
    for o in range(colors):
        spreads = [dot(taps[o, u], spread) for u in range(3)]
        small = [taps[o, u].astype(F32) for u in range(3)]
        for v in range(3):
            total = jnp.zeros((step + 8, wide), F32)
            for u in range(3):
                total = total + jnp.where(masks[u], spreads[u][v : v + 1], 0.0)
            g = v * colors + o
            table[g * step : (g + 1) * step, :] = total[:step].astype(BF16)
            start = 3 * colors * step + 8 * g
            table[start : start + 8, :] = total[step:].astype(BF16)
            ring_table[0, 8 * g : 8 * g + 8, :] = jnp.where(sub == 0, small[0][v : v + 1], 0.0).astype(BF16)
            ring_table[1, 8 * g : 8 * g + 8, :] = jnp.where(sub == 7, small[2][v : v + 1], 0.0).astype(BF16)
    copies[1].wait()
    for o in range(colors):
        bias_rows[o : o + 1, :] = jnp.full((1, TILE), bias_in[o], F32)
    for copy in copies[2:]:
        copy.wait()


def prepare(features, conv_weight, bias):
    chans, rows, cols = features.shape
    colors = bias.shape[0]
    weight = conv_weight.transpose(0, 2, 3, 1)
    hbm = pl.BlockSpec(memory_space=pltpu.HBM)
    vm = pl.BlockSpec(memory_space=pltpu.VMEM)
    return pl.pallas_call(
        partial(prepare_kernel, colors, chans),
        out_shape=[
            pltpu.VMEM(features.shape, BF16),
            pltpu.VMEM((3 * colors * 24, chans * 16), BF16),
            pltpu.VMEM((2, 3 * colors * 8, chans), BF16),
            pltpu.VMEM((colors, TILE), F32),
        ],
        in_specs=[hbm] * 3,
        out_specs=[vm] * 4,
        scratch_shapes=[
            pltpu.VMEM(weight.shape, BF16),
            pltpu.SMEM(bias.shape, F32),
            pltpu.SemaphoreType.DMA((10,)),
        ],
        compiler_params=pltpu.CompilerParams(vmem_limit_bytes=VMEM_LIMIT),
        name="prepare",
    )(*(pltpu.with_memory_space_constraint(x, pltpu.HBM) for x in (features, weight, bias)))


def head_kernel(colors, chans, band, second_halo, first_halo, feat, table, ring_table, bias, out):
    peers = out.shape[0]
    step = 16
    per = band // step
    groups = 3 * colors
    main_rows = groups * step
    me = lax.axis_index("col")

    lane = lax.broadcasted_iota(jnp.int32, (1, TILE), 1)
    lane_half = lax.broadcasted_iota(jnp.int32, (1, HALF), 1)
    outer = (lane_half == 0) | (lane_half == HALF - 1)
    sub = lax.broadcasted_iota(jnp.int32, (8, 1), 0)

    first, last = sub == 0, sub == 7

    def ring_of(block):
        return [block[v * 8 * colors : (v + 1) * 8 * colors] for v in range(3)]

    def chunk(i):
        return feat[:, i * step : (i + 1) * step, :].reshape(chans * step, TILE)

    prods = [None] * (peers * per)
    rings = [None] * (peers * per + 2)
    even = lax.axis_index("row") % 2 == 0
    one, two = first_halo[...].astype(F32), second_halo[...].astype(F32)
    above = jnp.where(even, two, one).astype(BF16)
    below = jnp.where(even, one, two).astype(BF16)
    rings[0] = ring_of(dot(ring_table[0], above))
    rings[-1] = ring_of(dot(ring_table[1], below))

    def multiply(j):
        for i in range(j * per, (j + 1) * per):
            prods[i] = dot(table[...], chunk(i))
            rings[i + 1] = ring_of(prods[i][main_rows:])

    def finish(j):
        slot = me ^ j
        total = None
        for i in range(per):
            at = j * per + i
            extra = None
            for o in range(colors):
                q = []
                for v in range(3):
                    g = v * colors + o
                    main = prods[at][g * step : (g + 1) * step]
                    top = main[:8] + jnp.where(first, rings[at][v][8 * o : 8 * o + 8], 0.0)
                    bottom = main[8:] + jnp.where(last, rings[at + 2][v][8 * o : 8 * o + 8], 0.0)
                    q.append(jnp.concatenate([top, bottom], 0))
                r0 = pltpu.roll(q[0], 1, 1)
                r2 = pltpu.roll(q[2], TILE - 1, 1)
                own = q[1] + jnp.where(lane == 0, 0.0, r0) + jnp.where(lane == TILE - 1, 0.0, r2) + bias[o : o + 1, :]
                code = jnp.exp2(CODE * jnp.tanh(own)).astype(BF16)
                row = o * band + i * step
                for h in range(2):
                    start = h * colors * band + row
                    out[slot, start : start + step, :] = code[:, h * HALF : (h + 1) * HALF]
                cross = jnp.where(lane_half == 0, r0[:, :HALF], r2[:, HALF:])
                cross = pltpu.roll(jnp.where(outer, cross, 0.0), 2, 1)
                edges = jnp.where(lane_half == 0, own[:, :HALF], own[:, HALF:])
                edges = jnp.where(outer, edges, cross)
                high = edges.astype(BF16).astype(F32)
                both = high + pltpu.roll(edges - high, edge_slot(0, 1), 1)
                shift = edge_slot(o, 0) + 64 * i
                if shift:
                    both = pltpu.roll(both, shift, 1)
                extra = both if extra is None else extra + both
            total = extra if total is None else total + extra
        base = 2 * colors * band
        out[slot, base : base + step, :] = total.astype(BF16)

    multiply(0)
    for j in range(peers):
        if j + 1 < peers:
            multiply(j + 1)
        finish(j)


def head(prepared, second_halo, first_halo, band, peers):
    features, table, ring_table, bias = prepared
    chans, rows, cols = features.shape
    colors = bias.shape[0]
    vm = pl.BlockSpec(memory_space=pltpu.VMEM)
    return pl.pallas_call(
        partial(head_kernel, colors, chans, band),
        out_shape=pltpu.VMEM((peers, 2 * colors * band + 16, HALF), BF16),
        in_specs=[vm] * 6,
        out_specs=vm,
        compiler_params=pltpu.CompilerParams(vmem_limit_bytes=VMEM_LIMIT),
        name="conv_head",
    )(second_halo, first_halo, features, table, ring_table, bias)


def sending_order(peers):
    return [*range(peers - 2, 0, -2), *range(peers - 1, 0, -2), 0]


def forward_y_kernel(colors, band, parts, *refs):
    peers = len(refs) - 7
    matrix, tw_c, tw_s, _, out, coded, left = refs[peers:]
    for i, k in enumerate(sending_order(peers)):
        coded[lax.axis_index("col") ^ k] = refs[i][...]
    step = 16
    lane = lax.broadcasted_iota(jnp.int32, (1, HALF), 1)
    width = TILE // parts

    def spread(o):
        for r in range(0, band, step):
            edge = []
            for p in range(peers):
                base = 2 * colors * band
                block = coded[p, base : base + step, :].astype(F32)
                shift = edge_slot(o, 0) + 64 * (r // step)
                if shift:
                    block = pltpu.roll(block, HALF - shift, 1)
                edge.append(block + pltpu.roll(block, HALF - edge_slot(0, 1), 1))
            cross = [pltpu.roll(x, HALF - 2, 1) for x in edge]
            zero = jnp.zeros_like(cross[0])
            fixed = []
            for p in range(peers):
                before = cross[p - 1] if p > 0 else zero
                after = cross[p + 1] if p + 1 < peers else zero
                fixed.append(CODE * jnp.tanh(edge[p] + jnp.where(lane < HALF // 2, before, after)))
            items = []
            for p in range(peers):
                for h in range(2):
                    start = (h * colors + o) * band + r
                    t = log2(coded[p, start : start + step, :].astype(F32))
                    t = jnp.where(lane == (HALF - 1) * h, fixed[p], t)
                    items.append(Pair(*sincos_half(t, 4, 1.0 / CODE)))
            for k, z in enumerate(small_dft(items, -1)):
                if k:
                    z = z.times(tw_c[k : k + 1, :], -tw_s[k : k + 1, :])
                for part, x in enumerate((z.re, z.im)):
                    high, low = split(x)
                    for j, value in enumerate((high, low, high)):
                        to = slice((2 * j + part) * HALF, (2 * j + part + 1) * HALF)
                        left[o, k, r : r + step, to] = value

    def multiply(o):
        return dot(left[o].reshape(2 * peers * band, 3 * TILE), matrix[...])

    def store(o, acc):
        code = encode(acc)
        for k in range(2 * peers):
            for q in range(parts):
                out[parts * k + q, o * band : (o + 1) * band, :] = code[k * band : (k + 1) * band, q * width : (q + 1) * width]

    held = None
    for o in range(colors):
        spread(o)
        acc = multiply(o)
        if held is not None:
            store(o - 1, held)
        held = acc
    store(colors - 1, held)


def forward_y(blocks, colors, band, parts, table):
    peers = len(blocks)
    tw_c, tw_s = dft_np(2 * peers, HALF, peers * TILE)
    vm = pl.BlockSpec(memory_space=pltpu.VMEM)
    sm = pl.BlockSpec(memory_space=pltpu.SMEM)
    matrix = tall(interleaved(complex_np(-1), parts))
    return pl.pallas_call(
        partial(forward_y_kernel, colors, band, parts),
        out_shape=pltpu.VMEM((2 * peers * parts, colors * band, TILE // parts), BF16),
        in_specs=[vm] * (peers + 3) + [pl.BlockSpec(memory_space=pl.ANY)],
        out_specs=vm,
        scratch_shapes=[
            pltpu.VMEM((peers,) + blocks[0].shape, BF16),
            pltpu.VMEM((colors, 2 * peers, band, 3 * TILE), BF16),
        ],
        compiler_params=pltpu.CompilerParams(vmem_limit_bytes=VMEM_LIMIT),
        name="forward_y",
    )(*(blocks[k] for k in sending_order(peers)), jnp.asarray(matrix), jnp.asarray(tw_c, F32), jnp.asarray(tw_s, F32), table)


def transfer_kernel(sizes, wave, travel, out):
    height, width, parts, inner, block = sizes
    position = lax.axis_index("row") * lax.axis_size("col") + lax.axis_index("col")
    k0 = position // parts
    q = position % parts
    colors, n = out.shape[0] - 1, out.shape[1]
    shape = (HALF // 4, out.shape[4])
    lane = lax.broadcasted_iota(jnp.int32, shape, 1)
    ky = k0 + inner * (block * q + lane % block)
    sy = jnp.where(ky < width // 2, ky, ky - width).astype(F32) * (1.0 / width)
    sy2 = sy * sy
    for k in range(n):
        for i in range(4):
            rows = slice(i * HALF // 4, (i + 1) * HALF // 4)
            m = lax.broadcasted_iota(jnp.int32, shape, 0) + i * HALF // 4
            half = 2 * k + lane // block
            kx = half + (height // HALF) * m
            sx = jnp.where(kx < height // 2, kx, kx - height).astype(F32) * (1.0 / height)
            f2 = sx * sx + sy2
            for color in range(colors):
                a = wave[color]
                turns = travel[0] * f2 / (a + jnp.sqrt(a * a - f2))
                turns = turns - jnp.round(turns)
                c, s = sincos_half(turns, 5, 2.0)
                out[color, k, 0, rows, :] = c * (1.0 / height)
                out[color, k, 1, rows, :] = s * (1.0 / height)
            turns = (half * m).astype(F32) * (1.0 / height)
            c, s = sincos_half(turns - jnp.round(turns), 5, 2.0)
            out[colors, k, 0, rows, :] = c
            out[colors, k, 1, rows, :] = s


def transfer(inv_wavelength, distance, sizes):
    height, width, parts, inner, block = sizes
    colors = inv_wavelength.shape[0]
    sm = pl.BlockSpec(memory_space=pltpu.SMEM)
    n = height // TILE
    return pl.pallas_call(
        partial(transfer_kernel, sizes),
        out_shape=pltpu.VMEM((colors + 1, n, 2, HALF, 2 * block), F32),
        in_specs=[sm] * 2,
        out_specs=pl.BlockSpec(memory_space=pltpu.VMEM),
        compiler_params=pltpu.CompilerParams(vmem_limit_bytes=VMEM_LIMIT),
        name="transfer",
    )(inv_wavelength, distance)


def middle_kernel(coded, tables, matrix, out, before, after):
    colors, n = out.shape[1], tables.shape[1]
    width = coded.shape[-1]
    block = width // 2
    per = coded.shape[0] // (2 * n)
    band = coded.shape[2]
    twiddles = tables.at[colors]
    lane = lax.broadcasted_iota(jnp.int32, (1, width), 1)
    left = lane < block
    step = 16
    turn_c = [jnp.where(left, 1.0, math.cos(math.pi * a / n)) for a in range(n)]
    turn_s = [jnp.where(left, 0.0, math.sin(math.pi * a / n)) for a in range(n)]

    def put(right, k, rows, z, order):
        for part, x in zip(order, (z.re, z.im)):
            high, low = split(x)
            for j, value in enumerate((high, high, low)):
                to = (2 * j + part) * HALF
                right[to + rows.start : to + rows.stop, k * width : (k + 1) * width] = value

    def spread(color):
        for i in range(HALF // step):
            s, r = divmod(i * step, band)
            rows = slice(i * step, (i + 1) * step)
            items = []
            for a in range(n):
                x = decode(coded[per * a + s, color, r : r + step, :])
                y = decode(coded[per * (a + n) + s, color, r : r + step, :])
                u, v = x + y, x - y
                z = Pair(jnp.where(left, u, lane_shift(v, block)), jnp.where(left, lane_shift(u, block), v))
                if a:
                    z = z.times(turn_c[a], -turn_s[a])
                items.append(z)
            for k, z in enumerate(small_dft(items, -1)):
                put(before.at[color], k, rows, z.times(twiddles[k, 0, rows, :], -twiddles[k, 1, rows, :]), (0, 1))

    def multiply(right, color):
        return dot(matrix[...], right[color])

    def filtered(color, acc):
        for k in range(n):
            cols = slice(k * width, (k + 1) * width)
            for i in range(HALF // step):
                rows = slice(i * step, (i + 1) * step)
                z = Pair(acc[rows, cols], acc[HALF + rows.start : HALF + rows.stop, cols])
                put(after.at[color], k, rows, z.times(tables[color, k, 0, rows, :], -tables[color, k, 1, rows, :]), (1, 0))

    def store(color, acc):
        for i in range(HALF // step):
            s, r = divmod(i * step, band)
            rows = slice(i * step, (i + 1) * step)
            items = []
            for k in range(n):
                cols = slice(k * width, (k + 1) * width)
                z = Pair(acc[HALF + rows.start : HALF + rows.stop, cols], acc[rows, cols])
                items.append(z.times(twiddles[k, 0, rows, :], twiddles[k, 1, rows, :]))
            for a, z in enumerate(small_dft(items, 1)):
                if a:
                    z = z.times(turn_c[a], turn_s[a])
                u = jnp.where(left, z.re, lane_shift(z.im, block))
                v = jnp.where(left, lane_shift(z.re, block), z.im)
                out[per * a + s, color, r : r + step, :] = encode(u + v)
                out[per * (a + n) + s, color, r : r + step, :] = encode(u - v)

    ahead, back = {}, {}
    for tick in range(colors + 2):
        if tick < colors:
            spread(tick)
            ahead[tick] = multiply(before, tick)
        if 0 <= tick - 1 < colors:
            filtered(tick - 1, ahead.pop(tick - 1))
            back[tick - 1] = multiply(after, tick - 1)
        if tick >= 2:
            store(tick - 2, back.pop(tick - 2))


def middle(coded, table):
    groups, colors, band, width = coded.shape
    n = table.shape[1]
    vm = pl.BlockSpec(memory_space=pltpu.VMEM)
    forward = wide(complex_np(-1).T)
    return pl.pallas_call(
        middle_kernel,
        out_shape=jax.ShapeDtypeStruct(coded.shape, BF16),
        in_specs=[vm] * 3,
        out_specs=vm,
        scratch_shapes=[pltpu.VMEM((colors, 3 * TILE, n * width), BF16)] * 2,
        compiler_params=pltpu.CompilerParams(vmem_limit_bytes=VMEM_LIMIT),
        name="middle_x",
    )(*(pltpu.with_memory_space_constraint(x, pltpu.VMEM) for x in (coded, table, jnp.asarray(forward))))


def inverse_y_kernel(parts, coded, matrix, tw_c, tw_s, target, left, out, sems):
    inner = tw_c.shape[0]
    colors, band, width = coded.shape[1], coded.shape[2], coded.shape[3]
    outs = []
    step = 16
    scale = 1.0 / (inner * HALF)

    def spread(o):
        for k in range(inner):
            for q in range(parts):
                high, low = split(decode(coded[parts * k + q, o]))
                for j, value in enumerate((high, low, high)):
                    left[o, k, :, j * TILE + q * width : j * TILE + (q + 1) * width] = value

    def multiply(o):
        return dot(left[o].reshape(inner * band, 3 * TILE), matrix[...])

    def store(o, acc):
        for r in range(0, band, step):
            items = []
            for k in range(inner):
                z = acc[k * band + r : k * band + r + step]
                items.append(Pair(z[:, :HALF], z[:, HALF:]).times(tw_c[k : k + 1, :] * scale, tw_s[k : k + 1, :] * scale))
            for a, z in enumerate(small_dft(items, 1)):
                out[o, 0, r : r + step, a * HALF : (a + 1) * HALF] = z.re.astype(BF16)
                out[o, 1, r : r + step, a * HALF : (a + 1) * HALF] = z.im.astype(BF16)
        outs.extend(fetch([pltpu.make_async_copy(out.at[o], target.at[o], sems.at[o])]))

    held = None
    for o in range(colors):
        spread(o)
        acc = multiply(o)
        if held is not None:
            store(o - 1, held)
        held = acc
    store(colors - 1, held)
    for copy in outs:
        copy.wait()


def inverse_y(coded, parts):
    groups, colors, band, width = coded.shape
    inner = groups // parts
    tw_c, tw_s = dft_np(inner, HALF, inner * HALF)
    matrix = tall(np.ascontiguousarray(interleaved(complex_np(1).T.copy(), parts).T))
    hbm = pl.BlockSpec(memory_space=pltpu.HBM)
    vm = pl.BlockSpec(memory_space=pltpu.VMEM)
    return pl.pallas_call(
        partial(inverse_y_kernel, parts),
        out_shape=jax.ShapeDtypeStruct((colors, 2, band, inner * HALF), BF16),
        in_specs=[vm] * 4,
        out_specs=hbm,
        scratch_shapes=[
            pltpu.VMEM((colors, inner, band, 3 * TILE), BF16),
            pltpu.VMEM((colors, 2, band, inner * HALF), BF16),
            pltpu.SemaphoreType.DMA((colors,)),
        ],
        compiler_params=pltpu.CompilerParams(vmem_limit_bytes=VMEM_LIMIT),
        name="inverse_y",
    )(coded, jnp.asarray(matrix), jnp.asarray(tw_c, F32), jnp.asarray(tw_s, F32))


def per_device(features, conv_weight, bias, inv_wavelength, distance):
    mesh_rows = lax.axis_size("row")
    mesh_cols = lax.axis_size("col")
    groups = mesh_rows * mesh_cols
    chans, tile_rows, tile_cols = features.shape
    colors = conv_weight.shape[0]
    band = tile_rows // mesh_cols
    height = tile_rows * mesh_rows
    width = tile_cols * mesh_cols
    block = width // groups
    parts = mesh_rows // 2
    edge_one, edge_two = edges(features)
    tile, *prepared = prepare(features, conv_weight, bias)
    halos = []
    for start, edge in ((1, edge_two), (0, edge_one)):
        pairs = [(i, i + 1) for i in range(start, mesh_rows - 1, 2)]
        halos.append(lax.ppermute(edge, "row", pairs + [(j, i) for i, j in pairs]))
    bands = head((tile, *prepared), *halos, band, mesh_cols)
    blocks = [bands[0]] * mesh_cols
    for k in range(mesh_cols - 1, 0, -1):
        blocks[k] = lax.ppermute(bands[k], "col", [(i, i ^ k) for i in range(mesh_cols)])
    table = transfer(inv_wavelength, distance, (height, width, parts, 2 * mesh_cols, block))
    spectrum = forward_y(blocks, colors, band, parts, table)
    spectrum = lax.all_to_all(spectrum, ("row", "col"), split_axis=0, concat_axis=0, tiled=True)
    back = middle(spectrum.reshape(groups, colors, band, 2 * block), table)
    back = lax.all_to_all(back, ("row", "col"), split_axis=0, concat_axis=0, tiled=True)
    return inverse_y(back, parts)


def solution(mesh):
    in_specs = (P(None, "row", "col"), P(), P(), P(), P())
    out_specs = P(None, None, ("row", "col"), None)
    return jax.shard_map(
        per_device, mesh=mesh, in_specs=in_specs, out_specs=out_specs, check_vma=False
    )
```

```python
from functools import partial
import math

import numpy as np
import jax
import jax.numpy as jnp
from jax import lax
from jax.experimental import pallas as pl
from jax.experimental.pallas import tpu as pltpu
from jax.sharding import PartitionSpec as P

F32 = jnp.float32
BF16 = jnp.bfloat16
TILE = 256
HALF = 128
CODE = 124.0
TINY = 1.2e-38
SHRINK = 2.0**-4
VMEM_LIMIT = 10 * 1024 * 1024


def split_np(table):
    high = table.astype(jnp.bfloat16)
    low = (table - high.astype(np.float64)).astype(jnp.bfloat16)
    return high, low


def dft_np(rows, cols, length):
    product = np.outer(np.arange(rows), np.arange(cols)) % length
    angle = 2.0 * np.pi * product / length
    return np.cos(angle), np.sin(angle)


def interleaved(table, parts):
    rows = table.shape[0]
    return table.reshape(rows, 2, parts, HALF // parts).transpose(0, 2, 1, 3).reshape(rows, 2 * HALF)


def complex_np(sign):
    c, s = dft_np(HALF, HALF, HALF)
    return np.block([[c, sign * s], [-sign * s, c]])


def tall(table):
    high, low = split_np(table)
    return np.concatenate([high, high, low], 0)


def wide(table):
    high, low = split_np(table)
    return np.concatenate([high, low, high], 1)


def fitted(func, terms, odd):
    t = np.cos(np.pi * (np.arange(400) + 0.5) / 800)
    powers = np.stack([t ** (2 * k + odd) for k in range(terms)], 1)
    return [float(v) for v in np.linalg.lstsq(powers, func(np.pi / 2 * t), rcond=None)[0]]


def sincos_half(t, terms=5, scale=1.0):
    u = t * t
    sines = [v * scale ** (2 * k + 1) for k, v in enumerate(fitted(np.sin, terms, 1))]
    cosines = [v * scale ** (2 * k) for k, v in enumerate(fitted(np.cos, terms, 0))]
    s = sines[-1]
    for coef in sines[-2::-1]:
        s = s * u + coef
    s = s * t
    c = cosines[-1]
    for coef in cosines[-2::-1]:
        c = c * u + coef
    s2 = s + s
    return 1.0 - s2 * s, s2 * c


def log2(x):
    return lax.log(x) * (1.0 / math.log(2.0))


def encode(v):
    v2 = v * v
    v4 = v2 * v2
    return (v4 * v4 * v).astype(BF16)


def decode(w):
    w = w.astype(F32)
    return w * jnp.exp2(lax.log(jnp.maximum(jnp.abs(w), TINY)) * (-8.0 / 9.0 / math.log(2.0)))


def fetch(copies):
    for copy in copies:
        copy.start()
    return copies


def split(x):
    high = x.astype(BF16)
    return high, (x - high.astype(F32)).astype(BF16)


def dot(a, b):
    return lax.dot_general(a, b, (((1,), (0,)), ((), ())), preferred_element_type=F32)


def lane_shift(x, shift):
    width = x.shape[-1]
    shift = shift % width
    if shift == 0:
        return x
    if width % 128 == 0:
        return pltpu.roll(x, shift, x.ndim - 1)
    return jnp.concatenate([x[..., width - shift :], x[..., : width - shift]], -1)


class Pair:
    def __init__(self, re, im):
        self.re, self.im = re, im

    def __add__(self, o):
        return Pair(self.re + o.re, self.im + o.im)

    def __sub__(self, o):
        return Pair(self.re - o.re, self.im - o.im)

    def times(self, c, s):
        return Pair(self.re * c - self.im * s, self.re * s + self.im * c)


def butterfly(even, odd, k, n, sign):
    if k == 0:
        return even + odd, even - odd
    if 4 * k == n:
        plus = Pair(even.re - odd.im, even.im + odd.re)
        minus = Pair(even.re + odd.im, even.im - odd.re)
        return (plus, minus) if sign > 0 else (minus, plus)
    if 8 * k in (n, 3 * n):
        h = math.sqrt(0.5)
        a, b = (odd.re - odd.im) * h, (odd.re + odd.im) * h
        if sign > 0 and 8 * k == n:
            return Pair(even.re + a, even.im + b), Pair(even.re - a, even.im - b)
        if sign > 0:
            return Pair(even.re - b, even.im + a), Pair(even.re + b, even.im - a)
        if 8 * k == n:
            return Pair(even.re + b, even.im - a), Pair(even.re - b, even.im + a)
        return Pair(even.re - a, even.im - b), Pair(even.re + a, even.im + b)
    angle = sign * 2.0 * math.pi * k / n
    o = odd.times(math.cos(angle), math.sin(angle))
    return even + o, even - o


def small_dft(items, sign):
    n = len(items)
    if n == 1:
        return items
    even = small_dft(items[0::2], sign)
    odd = small_dft(items[1::2], sign)
    out = [None] * n
    for k in range(n // 2):
        out[k], out[k + n // 2] = butterfly(even[k], odd[k], k, n, sign)
    return out


def edge_slot(color, part):
    return 16 * color + 8 * part


def edges_kernel(feat, first_edge, second_edge, edge, sems):
    step = 16
    rows = feat.shape[1]
    copies = fetch(
        [
            pltpu.make_async_copy(feat.at[:, pl.ds(0, step), :], edge.at[0], sems.at[0]),
            pltpu.make_async_copy(feat.at[:, pl.ds(rows - step, step), :], edge.at[1], sems.at[1]),
        ]
    )
    for copy in copies:
        copy.wait()
    top = edge[0].astype(F32)[:, 0, :]
    bottom = edge[1].astype(F32)[:, step - 1, :]
    even = lax.axis_index("row") % 2 == 0
    first_edge[...] = jnp.where(even, bottom, top).astype(BF16)
    second_edge[...] = jnp.where(even, top, bottom).astype(BF16)


def edges(features):
    chans, rows, cols = features.shape
    vm = pl.BlockSpec(memory_space=pltpu.VMEM)
    return pl.pallas_call(
        edges_kernel,
        out_shape=[pltpu.VMEM((chans, cols), BF16)] * 2,
        in_specs=[pl.BlockSpec(memory_space=pltpu.HBM)],
        out_specs=[vm] * 2,
        scratch_shapes=[pltpu.VMEM((2, chans, 16, cols), BF16), pltpu.SemaphoreType.DMA((2,))],
        compiler_params=pltpu.CompilerParams(vmem_limit_bytes=VMEM_LIMIT),
        name="edges",
    )(pltpu.with_memory_space_constraint(features, pltpu.HBM))


def prepare_kernel(colors, chans, feat, weight, bias, tile, table, ring_table, bias_rows, taps, bias_in, sems):
    step = 16
    copies = fetch(
        [
            pltpu.make_async_copy(weight, taps, sems.at[0]),
            pltpu.make_async_copy(bias, bias_in, sems.at[1]),
        ]
        + [
            pltpu.make_async_copy(feat.at[pl.ds(i * (chans // 8), chans // 8)], tile.at[pl.ds(i * (chans // 8), chans // 8)], sems.at[2 + i])
            for i in range(8)
        ]
    )
    copies[0].wait()
    wide = chans * step
    c_of = lax.broadcasted_iota(jnp.int32, (chans, wide), 1) // step
    spread = (c_of == lax.broadcasted_iota(jnp.int32, (chans, wide), 0)).astype(F32).astype(BF16)
    x_in = lax.broadcasted_iota(jnp.int32, (step + 8, wide), 1) % step
    row = lax.broadcasted_iota(jnp.int32, (step + 8, wide), 0)
    masks = []
    for u in range(3):
        main = (row < step) & (x_in - row + 1 == u)
        if u == 0:
            main = main | ((row == step) & (x_in == step - 1))
        if u == 2:
            main = main | ((row == step + 7) & (x_in == 0))
        masks.append(main)
    sub = lax.broadcasted_iota(jnp.int32, (8, chans), 0)
    for o in range(colors):
        spreads = [dot(taps[o, u], spread) for u in range(3)]
        small = [taps[o, u].astype(F32) for u in range(3)]
        for v in range(3):
            total = jnp.zeros((step + 8, wide), F32)
            for u in range(3):
                total = total + jnp.where(masks[u], spreads[u][v : v + 1], 0.0)
            g = v * colors + o
            table[g * step : (g + 1) * step, :] = total[:step].astype(BF16)
            start = 3 * colors * step + 8 * g
            table[start : start + 8, :] = total[step:].astype(BF16)
            ring_table[0, 8 * g : 8 * g + 8, :] = jnp.where(sub == 0, small[0][v : v + 1], 0.0).astype(BF16)
            ring_table[1, 8 * g : 8 * g + 8, :] = jnp.where(sub == 7, small[2][v : v + 1], 0.0).astype(BF16)
    copies[1].wait()
    for o in range(colors):
        bias_rows[o : o + 1, :] = jnp.full((1, TILE), bias_in[o], F32)
    for copy in copies[2:]:
        copy.wait()


def prepare(features, conv_weight, bias):
    chans, rows, cols = features.shape
    colors = bias.shape[0]
    weight = conv_weight.transpose(0, 2, 3, 1)
    hbm = pl.BlockSpec(memory_space=pltpu.HBM)
    vm = pl.BlockSpec(memory_space=pltpu.VMEM)
    return pl.pallas_call(
        partial(prepare_kernel, colors, chans),
        out_shape=[
            pltpu.VMEM(features.shape, BF16),
            pltpu.VMEM((3 * colors * 24, chans * 16), BF16),
            pltpu.VMEM((2, 3 * colors * 8, chans), BF16),
            pltpu.VMEM((colors, TILE), F32),
        ],
        in_specs=[hbm] * 3,
        out_specs=[vm] * 4,
        scratch_shapes=[
            pltpu.VMEM(weight.shape, BF16),
            pltpu.SMEM(bias.shape, F32),
            pltpu.SemaphoreType.DMA((10,)),
        ],
        compiler_params=pltpu.CompilerParams(vmem_limit_bytes=VMEM_LIMIT),
        name="prepare",
    )(*(pltpu.with_memory_space_constraint(x, pltpu.HBM) for x in (features, weight, bias)))


def head_kernel(colors, chans, band, second_halo, first_halo, feat, table, ring_table, bias, out):
    peers = out.shape[0]
    step = 16
    per = band // step
    groups = 3 * colors
    main_rows = groups * step
    me = lax.axis_index("col")

    lane = lax.broadcasted_iota(jnp.int32, (1, TILE), 1)
    lane_half = lax.broadcasted_iota(jnp.int32, (1, HALF), 1)
    outer = (lane_half == 0) | (lane_half == HALF - 1)
    sub = lax.broadcasted_iota(jnp.int32, (8, 1), 0)

    first, last = sub == 0, sub == 7

    def ring_of(block):
        return [block[v * 8 * colors : (v + 1) * 8 * colors] for v in range(3)]

    def chunk(i):
        return feat[:, i * step : (i + 1) * step, :].reshape(chans * step, TILE)

    prods = [None] * (peers * per)
    rings = [None] * (peers * per + 2)
    even = lax.axis_index("row") % 2 == 0
    one, two = first_halo[...].astype(F32), second_halo[...].astype(F32)
    above = jnp.where(even, two, one).astype(BF16)
    below = jnp.where(even, one, two).astype(BF16)
    rings[0] = ring_of(dot(ring_table[0], above))
    rings[-1] = ring_of(dot(ring_table[1], below))

    def multiply(j):
        for i in range(j * per, (j + 1) * per):
            prods[i] = dot(table[...], chunk(i))
            rings[i + 1] = ring_of(prods[i][main_rows:])

    def finish(j):
        slot = me ^ j
        total = None
        for i in range(per):
            at = j * per + i
            extra = None
            for o in range(colors):
                q = []
                for v in range(3):
                    g = v * colors + o
                    main = prods[at][g * step : (g + 1) * step]
                    top = main[:8] + jnp.where(first, rings[at][v][8 * o : 8 * o + 8], 0.0)
                    bottom = main[8:] + jnp.where(last, rings[at + 2][v][8 * o : 8 * o + 8], 0.0)
                    q.append(jnp.concatenate([top, bottom], 0))
                r0 = pltpu.roll(q[0], 1, 1)
                r2 = pltpu.roll(q[2], TILE - 1, 1)
                own = q[1] + jnp.where(lane == 0, 0.0, r0) + jnp.where(lane == TILE - 1, 0.0, r2) + bias[o : o + 1, :]
                code = jnp.exp2(CODE * jnp.tanh(own)).astype(BF16)
                row = o * band + i * step
                for h in range(2):
                    start = h * colors * band + row
                    out[slot, start : start + step, :] = code[:, h * HALF : (h + 1) * HALF]
                cross = jnp.where(lane_half == 0, r0[:, :HALF], r2[:, HALF:])
                cross = pltpu.roll(jnp.where(outer, cross, 0.0), 2, 1)
                edges = jnp.where(lane_half == 0, own[:, :HALF], own[:, HALF:])
                edges = jnp.where(outer, edges, cross)
                high = edges.astype(BF16).astype(F32)
                both = high + pltpu.roll(edges - high, edge_slot(0, 1), 1)
                shift = edge_slot(o, 0) + 64 * i
                if shift:
                    both = pltpu.roll(both, shift, 1)
                extra = both if extra is None else extra + both
            total = extra if total is None else total + extra
        base = 2 * colors * band
        out[slot, base : base + step, :] = total.astype(BF16)

    multiply(0)
    for j in range(peers):
        if j + 1 < peers:
            multiply(j + 1)
        finish(j)


def head(prepared, second_halo, first_halo, band, peers):
    features, table, ring_table, bias = prepared
    chans, rows, cols = features.shape
    colors = bias.shape[0]
    vm = pl.BlockSpec(memory_space=pltpu.VMEM)
    return pl.pallas_call(
        partial(head_kernel, colors, chans, band),
        out_shape=pltpu.VMEM((peers, 2 * colors * band + 16, HALF), BF16),
        in_specs=[vm] * 6,
        out_specs=vm,
        compiler_params=pltpu.CompilerParams(vmem_limit_bytes=VMEM_LIMIT),
        name="conv_head",
    )(second_halo, first_halo, features, table, ring_table, bias)


def sending_order(peers):
    return [*range(peers - 2, 0, -2), *range(peers - 1, 0, -2), 0]


def forward_y_kernel(colors, band, parts, *refs):
    peers = len(refs) - 7
    matrix, tw_c, tw_s, _, out, coded, left = refs[peers:]
    for i, k in enumerate(sending_order(peers)):
        coded[lax.axis_index("col") ^ k] = refs[i][...]
    step = 16
    lane = lax.broadcasted_iota(jnp.int32, (1, HALF), 1)
    width = TILE // parts

    def spread(o):
        for r in range(0, band, step):
            edge = []
            for p in range(peers):
                base = 2 * colors * band
                block = coded[p, base : base + step, :].astype(F32)
                shift = edge_slot(o, 0) + 64 * (r // step)
                if shift:
                    block = pltpu.roll(block, HALF - shift, 1)
                edge.append(block + pltpu.roll(block, HALF - edge_slot(0, 1), 1))
            cross = [pltpu.roll(x, HALF - 2, 1) for x in edge]
            zero = jnp.zeros_like(cross[0])
            fixed = []
            for p in range(peers):
                before = cross[p - 1] if p > 0 else zero
                after = cross[p + 1] if p + 1 < peers else zero
                fixed.append(CODE * jnp.tanh(edge[p] + jnp.where(lane < HALF // 2, before, after)))
            items = []
            for p in range(peers):
                for h in range(2):
                    start = (h * colors + o) * band + r
                    t = log2(coded[p, start : start + step, :].astype(F32))
                    t = jnp.where(lane == (HALF - 1) * h, fixed[p], t)
                    items.append(Pair(*sincos_half(t, 4, 1.0 / CODE)))
            for k, z in enumerate(small_dft(items, -1)):
                if k:
                    z = z.times(tw_c[k : k + 1, :], -tw_s[k : k + 1, :])
                for part, x in enumerate((z.re, z.im)):
                    high, low = split(x)
                    for j, value in enumerate((high, low, high)):
                        to = slice((2 * j + part) * HALF, (2 * j + part + 1) * HALF)
                        left[o, k, r : r + step, to] = value

    def multiply(o):
        return dot(left[o].reshape(2 * peers * band, 3 * TILE), matrix[...])

    def store(o, acc):
        code = encode(acc)
        for k in range(2 * peers):
            for q in range(parts):
                out[parts * k + q, o * band : (o + 1) * band, :] = code[k * band : (k + 1) * band, q * width : (q + 1) * width]

    held = None
    for o in range(colors):
        spread(o)
        acc = multiply(o)
        if held is not None:
            store(o - 1, held)
        held = acc
    store(colors - 1, held)


def forward_y(blocks, colors, band, parts, table):
    peers = len(blocks)
    tw_c, tw_s = dft_np(2 * peers, HALF, peers * TILE)
    vm = pl.BlockSpec(memory_space=pltpu.VMEM)
    sm = pl.BlockSpec(memory_space=pltpu.SMEM)
    matrix = tall(interleaved(complex_np(-1), parts))
    return pl.pallas_call(
        partial(forward_y_kernel, colors, band, parts),
        out_shape=pltpu.VMEM((2 * peers * parts, colors * band, TILE // parts), BF16),
        in_specs=[vm] * (peers + 3) + [pl.BlockSpec(memory_space=pl.ANY)],
        out_specs=vm,
        scratch_shapes=[
            pltpu.VMEM((peers,) + blocks[0].shape, BF16),
            pltpu.VMEM((colors, 2 * peers, band, 3 * TILE), BF16),
        ],
        compiler_params=pltpu.CompilerParams(vmem_limit_bytes=VMEM_LIMIT),
        name="forward_y",
    )(*(blocks[k] for k in sending_order(peers)), jnp.asarray(matrix), jnp.asarray(tw_c, F32), jnp.asarray(tw_s, F32), table)


def transfer_kernel(sizes, wave, travel, out):
    height, width, parts, inner, block = sizes
    position = lax.axis_index("row") * lax.axis_size("col") + lax.axis_index("col")
    k0 = position // parts
    q = position % parts
    colors, n = out.shape[0] - 1, out.shape[1]
    shape = (HALF // 4, out.shape[4])
    lane = lax.broadcasted_iota(jnp.int32, shape, 1)
    ky = k0 + inner * (block * q + lane % block)
    sy = jnp.where(ky < width // 2, ky, ky - width).astype(F32) * (1.0 / width)
    sy2 = sy * sy
    for k in range(n):
        for i in range(4):
            rows = slice(i * HALF // 4, (i + 1) * HALF // 4)
            m = lax.broadcasted_iota(jnp.int32, shape, 0) + i * HALF // 4
            half = 2 * k + lane // block
            kx = half + (height // HALF) * m
            sx = jnp.where(kx < height // 2, kx, kx - height).astype(F32) * (1.0 / height)
            f2 = sx * sx + sy2
            for color in range(colors):
                a = wave[color]
                turns = travel[0] * f2 / (a + jnp.sqrt(a * a - f2))
                turns = turns - jnp.round(turns)
                c, s = sincos_half(turns, 5, 2.0)
                out[color, k, 0, rows, :] = c * (SHRINK / height)
                out[color, k, 1, rows, :] = s * (SHRINK / height)
            turns = (half * m).astype(F32) * (1.0 / height)
            c, s = sincos_half(turns - jnp.round(turns), 5, 2.0)
            out[colors, k, 0, rows, :] = c
            out[colors, k, 1, rows, :] = s


def transfer(inv_wavelength, distance, sizes):
    height, width, parts, inner, block = sizes
    colors = inv_wavelength.shape[0]
    sm = pl.BlockSpec(memory_space=pltpu.SMEM)
    n = height // TILE
    return pl.pallas_call(
        partial(transfer_kernel, sizes),
        out_shape=pltpu.VMEM((colors + 1, n, 2, HALF, 2 * block), F32),
        in_specs=[sm] * 2,
        out_specs=pl.BlockSpec(memory_space=pltpu.VMEM),
        compiler_params=pltpu.CompilerParams(vmem_limit_bytes=VMEM_LIMIT),
        name="transfer",
    )(inv_wavelength, distance)


def middle_kernel(coded, tables, matrix, out, before, after):
    colors, n = out.shape[1], tables.shape[1]
    width = coded.shape[-1]
    block = width // 2
    per = coded.shape[0] // (2 * n)
    band = coded.shape[2]
    twiddles = tables.at[colors]
    lane = lax.broadcasted_iota(jnp.int32, (1, width), 1)
    left = lane < block
    step = 16
    turn_c = [jnp.where(left, 1.0, math.cos(math.pi * a / n)) for a in range(n)]
    turn_s = [jnp.where(left, 0.0, math.sin(math.pi * a / n)) for a in range(n)]

    def put(right, k, rows, z, order):
        for part, x in zip(order, (z.re, z.im)):
            high, low = split(x)
            for j, value in enumerate((high, high, low)):
                to = (2 * j + part) * HALF
                right[to + rows.start : to + rows.stop, k * width : (k + 1) * width] = value

    def spread(color):
        for i in range(HALF // step):
            s, r = divmod(i * step, band)
            rows = slice(i * step, (i + 1) * step)
            items = []
            for a in range(n):
                x = decode(coded[per * a + s, color, r : r + step, :])
                y = decode(coded[per * (a + n) + s, color, r : r + step, :])
                u, v = x + y, x - y
                z = Pair(jnp.where(left, u, lane_shift(v, block)), jnp.where(left, lane_shift(u, block), v))
                if a:
                    z = z.times(turn_c[a], -turn_s[a])
                items.append(z)
            for k, z in enumerate(small_dft(items, -1)):
                put(before.at[color], k, rows, z.times(twiddles[k, 0, rows, :], -twiddles[k, 1, rows, :]), (0, 1))

    def multiply(right, color):
        return dot(matrix[...], right[color])

    def filtered(color, acc):
        for k in range(n):
            cols = slice(k * width, (k + 1) * width)
            for i in range(HALF // step):
                rows = slice(i * step, (i + 1) * step)
                z = Pair(acc[rows, cols], acc[HALF + rows.start : HALF + rows.stop, cols])
                put(after.at[color], k, rows, z.times(tables[color, k, 0, rows, :], -tables[color, k, 1, rows, :]), (1, 0))

    def store(color, acc):
        for i in range(HALF // step):
            s, r = divmod(i * step, band)
            rows = slice(i * step, (i + 1) * step)
            items = []
            for k in range(n):
                cols = slice(k * width, (k + 1) * width)
                z = Pair(acc[HALF + rows.start : HALF + rows.stop, cols], acc[rows, cols])
                items.append(z.times(twiddles[k, 0, rows, :], twiddles[k, 1, rows, :]))
            for a, z in enumerate(small_dft(items, 1)):
                if a:
                    z = z.times(turn_c[a], turn_s[a])
                u = jnp.where(left, z.re, lane_shift(z.im, block))
                v = jnp.where(left, lane_shift(z.re, block), z.im)
                out[per * a + s, color, r : r + step, :] = encode(u + v)
                out[per * (a + n) + s, color, r : r + step, :] = encode(u - v)

    ahead, back = {}, {}
    for tick in range(colors + 2):
        if tick < colors:
            spread(tick)
            ahead[tick] = multiply(before, tick)
        if 0 <= tick - 1 < colors:
            filtered(tick - 1, ahead.pop(tick - 1))
            back[tick - 1] = multiply(after, tick - 1)
        if tick >= 2:
            store(tick - 2, back.pop(tick - 2))


def middle(coded, table):
    groups, colors, band, width = coded.shape
    n = table.shape[1]
    vm = pl.BlockSpec(memory_space=pltpu.VMEM)
    forward = wide(complex_np(-1).T)
    return pl.pallas_call(
        middle_kernel,
        out_shape=jax.ShapeDtypeStruct(coded.shape, BF16),
        in_specs=[vm] * 3,
        out_specs=vm,
        scratch_shapes=[pltpu.VMEM((colors, 3 * TILE, n * width), BF16)] * 2,
        compiler_params=pltpu.CompilerParams(vmem_limit_bytes=VMEM_LIMIT),
        name="middle_x",
    )(*(pltpu.with_memory_space_constraint(x, pltpu.VMEM) for x in (coded, table, jnp.asarray(forward))))


def inverse_y_kernel(parts, coded, matrix, tw_c, tw_s, target, left, out, sems):
    inner = tw_c.shape[0]
    colors, band, width = coded.shape[1], coded.shape[2], coded.shape[3]
    outs = []
    step = 16
    scale = 1.0 / (SHRINK * inner * HALF)

    def spread(o):
        for k in range(inner):
            for q in range(parts):
                high, low = split(decode(coded[parts * k + q, o]))
                for j, value in enumerate((high, low, high)):
                    left[o, k, :, j * TILE + q * width : j * TILE + (q + 1) * width] = value

    def multiply(o):
        return dot(left[o].reshape(inner * band, 3 * TILE), matrix[...])

    def store(o, acc):
        for r in range(0, band, step):
            items = []
            for k in range(inner):
                z = acc[k * band + r : k * band + r + step]
                items.append(Pair(z[:, :HALF], z[:, HALF:]).times(tw_c[k : k + 1, :] * scale, tw_s[k : k + 1, :] * scale))
            for a, z in enumerate(small_dft(items, 1)):
                out[o, 0, r : r + step, a * HALF : (a + 1) * HALF] = z.re.astype(BF16)
                out[o, 1, r : r + step, a * HALF : (a + 1) * HALF] = z.im.astype(BF16)
        outs.extend(fetch([pltpu.make_async_copy(out.at[o], target.at[o], sems.at[o])]))

    held = None
    for o in range(colors):
        spread(o)
        acc = multiply(o)
        if held is not None:
            store(o - 1, held)
        held = acc
    store(colors - 1, held)
    for copy in outs:
        copy.wait()


def inverse_y(coded, parts):
    groups, colors, band, width = coded.shape
    inner = groups // parts
    tw_c, tw_s = dft_np(inner, HALF, inner * HALF)
    matrix = tall(np.ascontiguousarray(interleaved(complex_np(1).T.copy(), parts).T))
    hbm = pl.BlockSpec(memory_space=pltpu.HBM)
    vm = pl.BlockSpec(memory_space=pltpu.VMEM)
    return pl.pallas_call(
        partial(inverse_y_kernel, parts),
        out_shape=jax.ShapeDtypeStruct((colors, 2, band, inner * HALF), BF16),
        in_specs=[vm] * 4,
        out_specs=hbm,
        scratch_shapes=[
            pltpu.VMEM((colors, inner, band, 3 * TILE), BF16),
            pltpu.VMEM((colors, 2, band, inner * HALF), BF16),
            pltpu.SemaphoreType.DMA((colors,)),
        ],
        compiler_params=pltpu.CompilerParams(vmem_limit_bytes=VMEM_LIMIT),
        name="inverse_y",
    )(coded, jnp.asarray(matrix), jnp.asarray(tw_c, F32), jnp.asarray(tw_s, F32))


def per_device(features, conv_weight, bias, inv_wavelength, distance):
    mesh_rows = lax.axis_size("row")
    mesh_cols = lax.axis_size("col")
    groups = mesh_rows * mesh_cols
    chans, tile_rows, tile_cols = features.shape
    colors = conv_weight.shape[0]
    band = tile_rows // mesh_cols
    height = tile_rows * mesh_rows
    width = tile_cols * mesh_cols
    block = width // groups
    parts = mesh_rows // 2
    edge_one, edge_two = edges(features)
    tile, *prepared = prepare(features, conv_weight, bias)
    halos = []
    for start, edge in ((1, edge_two), (0, edge_one)):
        pairs = [(i, i + 1) for i in range(start, mesh_rows - 1, 2)]
        halos.append(lax.ppermute(edge, "row", pairs + [(j, i) for i, j in pairs]))
    bands = head((tile, *prepared), *halos, band, mesh_cols)
    blocks = [bands[0]] * mesh_cols
    for k in range(mesh_cols - 1, 0, -1):
        blocks[k] = lax.ppermute(bands[k], "col", [(i, i ^ k) for i in range(mesh_cols)])
    table = transfer(inv_wavelength, distance, (height, width, parts, 2 * mesh_cols, block))
    spectrum = forward_y(blocks, colors, band, parts, table)
    spectrum = lax.all_to_all(spectrum, ("row", "col"), split_axis=0, concat_axis=0, tiled=True)
    back = middle(spectrum.reshape(groups, colors, band, 2 * block), table)
    back = lax.all_to_all(back, ("row", "col"), split_axis=0, concat_axis=0, tiled=True)
    return inverse_y(back, parts)


def solution(mesh):
    in_specs = (P(None, "row", "col"), P(), P(), P(), P())
    out_specs = P(None, None, ("row", "col"), None)
    return jax.shard_map(
        per_device, mesh=mesh, in_specs=in_specs, out_specs=out_specs, check_vma=False
    )
```

```python
from functools import partial
import math

import numpy as np
import jax
import jax.numpy as jnp
from jax import lax
from jax.experimental import pallas as pl
from jax.experimental.pallas import tpu as pltpu
from jax.sharding import PartitionSpec as P

F32 = jnp.float32
BF16 = jnp.bfloat16
TILE = 256
HALF = 128
CODE = 124.0
LOG_CODE = CODE * math.log(2.0)
TINY = 1.2e-38
SHRINK = 2.0**-4
VMEM_LIMIT = 10 * 1024 * 1024


def split_np(table):
    high = table.astype(jnp.bfloat16)
    low = (table - high.astype(np.float64)).astype(jnp.bfloat16)
    return high, low


def dft_np(rows, cols, length):
    product = np.outer(np.arange(rows), np.arange(cols)) % length
    angle = 2.0 * np.pi * product / length
    return np.cos(angle), np.sin(angle)


def interleaved(table, parts):
    rows = table.shape[0]
    return table.reshape(rows, 2, parts, HALF // parts).transpose(0, 2, 1, 3).reshape(rows, 2 * HALF)


def complex_np(sign):
    c, s = dft_np(HALF, HALF, HALF)
    return np.block([[c, sign * s], [-sign * s, c]])


def tall(table):
    high, low = split_np(table)
    return np.concatenate([high, high, low], 0)


def wide(table):
    high, low = split_np(table)
    return np.concatenate([high, low, high], 1)


def fitted(func, terms, odd):
    t = np.cos(np.pi * (np.arange(400) + 0.5) / 800)
    powers = np.stack([t ** (2 * k + odd) for k in range(terms)], 1)
    return [float(v) for v in np.linalg.lstsq(powers, func(np.pi / 2 * t), rcond=None)[0]]


def sincos_half(t, terms=5, scale=1.0):
    u = t * t
    sines = [v * scale ** (2 * k + 1) for k, v in enumerate(fitted(np.sin, terms, 1))]
    cosines = [v * scale ** (2 * k) for k, v in enumerate(fitted(np.cos, terms, 0))]
    s = sines[-1]
    for coef in sines[-2::-1]:
        s = s * u + coef
    s = s * t
    c = cosines[-1]
    for coef in cosines[-2::-1]:
        c = c * u + coef
    s2 = s + s
    return 1.0 - s2 * s, s2 * c


def encode(v):
    v2 = v * v
    v4 = v2 * v2
    return (v4 * v4 * v).astype(BF16)


def decode(w):
    w = w.astype(F32)
    return w * jnp.exp2(lax.log(jnp.maximum(jnp.abs(w), TINY)) * (-8.0 / 9.0 / math.log(2.0)))


def fetch(copies):
    for copy in copies:
        copy.start()
    return copies


def split(x):
    high = x.astype(BF16)
    return high, (x - high.astype(F32)).astype(BF16)


def dot(a, b):
    return lax.dot_general(a, b, (((1,), (0,)), ((), ())), preferred_element_type=F32)


def lane_shift(x, shift):
    width = x.shape[-1]
    shift = shift % width
    if shift == 0:
        return x
    if width % 128 == 0:
        return pltpu.roll(x, shift, x.ndim - 1)
    return jnp.concatenate([x[..., width - shift :], x[..., : width - shift]], -1)


class Pair:
    def __init__(self, re, im):
        self.re, self.im = re, im

    def __add__(self, o):
        return Pair(self.re + o.re, self.im + o.im)

    def __sub__(self, o):
        return Pair(self.re - o.re, self.im - o.im)

    def times(self, c, s):
        return Pair(self.re * c - self.im * s, self.re * s + self.im * c)


def butterfly(even, odd, k, n, sign):
    if k == 0:
        return even + odd, even - odd
    if 4 * k == n:
        plus = Pair(even.re - odd.im, even.im + odd.re)
        minus = Pair(even.re + odd.im, even.im - odd.re)
        return (plus, minus) if sign > 0 else (minus, plus)
    if 8 * k in (n, 3 * n):
        h = math.sqrt(0.5)
        a, b = (odd.re - odd.im) * h, (odd.re + odd.im) * h
        if sign > 0 and 8 * k == n:
            return Pair(even.re + a, even.im + b), Pair(even.re - a, even.im - b)
        if sign > 0:
            return Pair(even.re - b, even.im + a), Pair(even.re + b, even.im - a)
        if 8 * k == n:
            return Pair(even.re + b, even.im - a), Pair(even.re - b, even.im + a)
        return Pair(even.re - a, even.im - b), Pair(even.re + a, even.im + b)
    angle = sign * 2.0 * math.pi * k / n
    o = odd.times(math.cos(angle), math.sin(angle))
    return even + o, even - o


def small_dft(items, sign):
    n = len(items)
    if n == 1:
        return items
    even = small_dft(items[0::2], sign)
    odd = small_dft(items[1::2], sign)
    out = [None] * n
    for k in range(n // 2):
        out[k], out[k + n // 2] = butterfly(even[k], odd[k], k, n, sign)
    return out


def edge_slot(color, part):
    return 16 * color + 8 * part


def edges_kernel(feat, first_edge, second_edge, edge, sems):
    step = 16
    rows = feat.shape[1]
    copies = fetch(
        [
            pltpu.make_async_copy(feat.at[:, pl.ds(0, step), :], edge.at[0], sems.at[0]),
            pltpu.make_async_copy(feat.at[:, pl.ds(rows - step, step), :], edge.at[1], sems.at[1]),
        ]
    )
    for copy in copies:
        copy.wait()
    top = edge[0].astype(F32)[:, 0, :]
    bottom = edge[1].astype(F32)[:, step - 1, :]
    even = lax.axis_index("row") % 2 == 0
    first_edge[...] = jnp.where(even, bottom, top).astype(BF16)
    second_edge[...] = jnp.where(even, top, bottom).astype(BF16)


def edges(features):
    chans, rows, cols = features.shape
    vm = pl.BlockSpec(memory_space=pltpu.VMEM)
    return pl.pallas_call(
        edges_kernel,
        out_shape=[pltpu.VMEM((chans, cols), BF16)] * 2,
        in_specs=[pl.BlockSpec(memory_space=pltpu.HBM)],
        out_specs=[vm] * 2,
        scratch_shapes=[pltpu.VMEM((2, chans, 16, cols), BF16), pltpu.SemaphoreType.DMA((2,))],
        compiler_params=pltpu.CompilerParams(vmem_limit_bytes=VMEM_LIMIT),
        name="edges",
    )(pltpu.with_memory_space_constraint(features, pltpu.HBM))


def prepare_kernel(colors, chans, feat, weight, bias, tile, table, ring_table, bias_rows, taps, bias_in, sems):
    step = 16
    copies = fetch(
        [
            pltpu.make_async_copy(weight, taps, sems.at[0]),
            pltpu.make_async_copy(bias, bias_in, sems.at[1]),
        ]
        + [
            pltpu.make_async_copy(feat.at[pl.ds(i * (chans // 8), chans // 8)], tile.at[pl.ds(i * (chans // 8), chans // 8)], sems.at[2 + i])
            for i in range(8)
        ]
    )
    copies[0].wait()
    wide = chans * step
    c_of = lax.broadcasted_iota(jnp.int32, (chans, wide), 1) // step
    spread = (c_of == lax.broadcasted_iota(jnp.int32, (chans, wide), 0)).astype(F32).astype(BF16)
    x_in = lax.broadcasted_iota(jnp.int32, (step + 8, wide), 1) % step
    row = lax.broadcasted_iota(jnp.int32, (step + 8, wide), 0)
    masks = []
    for u in range(3):
        main = (row < step) & (x_in - row + 1 == u)
        if u == 0:
            main = main | ((row == step) & (x_in == step - 1))
        if u == 2:
            main = main | ((row == step + 7) & (x_in == 0))
        masks.append(main)
    sub = lax.broadcasted_iota(jnp.int32, (8, chans), 0)
    for o in range(colors):
        spreads = [dot(taps[o, u], spread) for u in range(3)]
        small = [taps[o, u].astype(F32) for u in range(3)]
        for v in range(3):
            total = jnp.zeros((step + 8, wide), F32)
            for u in range(3):
                total = total + jnp.where(masks[u], spreads[u][v : v + 1], 0.0)
            g = v * colors + o
            table[g * step : (g + 1) * step, :] = total[:step].astype(BF16)
            start = 3 * colors * step + 8 * g
            table[start : start + 8, :] = total[step:].astype(BF16)
            ring_table[0, 8 * g : 8 * g + 8, :] = jnp.where(sub == 0, small[0][v : v + 1], 0.0).astype(BF16)
            ring_table[1, 8 * g : 8 * g + 8, :] = jnp.where(sub == 7, small[2][v : v + 1], 0.0).astype(BF16)
    copies[1].wait()
    for o in range(colors):
        bias_rows[o : o + 1, :] = jnp.full((1, TILE), bias_in[o], F32)
    for copy in copies[2:]:
        copy.wait()


def prepare(features, conv_weight, bias):
    chans, rows, cols = features.shape
    colors = bias.shape[0]
    weight = conv_weight.transpose(0, 2, 3, 1)
    hbm = pl.BlockSpec(memory_space=pltpu.HBM)
    vm = pl.BlockSpec(memory_space=pltpu.VMEM)
    return pl.pallas_call(
        partial(prepare_kernel, colors, chans),
        out_shape=[
            pltpu.VMEM(features.shape, BF16),
            pltpu.VMEM((3 * colors * 24, chans * 16), BF16),
            pltpu.VMEM((2, 3 * colors * 8, chans), BF16),
            pltpu.VMEM((colors, TILE), F32),
        ],
        in_specs=[hbm] * 3,
        out_specs=[vm] * 4,
        scratch_shapes=[
            pltpu.VMEM(weight.shape, BF16),
            pltpu.SMEM(bias.shape, F32),
            pltpu.SemaphoreType.DMA((10,)),
        ],
        compiler_params=pltpu.CompilerParams(vmem_limit_bytes=VMEM_LIMIT),
        name="prepare",
    )(*(pltpu.with_memory_space_constraint(x, pltpu.HBM) for x in (features, weight, bias)))


def head_kernel(colors, chans, band, second_halo, first_halo, feat, table, ring_table, bias, out):
    peers = out.shape[0]
    step = 16
    per = band // step
    groups = 3 * colors
    main_rows = groups * step
    me = lax.axis_index("col")

    lane = lax.broadcasted_iota(jnp.int32, (1, TILE), 1)
    lane_half = lax.broadcasted_iota(jnp.int32, (1, HALF), 1)
    outer = (lane_half == 0) | (lane_half == HALF - 1)
    sub = lax.broadcasted_iota(jnp.int32, (8, 1), 0)

    first, last = sub == 0, sub == 7

    def ring_of(block):
        return [block[v * 8 * colors : (v + 1) * 8 * colors] for v in range(3)]

    def chunk(i):
        return feat[:, i * step : (i + 1) * step, :].reshape(chans * step, TILE)

    prods = [None] * (peers * per)
    rings = [None] * (peers * per + 2)
    even = lax.axis_index("row") % 2 == 0
    one, two = first_halo[...].astype(F32), second_halo[...].astype(F32)
    above = jnp.where(even, two, one).astype(BF16)
    below = jnp.where(even, one, two).astype(BF16)
    rings[0] = ring_of(dot(ring_table[0], above))
    rings[-1] = ring_of(dot(ring_table[1], below))

    def multiply(j):
        for i in range(j * per, (j + 1) * per):
            prods[i] = dot(table[...], chunk(i))
            rings[i + 1] = ring_of(prods[i][main_rows:])

    def finish(j):
        slot = me ^ j
        total = None
        for i in range(per):
            at = j * per + i
            extra = None
            for o in range(colors):
                q = []
                for v in range(3):
                    g = v * colors + o
                    main = prods[at][g * step : (g + 1) * step]
                    top = main[:8] + jnp.where(first, rings[at][v][8 * o : 8 * o + 8], 0.0)
                    bottom = main[8:] + jnp.where(last, rings[at + 2][v][8 * o : 8 * o + 8], 0.0)
                    q.append(jnp.concatenate([top, bottom], 0))
                r0 = pltpu.roll(q[0], 1, 1)
                r2 = pltpu.roll(q[2], TILE - 1, 1)
                own = q[1] + jnp.where(lane == 0, 0.0, r0) + jnp.where(lane == TILE - 1, 0.0, r2) + bias[o : o + 1, :]
                code = jnp.exp2(CODE * jnp.tanh(own)).astype(BF16)
                row = o * band + i * step
                for h in range(2):
                    start = h * colors * band + row
                    out[slot, start : start + step, :] = code[:, h * HALF : (h + 1) * HALF]
                cross = jnp.where(lane_half == 0, r0[:, :HALF], r2[:, HALF:])
                cross = pltpu.roll(jnp.where(outer, cross, 0.0), 2, 1)
                edges = jnp.where(lane_half == 0, own[:, :HALF], own[:, HALF:])
                edges = jnp.where(outer, edges, cross)
                high = edges.astype(BF16).astype(F32)
                both = high + pltpu.roll(edges - high, edge_slot(0, 1), 1)
                shift = edge_slot(o, 0) + 64 * i
                if shift:
                    both = pltpu.roll(both, shift, 1)
                extra = both if extra is None else extra + both
            total = extra if total is None else total + extra
        base = 2 * colors * band
        out[slot, base : base + step, :] = total.astype(BF16)

    multiply(0)
    for j in range(peers):
        if j + 1 < peers:
            multiply(j + 1)
        finish(j)


def head(prepared, second_halo, first_halo, band, peers):
    features, table, ring_table, bias = prepared
    chans, rows, cols = features.shape
    colors = bias.shape[0]
    vm = pl.BlockSpec(memory_space=pltpu.VMEM)
    return pl.pallas_call(
        partial(head_kernel, colors, chans, band),
        out_shape=pltpu.VMEM((peers, 2 * colors * band + 16, HALF), BF16),
        in_specs=[vm] * 6,
        out_specs=vm,
        compiler_params=pltpu.CompilerParams(vmem_limit_bytes=VMEM_LIMIT),
        name="conv_head",
    )(second_halo, first_halo, features, table, ring_table, bias)


def sending_order(peers):
    return [*range(peers - 2, 0, -2), *range(peers - 1, 0, -2), 0]


def forward_y_kernel(colors, band, parts, *refs):
    peers = len(refs) - 7
    matrix, tw_c, tw_s, _, out, coded, left = refs[peers:]
    for i, k in enumerate(sending_order(peers)):
        coded[lax.axis_index("col") ^ k] = refs[i][...]
    step = 16
    lane = lax.broadcasted_iota(jnp.int32, (1, HALF), 1)
    width = TILE // parts

    def spread(o):
        for r in range(0, band, step):
            edge = []
            for p in range(peers):
                base = 2 * colors * band
                block = coded[p, base : base + step, :].astype(F32)
                shift = edge_slot(o, 0) + 64 * (r // step)
                if shift:
                    block = pltpu.roll(block, HALF - shift, 1)
                edge.append(block + pltpu.roll(block, HALF - edge_slot(0, 1), 1))
            cross = [pltpu.roll(x, HALF - 2, 1) for x in edge]
            zero = jnp.zeros_like(cross[0])
            fixed = []
            for p in range(peers):
                before = cross[p - 1] if p > 0 else zero
                after = cross[p + 1] if p + 1 < peers else zero
                fixed.append(LOG_CODE * jnp.tanh(edge[p] + jnp.where(lane < HALF // 2, before, after)))
            items = []
            for p in range(peers):
                for h in range(2):
                    start = (h * colors + o) * band + r
                    t = lax.log(coded[p, start : start + step, :].astype(F32))
                    t = jnp.where(lane == (HALF - 1) * h, fixed[p], t)
                    items.append(Pair(*sincos_half(t, 4, 1.0 / LOG_CODE)))
            for k, z in enumerate(small_dft(items, -1)):
                if k:
                    z = z.times(tw_c[k : k + 1, :], -tw_s[k : k + 1, :])
                for part, x in enumerate((z.re, z.im)):
                    high, low = split(x)
                    for j, value in enumerate((high, low, high)):
                        to = slice((2 * j + part) * HALF, (2 * j + part + 1) * HALF)
                        left[o, k, r : r + step, to] = value

    def multiply(o):
        return dot(left[o].reshape(2 * peers * band, 3 * TILE), matrix[...])

    def store(o, acc):
        code = encode(acc)
        for k in range(2 * peers):
            for q in range(parts):
                out[parts * k + q, o * band : (o + 1) * band, :] = code[k * band : (k + 1) * band, q * width : (q + 1) * width]

    held = None
    for o in range(colors):
        spread(o)
        acc = multiply(o)
        if held is not None:
            store(o - 1, held)
        held = acc
    store(colors - 1, held)


def forward_y(blocks, colors, band, parts, table):
    peers = len(blocks)
    tw_c, tw_s = dft_np(2 * peers, HALF, peers * TILE)
    vm = pl.BlockSpec(memory_space=pltpu.VMEM)
    sm = pl.BlockSpec(memory_space=pltpu.SMEM)
    matrix = tall(interleaved(complex_np(-1), parts))
    return pl.pallas_call(
        partial(forward_y_kernel, colors, band, parts),
        out_shape=pltpu.VMEM((2 * peers * parts, colors * band, TILE // parts), BF16),
        in_specs=[vm] * (peers + 3) + [pl.BlockSpec(memory_space=pl.ANY)],
        out_specs=vm,
        scratch_shapes=[
            pltpu.VMEM((peers,) + blocks[0].shape, BF16),
            pltpu.VMEM((colors, 2 * peers, band, 3 * TILE), BF16),
        ],
        compiler_params=pltpu.CompilerParams(vmem_limit_bytes=VMEM_LIMIT),
        name="forward_y",
    )(*(blocks[k] for k in sending_order(peers)), jnp.asarray(matrix), jnp.asarray(tw_c, F32), jnp.asarray(tw_s, F32), table)


def transfer_kernel(sizes, wave, travel, out):
    height, width, parts, inner, block = sizes
    position = lax.axis_index("row") * lax.axis_size("col") + lax.axis_index("col")
    k0 = position // parts
    q = position % parts
    colors, n = out.shape[0] - 1, out.shape[1]
    shape = (HALF // 4, out.shape[4])
    lane = lax.broadcasted_iota(jnp.int32, shape, 1)
    ky = k0 + inner * (block * q + lane % block)
    sy = jnp.where(ky < width // 2, ky, ky - width).astype(F32) * (1.0 / width)
    sy2 = sy * sy
    for k in range(n):
        for i in range(4):
            rows = slice(i * HALF // 4, (i + 1) * HALF // 4)
            m = lax.broadcasted_iota(jnp.int32, shape, 0) + i * HALF // 4
            half = 2 * k + lane // block
            kx = half + (height // HALF) * m
            sx = jnp.where(kx < height // 2, kx, kx - height).astype(F32) * (1.0 / height)
            f2 = sx * sx + sy2
            for color in range(colors):
                a = wave[color]
                turns = travel[0] * f2 / (a + jnp.sqrt(a * a - f2))
                turns = turns - jnp.round(turns)
                c, s = sincos_half(turns, 4, 2.0)
                out[color, k, 0, rows, :] = c * (SHRINK / height)
                out[color, k, 1, rows, :] = s * (SHRINK / height)
            turns = (half * m).astype(F32) * (1.0 / height)
            c, s = sincos_half(turns - jnp.round(turns), 5, 2.0)
            out[colors, k, 0, rows, :] = c
            out[colors, k, 1, rows, :] = s


def transfer(inv_wavelength, distance, sizes):
    height, width, parts, inner, block = sizes
    colors = inv_wavelength.shape[0]
    sm = pl.BlockSpec(memory_space=pltpu.SMEM)
    n = height // TILE
    return pl.pallas_call(
        partial(transfer_kernel, sizes),
        out_shape=pltpu.VMEM((colors + 1, n, 2, HALF, 2 * block), F32),
        in_specs=[sm] * 2,
        out_specs=pl.BlockSpec(memory_space=pltpu.VMEM),
        compiler_params=pltpu.CompilerParams(vmem_limit_bytes=VMEM_LIMIT),
        name="transfer",
    )(inv_wavelength, distance)


def middle_kernel(coded, tables, matrix, out, before, after):
    colors, n = out.shape[1], tables.shape[1]
    width = coded.shape[-1]
    block = width // 2
    per = coded.shape[0] // (2 * n)
    band = coded.shape[2]
    twiddles = tables.at[colors]
    lane = lax.broadcasted_iota(jnp.int32, (1, width), 1)
    left = lane < block
    step = 16
    turn_c = [jnp.where(left, 1.0, math.cos(math.pi * a / n)) for a in range(n)]
    turn_s = [jnp.where(left, 0.0, math.sin(math.pi * a / n)) for a in range(n)]

    def put(right, k, rows, z, order):
        for part, x in zip(order, (z.re, z.im)):
            high, low = split(x)
            for j, value in enumerate((high, high, low)):
                to = (2 * j + part) * HALF
                right[to + rows.start : to + rows.stop, k * width : (k + 1) * width] = value

    def spread(color):
        for i in range(HALF // step):
            s, r = divmod(i * step, band)
            rows = slice(i * step, (i + 1) * step)
            items = []
            for a in range(n):
                x = decode(coded[per * a + s, color, r : r + step, :])
                y = decode(coded[per * (a + n) + s, color, r : r + step, :])
                u, v = x + y, x - y
                z = Pair(jnp.where(left, u, lane_shift(v, block)), jnp.where(left, lane_shift(u, block), v))
                if a:
                    z = z.times(turn_c[a], -turn_s[a])
                items.append(z)
            for k, z in enumerate(small_dft(items, -1)):
                put(before.at[color], k, rows, z.times(twiddles[k, 0, rows, :], -twiddles[k, 1, rows, :]), (0, 1))

    def multiply(right, color):
        return dot(matrix[...], right[color])

    def filtered(color, acc):
        for k in range(n):
            cols = slice(k * width, (k + 1) * width)
            for i in range(HALF // step):
                rows = slice(i * step, (i + 1) * step)
                z = Pair(acc[rows, cols], acc[HALF + rows.start : HALF + rows.stop, cols])
                put(after.at[color], k, rows, z.times(tables[color, k, 0, rows, :], -tables[color, k, 1, rows, :]), (1, 0))

    def store(color, acc):
        for i in range(HALF // step):
            s, r = divmod(i * step, band)
            rows = slice(i * step, (i + 1) * step)
            items = []
            for k in range(n):
                cols = slice(k * width, (k + 1) * width)
                z = Pair(acc[HALF + rows.start : HALF + rows.stop, cols], acc[rows, cols])
                items.append(z.times(twiddles[k, 0, rows, :], twiddles[k, 1, rows, :]))
            for a, z in enumerate(small_dft(items, 1)):
                if a:
                    z = z.times(turn_c[a], turn_s[a])
                u = jnp.where(left, z.re, lane_shift(z.im, block))
                v = jnp.where(left, lane_shift(z.re, block), z.im)
                out[per * a + s, color, r : r + step, :] = encode(u + v)
                out[per * (a + n) + s, color, r : r + step, :] = encode(u - v)

    ahead, back = {}, {}
    for tick in range(colors + 2):
        if tick < colors:
            spread(tick)
            ahead[tick] = multiply(before, tick)
        if 0 <= tick - 1 < colors:
            filtered(tick - 1, ahead.pop(tick - 1))
            back[tick - 1] = multiply(after, tick - 1)
        if tick >= 2:
            store(tick - 2, back.pop(tick - 2))


def middle(coded, table):
    groups, colors, band, width = coded.shape
    n = table.shape[1]
    vm = pl.BlockSpec(memory_space=pltpu.VMEM)
    forward = wide(complex_np(-1).T)
    return pl.pallas_call(
        middle_kernel,
        out_shape=jax.ShapeDtypeStruct(coded.shape, BF16),
        in_specs=[vm] * 3,
        out_specs=vm,
        scratch_shapes=[pltpu.VMEM((colors, 3 * TILE, n * width), BF16)] * 2,
        compiler_params=pltpu.CompilerParams(vmem_limit_bytes=VMEM_LIMIT),
        name="middle_x",
    )(*(pltpu.with_memory_space_constraint(x, pltpu.VMEM) for x in (coded, table, jnp.asarray(forward))))


def inverse_y_kernel(parts, coded, matrix, tw_c, tw_s, target, left, out, sems):
    inner = tw_c.shape[0]
    colors, band, width = coded.shape[1], coded.shape[2], coded.shape[3]
    outs = []
    step = 16
    scale = 1.0 / (SHRINK * inner * HALF)

    def spread(o):
        for k in range(inner):
            for q in range(parts):
                high, low = split(decode(coded[parts * k + q, o]))
                for j, value in enumerate((high, low, high)):
                    left[o, k, :, j * TILE + q * width : j * TILE + (q + 1) * width] = value

    def multiply(o):
        return dot(left[o].reshape(inner * band, 3 * TILE), matrix[...])

    def store(o, acc):
        for r in range(0, band, step):
            items = []
            for k in range(inner):
                z = acc[k * band + r : k * band + r + step]
                items.append(Pair(z[:, :HALF], z[:, HALF:]).times(tw_c[k : k + 1, :] * scale, tw_s[k : k + 1, :] * scale))
            for a, z in enumerate(small_dft(items, 1)):
                out[o, 0, r : r + step, a * HALF : (a + 1) * HALF] = z.re.astype(BF16)
                out[o, 1, r : r + step, a * HALF : (a + 1) * HALF] = z.im.astype(BF16)
        outs.extend(fetch([pltpu.make_async_copy(out.at[o], target.at[o], sems.at[o])]))

    held = None
    for o in range(colors):
        spread(o)
        acc = multiply(o)
        if held is not None:
            store(o - 1, held)
        held = acc
    store(colors - 1, held)
    for copy in outs:
        copy.wait()


def inverse_y(coded, parts):
    groups, colors, band, width = coded.shape
    inner = groups // parts
    tw_c, tw_s = dft_np(inner, HALF, inner * HALF)
    matrix = tall(np.ascontiguousarray(interleaved(complex_np(1).T.copy(), parts).T))
    hbm = pl.BlockSpec(memory_space=pltpu.HBM)
    vm = pl.BlockSpec(memory_space=pltpu.VMEM)
    return pl.pallas_call(
        partial(inverse_y_kernel, parts),
        out_shape=jax.ShapeDtypeStruct((colors, 2, band, inner * HALF), BF16),
        in_specs=[vm] * 4,
        out_specs=hbm,
        scratch_shapes=[
            pltpu.VMEM((colors, inner, band, 3 * TILE), BF16),
            pltpu.VMEM((colors, 2, band, inner * HALF), BF16),
            pltpu.SemaphoreType.DMA((colors,)),
        ],
        compiler_params=pltpu.CompilerParams(vmem_limit_bytes=VMEM_LIMIT),
        name="inverse_y",
    )(coded, jnp.asarray(matrix), jnp.asarray(tw_c, F32), jnp.asarray(tw_s, F32))


def per_device(features, conv_weight, bias, inv_wavelength, distance):
    mesh_rows = lax.axis_size("row")
    mesh_cols = lax.axis_size("col")
    groups = mesh_rows * mesh_cols
    chans, tile_rows, tile_cols = features.shape
    colors = conv_weight.shape[0]
    band = tile_rows // mesh_cols
    height = tile_rows * mesh_rows
    width = tile_cols * mesh_cols
    block = width // groups
    parts = mesh_rows // 2
    edge_one, edge_two = edges(features)
    tile, *prepared = prepare(features, conv_weight, bias)
    halos = []
    for start, edge in ((1, edge_two), (0, edge_one)):
        pairs = [(i, i + 1) for i in range(start, mesh_rows - 1, 2)]
        halos.append(lax.ppermute(edge, "row", pairs + [(j, i) for i, j in pairs]))
    bands = head((tile, *prepared), *halos, band, mesh_cols)
    blocks = [bands[0]] * mesh_cols
    for k in range(mesh_cols - 1, 0, -1):
        blocks[k] = lax.ppermute(bands[k], "col", [(i, i ^ k) for i in range(mesh_cols)])
    table = transfer(inv_wavelength, distance, (height, width, parts, 2 * mesh_cols, block))
    spectrum = forward_y(blocks, colors, band, parts, table)
    spectrum = lax.all_to_all(spectrum, ("row", "col"), split_axis=0, concat_axis=0, tiled=True)
    back = middle(spectrum.reshape(groups, colors, band, 2 * block), table)
    back = lax.all_to_all(back, ("row", "col"), split_axis=0, concat_axis=0, tiled=True)
    return inverse_y(back, parts)


def solution(mesh):
    in_specs = (P(None, "row", "col"), P(), P(), P(), P())
    out_specs = P(None, None, ("row", "col"), None)
    return jax.shard_map(
        per_device, mesh=mesh, in_specs=in_specs, out_specs=out_specs, check_vma=False
    )
```

```python
from functools import partial
import math

import numpy as np
import jax
import jax.numpy as jnp
from jax import lax
from jax.experimental import pallas as pl
from jax.experimental.pallas import tpu as pltpu
from jax.sharding import PartitionSpec as P

F32 = jnp.float32
BF16 = jnp.bfloat16
TILE = 256
HALF = 128
CODE = 124.0
LOG_CODE = CODE * math.log(2.0)
TINY = 1.2e-38
SHRINK = 2.0**-4
VMEM_LIMIT = 10 * 1024 * 1024


def split_np(table):
    high = table.astype(jnp.bfloat16)
    low = (table - high.astype(np.float64)).astype(jnp.bfloat16)
    return high, low


def dft_np(rows, cols, length):
    product = np.outer(np.arange(rows), np.arange(cols)) % length
    angle = 2.0 * np.pi * product / length
    return np.cos(angle), np.sin(angle)


def interleaved(table, parts):
    rows = table.shape[0]
    return table.reshape(rows, 2, parts, HALF // parts).transpose(0, 2, 1, 3).reshape(rows, 2 * HALF)


def complex_np(sign):
    c, s = dft_np(HALF, HALF, HALF)
    return np.block([[c, sign * s], [-sign * s, c]])


def tall(table):
    high, low = split_np(table)
    return np.concatenate([high, high, low], 0)


def wide(table):
    high, low = split_np(table)
    return np.concatenate([high, low, high], 1)


def fitted(func, terms, odd):
    t = np.cos(np.pi * (np.arange(400) + 0.5) / 800)
    powers = np.stack([t ** (2 * k + odd) for k in range(terms)], 1)
    return [float(v) for v in np.linalg.lstsq(powers, func(np.pi / 2 * t), rcond=None)[0]]


def sincos_half(t, terms=5, scale=1.0):
    u = t * t
    sines = [v * scale ** (2 * k + 1) for k, v in enumerate(fitted(np.sin, terms, 1))]
    cosines = [v * scale ** (2 * k) for k, v in enumerate(fitted(np.cos, terms, 0))]
    s = sines[-1]
    for coef in sines[-2::-1]:
        s = s * u + coef
    s = s * t
    c = cosines[-1]
    for coef in cosines[-2::-1]:
        c = c * u + coef
    s2 = s + s
    return 1.0 - s2 * s, s2 * c


def encode(v):
    v2 = v * v
    v4 = v2 * v2
    return (v4 * v4 * v).astype(BF16)


def decode(w):
    w = w.astype(F32)
    return w * jnp.exp2(lax.log(jnp.maximum(jnp.abs(w), TINY)) * (-8.0 / 9.0 / math.log(2.0)))


def fetch(copies):
    for copy in copies:
        copy.start()
    return copies


def split(x):
    high = x.astype(BF16)
    return high, (x - high.astype(F32)).astype(BF16)


def dot(a, b):
    return lax.dot_general(a, b, (((1,), (0,)), ((), ())), preferred_element_type=F32)


def lane_shift(x, shift):
    width = x.shape[-1]
    shift = shift % width
    if shift == 0:
        return x
    if width % 128 == 0:
        return pltpu.roll(x, shift, x.ndim - 1)
    return jnp.concatenate([x[..., width - shift :], x[..., : width - shift]], -1)


class Pair:
    def __init__(self, re, im):
        self.re, self.im = re, im

    def __add__(self, o):
        return Pair(self.re + o.re, self.im + o.im)

    def __sub__(self, o):
        return Pair(self.re - o.re, self.im - o.im)

    def times(self, c, s):
        return Pair(self.re * c - self.im * s, self.re * s + self.im * c)


def butterfly(even, odd, k, n, sign):
    if k == 0:
        return even + odd, even - odd
    if 4 * k == n:
        plus = Pair(even.re - odd.im, even.im + odd.re)
        minus = Pair(even.re + odd.im, even.im - odd.re)
        return (plus, minus) if sign > 0 else (minus, plus)
    if 8 * k in (n, 3 * n):
        h = math.sqrt(0.5)
        a, b = (odd.re - odd.im) * h, (odd.re + odd.im) * h
        if sign > 0 and 8 * k == n:
            return Pair(even.re + a, even.im + b), Pair(even.re - a, even.im - b)
        if sign > 0:
            return Pair(even.re - b, even.im + a), Pair(even.re + b, even.im - a)
        if 8 * k == n:
            return Pair(even.re + b, even.im - a), Pair(even.re - b, even.im + a)
        return Pair(even.re - a, even.im - b), Pair(even.re + a, even.im + b)
    angle = sign * 2.0 * math.pi * k / n
    o = odd.times(math.cos(angle), math.sin(angle))
    return even + o, even - o


def small_dft(items, sign):
    n = len(items)
    if n == 1:
        return items
    even = small_dft(items[0::2], sign)
    odd = small_dft(items[1::2], sign)
    out = [None] * n
    for k in range(n // 2):
        out[k], out[k + n // 2] = butterfly(even[k], odd[k], k, n, sign)
    return out


def edge_slot(color, part):
    return 16 * color + 8 * part


def edges_kernel(feat, first_edge, second_edge, edge, sems):
    step = 16
    rows = feat.shape[1]
    copies = fetch(
        [
            pltpu.make_async_copy(feat.at[:, pl.ds(0, step), :], edge.at[0], sems.at[0]),
            pltpu.make_async_copy(feat.at[:, pl.ds(rows - step, step), :], edge.at[1], sems.at[1]),
        ]
    )
    for copy in copies:
        copy.wait()
    top = edge[0].astype(F32)[:, 0, :]
    bottom = edge[1].astype(F32)[:, step - 1, :]
    even = lax.axis_index("row") % 2 == 0
    first_edge[...] = jnp.where(even, bottom, top).astype(BF16)
    second_edge[...] = jnp.where(even, top, bottom).astype(BF16)


def edges(features):
    chans, rows, cols = features.shape
    vm = pl.BlockSpec(memory_space=pltpu.VMEM)
    return pl.pallas_call(
        edges_kernel,
        out_shape=[pltpu.VMEM((chans, cols), BF16)] * 2,
        in_specs=[pl.BlockSpec(memory_space=pltpu.HBM)],
        out_specs=[vm] * 2,
        scratch_shapes=[pltpu.VMEM((2, chans, 16, cols), BF16), pltpu.SemaphoreType.DMA((2,))],
        compiler_params=pltpu.CompilerParams(vmem_limit_bytes=VMEM_LIMIT),
        name="edges",
    )(pltpu.with_memory_space_constraint(features, pltpu.HBM))


def prepare_kernel(colors, chans, feat, weight, bias, tile, table, ring_table, bias_rows, taps, bias_in, sems):
    step = 16
    copies = fetch(
        [
            pltpu.make_async_copy(weight, taps, sems.at[0]),
            pltpu.make_async_copy(bias, bias_in, sems.at[1]),
        ]
        + [
            pltpu.make_async_copy(feat.at[pl.ds(i * (chans // 8), chans // 8)], tile.at[pl.ds(i * (chans // 8), chans // 8)], sems.at[2 + i])
            for i in range(8)
        ]
    )
    copies[0].wait()
    wide = chans * step
    c_of = lax.broadcasted_iota(jnp.int32, (chans, wide), 1) // step
    spread = (c_of == lax.broadcasted_iota(jnp.int32, (chans, wide), 0)).astype(F32).astype(BF16)
    x_in = lax.broadcasted_iota(jnp.int32, (step + 8, wide), 1) % step
    row = lax.broadcasted_iota(jnp.int32, (step + 8, wide), 0)
    masks = []
    for u in range(3):
        main = (row < step) & (x_in - row + 1 == u)
        if u == 0:
            main = main | ((row == step) & (x_in == step - 1))
        if u == 2:
            main = main | ((row == step + 7) & (x_in == 0))
        masks.append(main)
    sub = lax.broadcasted_iota(jnp.int32, (8, chans), 0)
    for o in range(colors):
        spreads = [dot(taps[o, u], spread) for u in range(3)]
        small = [taps[o, u].astype(F32) for u in range(3)]
        for v in range(3):
            total = jnp.zeros((step + 8, wide), F32)
            for u in range(3):
                total = total + jnp.where(masks[u], spreads[u][v : v + 1], 0.0)
            g = v * colors + o
            table[g * step : (g + 1) * step, :] = total[:step].astype(BF16)
            start = 3 * colors * step + 8 * g
            table[start : start + 8, :] = total[step:].astype(BF16)
            ring_table[0, 8 * g : 8 * g + 8, :] = jnp.where(sub == 0, small[0][v : v + 1], 0.0).astype(BF16)
            ring_table[1, 8 * g : 8 * g + 8, :] = jnp.where(sub == 7, small[2][v : v + 1], 0.0).astype(BF16)
    copies[1].wait()
    for o in range(colors):
        bias_rows[o : o + 1, :] = jnp.full((1, TILE), bias_in[o], F32)
    for copy in copies[2:]:
        copy.wait()


def prepare(features, conv_weight, bias):
    chans, rows, cols = features.shape
    colors = bias.shape[0]
    weight = conv_weight.transpose(0, 2, 3, 1)
    hbm = pl.BlockSpec(memory_space=pltpu.HBM)
    vm = pl.BlockSpec(memory_space=pltpu.VMEM)
    return pl.pallas_call(
        partial(prepare_kernel, colors, chans),
        out_shape=[
            pltpu.VMEM(features.shape, BF16),
            pltpu.VMEM((3 * colors * 24, chans * 16), BF16),
            pltpu.VMEM((2, 3 * colors * 8, chans), BF16),
            pltpu.VMEM((colors, TILE), F32),
        ],
        in_specs=[hbm] * 3,
        out_specs=[vm] * 4,
        scratch_shapes=[
            pltpu.VMEM(weight.shape, BF16),
            pltpu.SMEM(bias.shape, F32),
            pltpu.SemaphoreType.DMA((10,)),
        ],
        compiler_params=pltpu.CompilerParams(vmem_limit_bytes=VMEM_LIMIT),
        name="prepare",
    )(*(pltpu.with_memory_space_constraint(x, pltpu.HBM) for x in (features, weight, bias)))


def head_kernel(colors, chans, band, second_halo, first_halo, feat, table, ring_table, bias, out):
    peers = out.shape[0]
    step = 16
    per = band // step
    groups = 3 * colors
    main_rows = groups * step
    me = lax.axis_index("col")

    lane = lax.broadcasted_iota(jnp.int32, (1, TILE), 1)
    lane_half = lax.broadcasted_iota(jnp.int32, (1, HALF), 1)
    outer = (lane_half == 0) | (lane_half == HALF - 1)
    sub = lax.broadcasted_iota(jnp.int32, (8, 1), 0)

    first, last = sub == 0, sub == 7

    def ring_of(block):
        return [block[v * 8 * colors : (v + 1) * 8 * colors] for v in range(3)]

    def chunk(i):
        return feat[:, i * step : (i + 1) * step, :].reshape(chans * step, TILE)

    prods = [None] * (peers * per)
    rings = [None] * (peers * per + 2)
    even = lax.axis_index("row") % 2 == 0
    one, two = first_halo[...].astype(F32), second_halo[...].astype(F32)
    above = jnp.where(even, two, one).astype(BF16)
    below = jnp.where(even, one, two).astype(BF16)
    rings[0] = ring_of(dot(ring_table[0], above))
    rings[-1] = ring_of(dot(ring_table[1], below))

    def multiply(j):
        for i in range(j * per, (j + 1) * per):
            prods[i] = dot(table[...], chunk(i))
            rings[i + 1] = ring_of(prods[i][main_rows:])

    def finish(j):
        slot = me ^ j
        total = None
        for i in range(per):
            at = j * per + i
            extra = None
            for o in range(colors):
                q = []
                for v in range(3):
                    g = v * colors + o
                    main = prods[at][g * step : (g + 1) * step]
                    top = main[:8] + jnp.where(first, rings[at][v][8 * o : 8 * o + 8], 0.0)
                    bottom = main[8:] + jnp.where(last, rings[at + 2][v][8 * o : 8 * o + 8], 0.0)
                    q.append(jnp.concatenate([top, bottom], 0))
                r0 = pltpu.roll(q[0], 1, 1)
                r2 = pltpu.roll(q[2], TILE - 1, 1)
                own = q[1] + jnp.where(lane == 0, 0.0, r0) + jnp.where(lane == TILE - 1, 0.0, r2) + bias[o : o + 1, :]
                code = jnp.exp2(CODE * jnp.tanh(own)).astype(BF16)
                row = o * band + i * step
                for h in range(2):
                    start = h * colors * band + row
                    out[slot, start : start + step, :] = code[:, h * HALF : (h + 1) * HALF]
                cross = jnp.where(lane_half == 0, r0[:, :HALF], r2[:, HALF:])
                cross = pltpu.roll(jnp.where(outer, cross, 0.0), 2, 1)
                edges = jnp.where(lane_half == 0, own[:, :HALF], own[:, HALF:])
                edges = jnp.where(outer, edges, cross)
                high = edges.astype(BF16).astype(F32)
                both = high + pltpu.roll(edges - high, edge_slot(0, 1), 1)
                shift = edge_slot(o, 0) + 64 * i
                if shift:
                    both = pltpu.roll(both, shift, 1)
                extra = both if extra is None else extra + both
            total = extra if total is None else total + extra
        base = 2 * colors * band
        out[slot, base : base + step, :] = total.astype(BF16)

    multiply(0)
    for j in range(peers):
        if j + 1 < peers:
            multiply(j + 1)
        finish(j)


def head(prepared, second_halo, first_halo, band, peers):
    features, table, ring_table, bias = prepared
    chans, rows, cols = features.shape
    colors = bias.shape[0]
    vm = pl.BlockSpec(memory_space=pltpu.VMEM)
    return pl.pallas_call(
        partial(head_kernel, colors, chans, band),
        out_shape=pltpu.VMEM((peers, 2 * colors * band + 16, HALF), BF16),
        in_specs=[vm] * 6,
        out_specs=vm,
        compiler_params=pltpu.CompilerParams(vmem_limit_bytes=VMEM_LIMIT),
        name="conv_head",
    )(second_halo, first_halo, features, table, ring_table, bias)


def sending_order(peers):
    half = peers // 2
    chips = [half, *(k for k in range(peers - 2, 0, -2) if k != half)]
    return [*chips, *(k + 1 for k in chips), 1, 0]


def forward_y_kernel(colors, band, parts, *refs):
    peers = len(refs) - 7
    matrix, tw_c, tw_s, _, out, coded, left = refs[peers:]
    for i, k in enumerate(sending_order(peers)):
        coded[lax.axis_index("col") ^ k] = refs[i][...]
    step = 16
    lane = lax.broadcasted_iota(jnp.int32, (1, HALF), 1)
    width = TILE // parts

    def spread(o):
        for r in range(0, band, step):
            edge = []
            for p in range(peers):
                base = 2 * colors * band
                block = coded[p, base : base + step, :].astype(F32)
                shift = edge_slot(o, 0) + 64 * (r // step)
                if shift:
                    block = pltpu.roll(block, HALF - shift, 1)
                edge.append(block + pltpu.roll(block, HALF - edge_slot(0, 1), 1))
            cross = [pltpu.roll(x, HALF - 2, 1) for x in edge]
            zero = jnp.zeros_like(cross[0])
            fixed = []
            for p in range(peers):
                before = cross[p - 1] if p > 0 else zero
                after = cross[p + 1] if p + 1 < peers else zero
                fixed.append(LOG_CODE * jnp.tanh(edge[p] + jnp.where(lane < HALF // 2, before, after)))
            items = []
            for p in range(peers):
                for h in range(2):
                    start = (h * colors + o) * band + r
                    t = lax.log(coded[p, start : start + step, :].astype(F32))
                    t = jnp.where(lane == (HALF - 1) * h, fixed[p], t)
                    items.append(Pair(*sincos_half(t, 4, 1.0 / LOG_CODE)))
            for k, z in enumerate(small_dft(items, -1)):
                if k:
                    z = z.times(tw_c[k : k + 1, :], -tw_s[k : k + 1, :])
                for part, x in enumerate((z.re, z.im)):
                    high, low = split(x)
                    for j, value in enumerate((high, low, high)):
                        to = slice((2 * j + part) * HALF, (2 * j + part + 1) * HALF)
                        left[o, k, r : r + step, to] = value

    def multiply(o):
        return dot(left[o].reshape(2 * peers * band, 3 * TILE), matrix[...])

    def store(o, acc):
        code = encode(acc)
        for k in range(2 * peers):
            for q in range(parts):
                out[parts * k + q, o * band : (o + 1) * band, :] = code[k * band : (k + 1) * band, q * width : (q + 1) * width]

    held = None
    for o in range(colors):
        spread(o)
        acc = multiply(o)
        if held is not None:
            store(o - 1, held)
        held = acc
    store(colors - 1, held)


def forward_y(blocks, colors, band, parts, table):
    peers = len(blocks)
    tw_c, tw_s = dft_np(2 * peers, HALF, peers * TILE)
    vm = pl.BlockSpec(memory_space=pltpu.VMEM)
    sm = pl.BlockSpec(memory_space=pltpu.SMEM)
    matrix = tall(interleaved(complex_np(-1), parts))
    return pl.pallas_call(
        partial(forward_y_kernel, colors, band, parts),
        out_shape=pltpu.VMEM((2 * peers * parts, colors * band, TILE // parts), BF16),
        in_specs=[vm] * (peers + 3) + [pl.BlockSpec(memory_space=pl.ANY)],
        out_specs=vm,
        scratch_shapes=[
            pltpu.VMEM((peers,) + blocks[0].shape, BF16),
            pltpu.VMEM((colors, 2 * peers, band, 3 * TILE), BF16),
        ],
        compiler_params=pltpu.CompilerParams(vmem_limit_bytes=VMEM_LIMIT),
        name="forward_y",
    )(*(blocks[k] for k in sending_order(peers)), jnp.asarray(matrix), jnp.asarray(tw_c, F32), jnp.asarray(tw_s, F32), table)


def transfer_kernel(sizes, wave, travel, out):
    height, width, parts, inner, block = sizes
    position = lax.axis_index("row") * lax.axis_size("col") + lax.axis_index("col")
    k0 = position // parts
    q = position % parts
    colors, n = out.shape[0] - 1, out.shape[1]
    shape = (HALF // 4, out.shape[4])
    lane = lax.broadcasted_iota(jnp.int32, shape, 1)
    ky = k0 + inner * (block * q + lane % block)
    sy = jnp.where(ky < width // 2, ky, ky - width).astype(F32) * (1.0 / width)
    sy2 = sy * sy
    for k in range(n):
        for i in range(4):
            rows = slice(i * HALF // 4, (i + 1) * HALF // 4)
            m = lax.broadcasted_iota(jnp.int32, shape, 0) + i * HALF // 4
            half = 2 * k + lane // block
            kx = half + (height // HALF) * m
            sx = jnp.where(kx < height // 2, kx, kx - height).astype(F32) * (1.0 / height)
            f2 = sx * sx + sy2
            for color in range(colors):
                a = wave[color]
                turns = travel[0] * f2 / (a + jnp.sqrt(a * a - f2))
                turns = turns - jnp.round(turns)
                c, s = sincos_half(turns, 4, 2.0)
                out[color, k, 0, rows, :] = c * (SHRINK / height)
                out[color, k, 1, rows, :] = s * (SHRINK / height)
            turns = (half * m).astype(F32) * (1.0 / height)
            c, s = sincos_half(turns - jnp.round(turns), 5, 2.0)
            out[colors, k, 0, rows, :] = c
            out[colors, k, 1, rows, :] = s


def transfer(inv_wavelength, distance, sizes):
    height, width, parts, inner, block = sizes
    colors = inv_wavelength.shape[0]
    sm = pl.BlockSpec(memory_space=pltpu.SMEM)
    n = height // TILE
    return pl.pallas_call(
        partial(transfer_kernel, sizes),
        out_shape=pltpu.VMEM((colors + 1, n, 2, HALF, 2 * block), F32),
        in_specs=[sm] * 2,
        out_specs=pl.BlockSpec(memory_space=pltpu.VMEM),
        compiler_params=pltpu.CompilerParams(vmem_limit_bytes=VMEM_LIMIT),
        name="transfer",
    )(inv_wavelength, distance)


def middle_kernel(coded, tables, matrix, out, before, after):
    colors, n = out.shape[1], tables.shape[1]
    width = coded.shape[-1]
    block = width // 2
    per = coded.shape[0] // (2 * n)
    band = coded.shape[2]
    twiddles = tables.at[colors]
    lane = lax.broadcasted_iota(jnp.int32, (1, width), 1)
    left = lane < block
    step = 16
    turn_c = [jnp.where(left, 1.0, math.cos(math.pi * a / n)) for a in range(n)]
    turn_s = [jnp.where(left, 0.0, math.sin(math.pi * a / n)) for a in range(n)]

    def put(right, k, rows, z, order):
        for part, x in zip(order, (z.re, z.im)):
            high, low = split(x)
            for j, value in enumerate((high, high, low)):
                to = (2 * j + part) * HALF
                right[to + rows.start : to + rows.stop, k * width : (k + 1) * width] = value

    def spread(color):
        for i in range(HALF // step):
            s, r = divmod(i * step, band)
            rows = slice(i * step, (i + 1) * step)
            items = []
            for a in range(n):
                x = decode(coded[per * a + s, color, r : r + step, :])
                y = decode(coded[per * (a + n) + s, color, r : r + step, :])
                u, v = x + y, x - y
                z = Pair(jnp.where(left, u, lane_shift(v, block)), jnp.where(left, lane_shift(u, block), v))
                if a:
                    z = z.times(turn_c[a], -turn_s[a])
                items.append(z)
            for k, z in enumerate(small_dft(items, -1)):
                put(before.at[color], k, rows, z.times(twiddles[k, 0, rows, :], -twiddles[k, 1, rows, :]), (0, 1))

    def multiply(right, color):
        return dot(matrix[...], right[color])

    def filtered(color, acc):
        for k in range(n):
            cols = slice(k * width, (k + 1) * width)
            for i in range(HALF // step):
                rows = slice(i * step, (i + 1) * step)
                z = Pair(acc[rows, cols], acc[HALF + rows.start : HALF + rows.stop, cols])
                put(after.at[color], k, rows, z.times(tables[color, k, 0, rows, :], -tables[color, k, 1, rows, :]), (1, 0))

    def store(color, acc):
        for i in range(HALF // step):
            s, r = divmod(i * step, band)
            rows = slice(i * step, (i + 1) * step)
            items = []
            for k in range(n):
                cols = slice(k * width, (k + 1) * width)
                z = Pair(acc[HALF + rows.start : HALF + rows.stop, cols], acc[rows, cols])
                items.append(z.times(twiddles[k, 0, rows, :], twiddles[k, 1, rows, :]))
            for a, z in enumerate(small_dft(items, 1)):
                if a:
                    z = z.times(turn_c[a], turn_s[a])
                u = jnp.where(left, z.re, lane_shift(z.im, block))
                v = jnp.where(left, lane_shift(z.re, block), z.im)
                out[per * a + s, color, r : r + step, :] = encode(u + v)
                out[per * (a + n) + s, color, r : r + step, :] = encode(u - v)

    ahead, back = {}, {}
    for tick in range(colors + 2):
        if tick < colors:
            spread(tick)
            ahead[tick] = multiply(before, tick)
        if 0 <= tick - 1 < colors:
            filtered(tick - 1, ahead.pop(tick - 1))
            back[tick - 1] = multiply(after, tick - 1)
        if tick >= 2:
            store(tick - 2, back.pop(tick - 2))


def middle(coded, table):
    groups, colors, band, width = coded.shape
    n = table.shape[1]
    vm = pl.BlockSpec(memory_space=pltpu.VMEM)
    forward = wide(complex_np(-1).T)
    return pl.pallas_call(
        middle_kernel,
        out_shape=jax.ShapeDtypeStruct(coded.shape, BF16),
        in_specs=[vm] * 3,
        out_specs=vm,
        scratch_shapes=[pltpu.VMEM((colors, 3 * TILE, n * width), BF16)] * 2,
        compiler_params=pltpu.CompilerParams(vmem_limit_bytes=VMEM_LIMIT),
        name="middle_x",
    )(*(pltpu.with_memory_space_constraint(x, pltpu.VMEM) for x in (coded, table, jnp.asarray(forward))))


def inverse_y_kernel(parts, coded, matrix, tw_c, tw_s, target, left, out, sems):
    inner = tw_c.shape[0]
    colors, band, width = coded.shape[1], coded.shape[2], coded.shape[3]
    outs = []
    step = 16
    scale = 1.0 / (SHRINK * inner * HALF)

    def spread(o):
        for k in range(inner):
            for q in range(parts):
                high, low = split(decode(coded[parts * k + q, o]))
                for j, value in enumerate((high, low, high)):
                    left[o, k, :, j * TILE + q * width : j * TILE + (q + 1) * width] = value

    def multiply(o):
        return dot(left[o].reshape(inner * band, 3 * TILE), matrix[...])

    def store(o, acc):
        for r in range(0, band, step):
            items = []
            for k in range(inner):
                z = acc[k * band + r : k * band + r + step]
                items.append(Pair(z[:, :HALF], z[:, HALF:]).times(tw_c[k : k + 1, :] * scale, tw_s[k : k + 1, :] * scale))
            for a, z in enumerate(small_dft(items, 1)):
                out[o, 0, r : r + step, a * HALF : (a + 1) * HALF] = z.re.astype(BF16)
                out[o, 1, r : r + step, a * HALF : (a + 1) * HALF] = z.im.astype(BF16)
        outs.extend(fetch([pltpu.make_async_copy(out.at[o], target.at[o], sems.at[o])]))

    held = None
    for o in range(colors):
        spread(o)
        acc = multiply(o)
        if held is not None:
            store(o - 1, held)
        held = acc
    store(colors - 1, held)
    for copy in outs:
        copy.wait()


def inverse_y(coded, parts):
    groups, colors, band, width = coded.shape
    inner = groups // parts
    tw_c, tw_s = dft_np(inner, HALF, inner * HALF)
    matrix = tall(np.ascontiguousarray(interleaved(complex_np(1).T.copy(), parts).T))
    hbm = pl.BlockSpec(memory_space=pltpu.HBM)
    vm = pl.BlockSpec(memory_space=pltpu.VMEM)
    return pl.pallas_call(
        partial(inverse_y_kernel, parts),
        out_shape=jax.ShapeDtypeStruct((colors, 2, band, inner * HALF), BF16),
        in_specs=[vm] * 4,
        out_specs=hbm,
        scratch_shapes=[
            pltpu.VMEM((colors, inner, band, 3 * TILE), BF16),
            pltpu.VMEM((colors, 2, band, inner * HALF), BF16),
            pltpu.SemaphoreType.DMA((colors,)),
        ],
        compiler_params=pltpu.CompilerParams(vmem_limit_bytes=VMEM_LIMIT),
        name="inverse_y",
    )(coded, jnp.asarray(matrix), jnp.asarray(tw_c, F32), jnp.asarray(tw_s, F32))


def per_device(features, conv_weight, bias, inv_wavelength, distance):
    mesh_rows = lax.axis_size("row")
    mesh_cols = lax.axis_size("col")
    groups = mesh_rows * mesh_cols
    chans, tile_rows, tile_cols = features.shape
    colors = conv_weight.shape[0]
    band = tile_rows // mesh_cols
    height = tile_rows * mesh_rows
    width = tile_cols * mesh_cols
    block = width // groups
    parts = mesh_rows // 2
    edge_one, edge_two = edges(features)
    tile, *prepared = prepare(features, conv_weight, bias)
    halos = []
    for start, edge in ((1, edge_two), (0, edge_one)):
        pairs = [(i, i + 1) for i in range(start, mesh_rows - 1, 2)]
        halos.append(lax.ppermute(edge, "row", pairs + [(j, i) for i, j in pairs]))
    bands = head((tile, *prepared), *halos, band, mesh_cols)
    blocks = [bands[0]] * mesh_cols
    for k in range(mesh_cols - 1, 0, -1):
        blocks[k] = lax.ppermute(bands[k], "col", [(i, i ^ k) for i in range(mesh_cols)])
    table = transfer(inv_wavelength, distance, (height, width, parts, 2 * mesh_cols, block))
    spectrum = forward_y(blocks, colors, band, parts, table)
    spectrum = lax.all_to_all(spectrum, ("row", "col"), split_axis=0, concat_axis=0, tiled=True)
    back = middle(spectrum.reshape(groups, colors, band, 2 * block), table)
    back = lax.all_to_all(back, ("row", "col"), split_axis=0, concat_axis=0, tiled=True)
    return inverse_y(back, parts)


def solution(mesh):
    in_specs = (P(None, "row", "col"), P(), P(), P(), P())
    out_specs = P(None, None, ("row", "col"), None)
    return jax.shard_map(
        per_device, mesh=mesh, in_specs=in_specs, out_specs=out_specs, check_vma=False
    )
```

```python
from functools import partial
import math

import numpy as np
import jax
import jax.numpy as jnp
from jax import lax
from jax.experimental import pallas as pl
from jax.experimental.pallas import tpu as pltpu
from jax.sharding import PartitionSpec as P

F32 = jnp.float32
BF16 = jnp.bfloat16
TILE = 256
HALF = 128
CODE = 124.0
TINY = 1.2e-38
SHRINK = 2.0**-4
VMEM_LIMIT = 10 * 1024 * 1024


def split_np(table):
    high = table.astype(jnp.bfloat16)
    low = (table - high.astype(np.float64)).astype(jnp.bfloat16)
    return high, low


def dft_np(rows, cols, length):
    product = np.outer(np.arange(rows), np.arange(cols)) % length
    angle = 2.0 * np.pi * product / length
    return np.cos(angle), np.sin(angle)


def interleaved(table, parts):
    rows = table.shape[0]
    return table.reshape(rows, 2, parts, HALF // parts).transpose(0, 2, 1, 3).reshape(rows, 2 * HALF)


def complex_np(sign):
    c, s = dft_np(HALF, HALF, HALF)
    return np.block([[c, sign * s], [-sign * s, c]])


def tall(table):
    high, low = split_np(table)
    return np.concatenate([high, high, low], 0)


def wide(table):
    high, low = split_np(table)
    return np.concatenate([high, low, high], 1)


def fitted(func, terms, odd):
    t = np.cos(np.pi * (np.arange(400) + 0.5) / 800)
    powers = np.stack([t ** (2 * k + odd) for k in range(terms)], 1)
    return [float(v) for v in np.linalg.lstsq(powers, func(np.pi / 2 * t), rcond=None)[0]]


def sincos_half(t, terms=5, scale=1.0):
    u = t * t
    sines = [v * scale ** (2 * k + 1) for k, v in enumerate(fitted(np.sin, terms, 1))]
    cosines = [v * scale ** (2 * k) for k, v in enumerate(fitted(np.cos, terms, 0))]
    s = sines[-1]
    for coef in sines[-2::-1]:
        s = s * u + coef
    s = s * t
    c = cosines[-1]
    for coef in cosines[-2::-1]:
        c = c * u + coef
    s2 = s + s
    return 1.0 - s2 * s, s2 * c


def log2(x):
    return lax.log(x) * (1.0 / math.log(2.0))


def encode(v):
    v2 = v * v
    v4 = v2 * v2
    return (v4 * v4 * v).astype(BF16)


def decode(w):
    w = w.astype(F32)
    return w * jnp.exp2(lax.log(jnp.maximum(jnp.abs(w), TINY)) * (-8.0 / 9.0 / math.log(2.0)))


def fetch(copies):
    for copy in copies:
        copy.start()
    return copies


def split(x):
    high = x.astype(BF16)
    return high, (x - high.astype(F32)).astype(BF16)


def dot(a, b):
    return lax.dot_general(a, b, (((1,), (0,)), ((), ())), preferred_element_type=F32)


def lane_shift(x, shift):
    width = x.shape[-1]
    shift = shift % width
    if shift == 0:
        return x
    if width % 128 == 0:
        return pltpu.roll(x, shift, x.ndim - 1)
    return jnp.concatenate([x[..., width - shift :], x[..., : width - shift]], -1)


class Pair:
    def __init__(self, re, im):
        self.re, self.im = re, im

    def __add__(self, o):
        return Pair(self.re + o.re, self.im + o.im)

    def __sub__(self, o):
        return Pair(self.re - o.re, self.im - o.im)

    def times(self, c, s):
        return Pair(self.re * c - self.im * s, self.re * s + self.im * c)


def butterfly(even, odd, k, n, sign):
    if k == 0:
        return even + odd, even - odd
    if 4 * k == n:
        plus = Pair(even.re - odd.im, even.im + odd.re)
        minus = Pair(even.re + odd.im, even.im - odd.re)
        return (plus, minus) if sign > 0 else (minus, plus)
    if 8 * k in (n, 3 * n):
        h = math.sqrt(0.5)
        a, b = (odd.re - odd.im) * h, (odd.re + odd.im) * h
        if sign > 0 and 8 * k == n:
            return Pair(even.re + a, even.im + b), Pair(even.re - a, even.im - b)
        if sign > 0:
            return Pair(even.re - b, even.im + a), Pair(even.re + b, even.im - a)
        if 8 * k == n:
            return Pair(even.re + b, even.im - a), Pair(even.re - b, even.im + a)
        return Pair(even.re - a, even.im - b), Pair(even.re + a, even.im + b)
    angle = sign * 2.0 * math.pi * k / n
    o = odd.times(math.cos(angle), math.sin(angle))
    return even + o, even - o


def small_dft(items, sign):
    n = len(items)
    if n == 1:
        return items
    even = small_dft(items[0::2], sign)
    odd = small_dft(items[1::2], sign)
    out = [None] * n
    for k in range(n // 2):
        out[k], out[k + n // 2] = butterfly(even[k], odd[k], k, n, sign)
    return out


def edge_slot(color, part):
    return 16 * color + 8 * part


def edges_kernel(feat, first_edge, second_edge, edge, sems):
    step = 16
    rows = feat.shape[1]
    copies = fetch(
        [
            pltpu.make_async_copy(feat.at[:, pl.ds(0, step), :], edge.at[0], sems.at[0]),
            pltpu.make_async_copy(feat.at[:, pl.ds(rows - step, step), :], edge.at[1], sems.at[1]),
        ]
    )
    for copy in copies:
        copy.wait()
    top = edge[0].astype(F32)[:, 0, :]
    bottom = edge[1].astype(F32)[:, step - 1, :]
    even = lax.axis_index("row") % 2 == 0
    first_edge[...] = jnp.where(even, bottom, top).astype(BF16)
    second_edge[...] = jnp.where(even, top, bottom).astype(BF16)


def edges(features):
    chans, rows, cols = features.shape
    vm = pl.BlockSpec(memory_space=pltpu.VMEM)
    return pl.pallas_call(
        edges_kernel,
        out_shape=[pltpu.VMEM((chans, cols), BF16)] * 2,
        in_specs=[pl.BlockSpec(memory_space=pltpu.HBM)],
        out_specs=[vm] * 2,
        scratch_shapes=[pltpu.VMEM((2, chans, 16, cols), BF16), pltpu.SemaphoreType.DMA((2,))],
        compiler_params=pltpu.CompilerParams(vmem_limit_bytes=VMEM_LIMIT),
        name="edges",
    )(pltpu.with_memory_space_constraint(features, pltpu.HBM))


def prepare_kernel(colors, chans, feat, weight, bias, tile, table, ring_table, bias_rows, taps, bias_in, sems):
    step = 16
    copies = fetch(
        [
            pltpu.make_async_copy(weight, taps, sems.at[0]),
            pltpu.make_async_copy(bias, bias_in, sems.at[1]),
        ]
        + [
            pltpu.make_async_copy(feat.at[pl.ds(i * (chans // 8), chans // 8)], tile.at[pl.ds(i * (chans // 8), chans // 8)], sems.at[2 + i])
            for i in range(8)
        ]
    )
    copies[0].wait()
    wide = chans * step
    c_of = lax.broadcasted_iota(jnp.int32, (chans, wide), 1) // step
    spread = (c_of == lax.broadcasted_iota(jnp.int32, (chans, wide), 0)).astype(F32).astype(BF16)
    x_in = lax.broadcasted_iota(jnp.int32, (step + 8, wide), 1) % step
    row = lax.broadcasted_iota(jnp.int32, (step + 8, wide), 0)
    masks = []
    for u in range(3):
        main = (row < step) & (x_in - row + 1 == u)
        if u == 0:
            main = main | ((row == step) & (x_in == step - 1))
        if u == 2:
            main = main | ((row == step + 7) & (x_in == 0))
        masks.append(main)
    sub = lax.broadcasted_iota(jnp.int32, (8, chans), 0)
    for o in range(colors):
        spreads = [dot(taps[o, u], spread) for u in range(3)]
        small = [taps[o, u].astype(F32) for u in range(3)]
        for v in range(3):
            total = jnp.zeros((step + 8, wide), F32)
            for u in range(3):
                total = total + jnp.where(masks[u], spreads[u][v : v + 1], 0.0)
            g = v * colors + o
            table[g * step : (g + 1) * step, :] = total[:step].astype(BF16)
            start = 3 * colors * step + 8 * g
            table[start : start + 8, :] = total[step:].astype(BF16)
            ring_table[0, 8 * g : 8 * g + 8, :] = jnp.where(sub == 0, small[0][v : v + 1], 0.0).astype(BF16)
            ring_table[1, 8 * g : 8 * g + 8, :] = jnp.where(sub == 7, small[2][v : v + 1], 0.0).astype(BF16)
    copies[1].wait()
    for o in range(colors):
        bias_rows[o : o + 1, :] = jnp.full((1, TILE), bias_in[o], F32)
    for copy in copies[2:]:
        copy.wait()


def prepare(features, conv_weight, bias):
    chans, rows, cols = features.shape
    colors = bias.shape[0]
    weight = conv_weight.transpose(0, 2, 3, 1)
    hbm = pl.BlockSpec(memory_space=pltpu.HBM)
    vm = pl.BlockSpec(memory_space=pltpu.VMEM)
    return pl.pallas_call(
        partial(prepare_kernel, colors, chans),
        out_shape=[
            pltpu.VMEM(features.shape, BF16),
            pltpu.VMEM((3 * colors * 24, chans * 16), BF16),
            pltpu.VMEM((2, 3 * colors * 8, chans), BF16),
            pltpu.VMEM((colors, TILE), F32),
        ],
        in_specs=[hbm] * 3,
        out_specs=[vm] * 4,
        scratch_shapes=[
            pltpu.VMEM(weight.shape, BF16),
            pltpu.SMEM(bias.shape, F32),
            pltpu.SemaphoreType.DMA((10,)),
        ],
        compiler_params=pltpu.CompilerParams(vmem_limit_bytes=VMEM_LIMIT),
        name="prepare",
    )(*(pltpu.with_memory_space_constraint(x, pltpu.HBM) for x in (features, weight, bias)))


def head_kernel(colors, chans, band, second_halo, first_halo, feat, table, ring_table, bias, out):
    peers = out.shape[0]
    step = 16
    per = band // step
    groups = 3 * colors
    main_rows = groups * step
    me = lax.axis_index("col")

    lane = lax.broadcasted_iota(jnp.int32, (1, TILE), 1)
    lane_half = lax.broadcasted_iota(jnp.int32, (1, HALF), 1)
    outer = (lane_half == 0) | (lane_half == HALF - 1)
    sub = lax.broadcasted_iota(jnp.int32, (8, 1), 0)

    first, last = sub == 0, sub == 7

    def ring_of(block):
        return [block[v * 8 * colors : (v + 1) * 8 * colors] for v in range(3)]

    def chunk(i):
        return feat[:, i * step : (i + 1) * step, :].reshape(chans * step, TILE)

    prods = [None] * (peers * per)
    rings = [None] * (peers * per + 2)
    even = lax.axis_index("row") % 2 == 0
    one, two = first_halo[...].astype(F32), second_halo[...].astype(F32)
    above = jnp.where(even, two, one).astype(BF16)
    below = jnp.where(even, one, two).astype(BF16)
    rings[0] = ring_of(dot(ring_table[0], above))
    rings[-1] = ring_of(dot(ring_table[1], below))

    def multiply(j):
        for i in range(j * per, (j + 1) * per):
            prods[i] = dot(table[...], chunk(i))
            rings[i + 1] = ring_of(prods[i][main_rows:])

    def finish(j):
        slot = me ^ j
        total = None
        for i in range(per):
            at = j * per + i
            extra = None
            for o in range(colors):
                q = []
                for v in range(3):
                    g = v * colors + o
                    main = prods[at][g * step : (g + 1) * step]
                    top = main[:8] + jnp.where(first, rings[at][v][8 * o : 8 * o + 8], 0.0)
                    bottom = main[8:] + jnp.where(last, rings[at + 2][v][8 * o : 8 * o + 8], 0.0)
                    q.append(jnp.concatenate([top, bottom], 0))
                r0 = pltpu.roll(q[0], 1, 1)
                r2 = pltpu.roll(q[2], TILE - 1, 1)
                own = q[1] + jnp.where(lane == 0, 0.0, r0) + jnp.where(lane == TILE - 1, 0.0, r2) + bias[o : o + 1, :]
                code = jnp.exp2(CODE * jnp.tanh(own)).astype(BF16)
                row = o * band + i * step
                for h in range(2):
                    start = h * colors * band + row
                    out[slot, start : start + step, :] = code[:, h * HALF : (h + 1) * HALF]
                cross = jnp.where(lane_half == 0, r0[:, :HALF], r2[:, HALF:])
                cross = pltpu.roll(jnp.where(outer, cross, 0.0), 2, 1)
                edges = jnp.where(lane_half == 0, own[:, :HALF], own[:, HALF:])
                edges = jnp.where(outer, edges, cross)
                high = edges.astype(BF16).astype(F32)
                both = high + pltpu.roll(edges - high, edge_slot(0, 1), 1)
                shift = edge_slot(o, 0) + 64 * i
                if shift:
                    both = pltpu.roll(both, shift, 1)
                extra = both if extra is None else extra + both
            total = extra if total is None else total + extra
        base = 2 * colors * band
        out[slot, base : base + step, :] = total.astype(BF16)

    multiply(0)
    for j in range(peers):
        if j + 1 < peers:
            multiply(j + 1)
        finish(j)


def head(prepared, second_halo, first_halo, band, peers):
    features, table, ring_table, bias = prepared
    chans, rows, cols = features.shape
    colors = bias.shape[0]
    vm = pl.BlockSpec(memory_space=pltpu.VMEM)
    return pl.pallas_call(
        partial(head_kernel, colors, chans, band),
        out_shape=pltpu.VMEM((peers, 2 * colors * band + 16, HALF), BF16),
        in_specs=[vm] * 6,
        out_specs=vm,
        compiler_params=pltpu.CompilerParams(vmem_limit_bytes=VMEM_LIMIT),
        name="conv_head",
    )(second_halo, first_halo, features, table, ring_table, bias)


def sending_order(peers):
    return [*range(peers - 2, 0, -2), *range(peers - 1, 0, -2), 0]


def forward_y_kernel(colors, band, parts, *refs):
    peers = len(refs) - 7
    matrix, tw_c, tw_s, _, out, coded, left = refs[peers:]
    for i, k in enumerate(sending_order(peers)):
        coded[lax.axis_index("col") ^ k] = refs[i][...]
    step = 16
    lane = lax.broadcasted_iota(jnp.int32, (1, HALF), 1)
    width = TILE // parts

    def spread(o):
        for r in range(0, band, step):
            edge = []
            for p in range(peers):
                base = 2 * colors * band
                block = coded[p, base : base + step, :].astype(F32)
                shift = edge_slot(o, 0) + 64 * (r // step)
                if shift:
                    block = pltpu.roll(block, HALF - shift, 1)
                edge.append(block + pltpu.roll(block, HALF - edge_slot(0, 1), 1))
            cross = [pltpu.roll(x, HALF - 2, 1) for x in edge]
            zero = jnp.zeros_like(cross[0])
            fixed = []
            for p in range(peers):
                before = cross[p - 1] if p > 0 else zero
                after = cross[p + 1] if p + 1 < peers else zero
                fixed.append(CODE * jnp.tanh(edge[p] + jnp.where(lane < HALF // 2, before, after)))
            items = []
            for p in range(peers):
                for h in range(2):
                    start = (h * colors + o) * band + r
                    t = log2(coded[p, start : start + step, :].astype(F32))
                    t = jnp.where(lane == (HALF - 1) * h, fixed[p], t)
                    items.append(Pair(*sincos_half(t, 4, 1.0 / CODE)))
            for k, z in enumerate(small_dft(items, -1)):
                if k:
                    z = z.times(tw_c[k : k + 1, :], -tw_s[k : k + 1, :])
                for part, x in enumerate((z.re, z.im)):
                    high, low = split(x)
                    for j, value in enumerate((high, low, high)):
                        to = slice((2 * j + part) * HALF, (2 * j + part + 1) * HALF)
                        left[o, k, r : r + step, to] = value

    def multiply(o):
        return dot(left[o].reshape(2 * peers * band, 3 * TILE), matrix[...])

    def store(o, acc):
        code = encode(acc)
        for k in range(2 * peers):
            for q in range(parts):
                out[parts * k + q, o * band : (o + 1) * band, :] = code[k * band : (k + 1) * band, q * width : (q + 1) * width]

    held = None
    for o in range(colors):
        spread(o)
        acc = multiply(o)
        if held is not None:
            store(o - 1, held)
        held = acc
    store(colors - 1, held)


def forward_y(blocks, colors, band, parts, table):
    peers = len(blocks)
    tw_c, tw_s = dft_np(2 * peers, HALF, peers * TILE)
    vm = pl.BlockSpec(memory_space=pltpu.VMEM)
    sm = pl.BlockSpec(memory_space=pltpu.SMEM)
    matrix = tall(interleaved(complex_np(-1), parts))
    return pl.pallas_call(
        partial(forward_y_kernel, colors, band, parts),
        out_shape=pltpu.VMEM((2 * peers * parts, colors * band, TILE // parts), BF16),
        in_specs=[vm] * (peers + 3) + [pl.BlockSpec(memory_space=pl.ANY)],
        out_specs=vm,
        scratch_shapes=[
            pltpu.VMEM((peers,) + blocks[0].shape, BF16),
            pltpu.VMEM((colors, 2 * peers, band, 3 * TILE), BF16),
        ],
        compiler_params=pltpu.CompilerParams(vmem_limit_bytes=VMEM_LIMIT),
        name="forward_y",
    )(*(blocks[k] for k in sending_order(peers)), jnp.asarray(matrix), jnp.asarray(tw_c, F32), jnp.asarray(tw_s, F32), table)


def transfer_kernel(sizes, wave, travel, out):
    height, width, parts, inner, block = sizes
    position = lax.axis_index("row") * lax.axis_size("col") + lax.axis_index("col")
    k0 = position // parts
    q = position % parts
    colors, n = out.shape[0] - 1, out.shape[1]
    shape = (HALF // 4, out.shape[4])
    lane = lax.broadcasted_iota(jnp.int32, shape, 1)
    ky = k0 + inner * (block * q + lane % block)
    sy = jnp.where(ky < width // 2, ky, ky - width).astype(F32) * (1.0 / width)
    sy2 = sy * sy
    for k in range(n):
        for i in range(4):
            rows = slice(i * HALF // 4, (i + 1) * HALF // 4)
            m = lax.broadcasted_iota(jnp.int32, shape, 0) + i * HALF // 4
            half = 2 * k + lane // block
            kx = half + (height // HALF) * m
            sx = jnp.where(kx < height // 2, kx, kx - height).astype(F32) * (1.0 / height)
            f2 = sx * sx + sy2
            for color in range(colors):
                a = wave[color]
                turns = travel[0] * f2 / (a + jnp.sqrt(a * a - f2))
                turns = turns - jnp.round(turns)
                c, s = sincos_half(turns, 5, 2.0)
                out[color, k, 0, rows, :] = c * (SHRINK / height)
                out[color, k, 1, rows, :] = s * (SHRINK / height)
            turns = (half * m).astype(F32) * (1.0 / height)
            c, s = sincos_half(turns - jnp.round(turns), 5, 2.0)
            out[colors, k, 0, rows, :] = c
            out[colors, k, 1, rows, :] = s


def transfer(inv_wavelength, distance, sizes):
    height, width, parts, inner, block = sizes
    colors = inv_wavelength.shape[0]
    sm = pl.BlockSpec(memory_space=pltpu.SMEM)
    n = height // TILE
    return pl.pallas_call(
        partial(transfer_kernel, sizes),
        out_shape=pltpu.VMEM((colors + 1, n, 2, HALF, 2 * block), F32),
        in_specs=[sm] * 2,
        out_specs=pl.BlockSpec(memory_space=pltpu.VMEM),
        compiler_params=pltpu.CompilerParams(vmem_limit_bytes=VMEM_LIMIT),
        name="transfer",
    )(inv_wavelength, distance)


def middle_kernel(coded, tables, matrix, out, before, after):
    colors, n = out.shape[1], tables.shape[1]
    width = coded.shape[-1]
    block = width // 2
    per = coded.shape[0] // (2 * n)
    band = coded.shape[2]
    twiddles = tables.at[colors]
    lane = lax.broadcasted_iota(jnp.int32, (1, width), 1)
    left = lane < block
    step = 16
    turn_c = [jnp.where(left, 1.0, math.cos(math.pi * a / n)) for a in range(n)]
    turn_s = [jnp.where(left, 0.0, math.sin(math.pi * a / n)) for a in range(n)]

    def put(right, k, rows, z, order):
        for part, x in zip(order, (z.re, z.im)):
            high, low = split(x)
            for j, value in enumerate((high, high, low)):
                to = (2 * j + part) * HALF
                right[to + rows.start : to + rows.stop, k * width : (k + 1) * width] = value

    def spread(color):
        for i in range(HALF // step):
            s, r = divmod(i * step, band)
            rows = slice(i * step, (i + 1) * step)
            items = []
            for a in range(n):
                x = decode(coded[per * a + s, color, r : r + step, :])
                y = decode(coded[per * (a + n) + s, color, r : r + step, :])
                u, v = x + y, x - y
                z = Pair(jnp.where(left, u, lane_shift(v, block)), jnp.where(left, lane_shift(u, block), v))
                if a:
                    z = z.times(turn_c[a], -turn_s[a])
                items.append(z)
            for k, z in enumerate(small_dft(items, -1)):
                put(before.at[color], k, rows, z.times(twiddles[k, 0, rows, :], -twiddles[k, 1, rows, :]), (0, 1))

    def multiply(right, color):
        return dot(matrix[...], right[color])

    def filtered(color, acc):
        for k in range(n):
            cols = slice(k * width, (k + 1) * width)
            for i in range(HALF // step):
                rows = slice(i * step, (i + 1) * step)
                z = Pair(acc[rows, cols], acc[HALF + rows.start : HALF + rows.stop, cols])
                put(after.at[color], k, rows, z.times(tables[color, k, 0, rows, :], -tables[color, k, 1, rows, :]), (1, 0))

    def store(color, acc):
        for i in range(HALF // step):
            s, r = divmod(i * step, band)
            rows = slice(i * step, (i + 1) * step)
            items = []
            for k in range(n):
                cols = slice(k * width, (k + 1) * width)
                z = Pair(acc[HALF + rows.start : HALF + rows.stop, cols], acc[rows, cols])
                items.append(z.times(twiddles[k, 0, rows, :], twiddles[k, 1, rows, :]))
            for a, z in enumerate(small_dft(items, 1)):
                if a:
                    z = z.times(turn_c[a], turn_s[a])
                u = jnp.where(left, z.re, lane_shift(z.im, block))
                v = jnp.where(left, lane_shift(z.re, block), z.im)
                out[per * a + s, color, r : r + step, :] = encode(u + v)
                out[per * (a + n) + s, color, r : r + step, :] = encode(u - v)

    ahead, back = {}, {}
    for tick in range(colors + 2):
        if tick < colors:
            spread(tick)
            ahead[tick] = multiply(before, tick)
        if 0 <= tick - 1 < colors:
            filtered(tick - 1, ahead.pop(tick - 1))
            back[tick - 1] = multiply(after, tick - 1)
        if tick >= 2:
            store(tick - 2, back.pop(tick - 2))


def middle(coded, table):
    groups, colors, band, width = coded.shape
    n = table.shape[1]
    vm = pl.BlockSpec(memory_space=pltpu.VMEM)
    forward = wide(complex_np(-1).T)
    return pl.pallas_call(
        middle_kernel,
        out_shape=jax.ShapeDtypeStruct(coded.shape, BF16),
        in_specs=[vm] * 3,
        out_specs=vm,
        scratch_shapes=[pltpu.VMEM((colors, 3 * TILE, n * width), BF16)] * 2,
        compiler_params=pltpu.CompilerParams(vmem_limit_bytes=VMEM_LIMIT),
        name="middle_x",
    )(*(pltpu.with_memory_space_constraint(x, pltpu.VMEM) for x in (coded, table, jnp.asarray(forward))))


def inverse_y_kernel(parts, coded, matrix, tw_c, tw_s, target, left, out, sems):
    inner = tw_c.shape[0]
    colors, band, width = coded.shape[1], coded.shape[2], coded.shape[3]
    outs = []
    step = 16

    def spread(o):
        for k in range(inner):
            for q in range(parts):
                high, low = split(decode(coded[parts * k + q, o]))
                for j, value in enumerate((high, low, high)):
                    left[o, k, :, j * TILE + q * width : j * TILE + (q + 1) * width] = value

    def multiply(o):
        return dot(left[o].reshape(inner * band, 3 * TILE), matrix[...])

    def store(o, acc):
        for r in range(0, band, step):
            items = []
            for k in range(inner):
                z = acc[k * band + r : k * band + r + step]
                items.append(Pair(z[:, :HALF], z[:, HALF:]).times(tw_c[k : k + 1, :], tw_s[k : k + 1, :]))
            for a, z in enumerate(small_dft(items, 1)):
                out[o, 0, r : r + step, a * HALF : (a + 1) * HALF] = z.re.astype(BF16)
                out[o, 1, r : r + step, a * HALF : (a + 1) * HALF] = z.im.astype(BF16)
        outs.extend(fetch([pltpu.make_async_copy(out.at[o], target.at[o], sems.at[o])]))

    held = None
    for o in range(colors):
        spread(o)
        acc = multiply(o)
        if held is not None:
            store(o - 1, held)
        held = acc
    store(colors - 1, held)
    for copy in outs:
        copy.wait()


def inverse_y(coded, parts):
    groups, colors, band, width = coded.shape
    inner = groups // parts
    tw_c, tw_s = (x / (SHRINK * inner * HALF) for x in dft_np(inner, HALF, inner * HALF))
    matrix = tall(np.ascontiguousarray(interleaved(complex_np(1).T.copy(), parts).T))
    hbm = pl.BlockSpec(memory_space=pltpu.HBM)
    vm = pl.BlockSpec(memory_space=pltpu.VMEM)
    return pl.pallas_call(
        partial(inverse_y_kernel, parts),
        out_shape=jax.ShapeDtypeStruct((colors, 2, band, inner * HALF), BF16),
        in_specs=[vm] * 4,
        out_specs=hbm,
        scratch_shapes=[
            pltpu.VMEM((colors, inner, band, 3 * TILE), BF16),
            pltpu.VMEM((colors, 2, band, inner * HALF), BF16),
            pltpu.SemaphoreType.DMA((colors,)),
        ],
        compiler_params=pltpu.CompilerParams(vmem_limit_bytes=VMEM_LIMIT),
        name="inverse_y",
    )(coded, jnp.asarray(matrix), jnp.asarray(tw_c, F32), jnp.asarray(tw_s, F32))


def per_device(features, conv_weight, bias, inv_wavelength, distance):
    mesh_rows = lax.axis_size("row")
    mesh_cols = lax.axis_size("col")
    groups = mesh_rows * mesh_cols
    chans, tile_rows, tile_cols = features.shape
    colors = conv_weight.shape[0]
    band = tile_rows // mesh_cols
    height = tile_rows * mesh_rows
    width = tile_cols * mesh_cols
    block = width // groups
    parts = mesh_rows // 2
    edge_one, edge_two = edges(features)
    tile, *prepared = prepare(features, conv_weight, bias)
    halos = []
    for start, edge in ((1, edge_two), (0, edge_one)):
        pairs = [(i, i + 1) for i in range(start, mesh_rows - 1, 2)]
        halos.append(lax.ppermute(edge, "row", pairs + [(j, i) for i, j in pairs]))
    bands = head((tile, *prepared), *halos, band, mesh_cols)
    blocks = [bands[0]] * mesh_cols
    for k in range(mesh_cols - 1, 0, -1):
        blocks[k] = lax.ppermute(bands[k], "col", [(i, i ^ k) for i in range(mesh_cols)])
    table = transfer(inv_wavelength, distance, (height, width, parts, 2 * mesh_cols, block))
    spectrum = forward_y(blocks, colors, band, parts, table)
    spectrum = lax.all_to_all(spectrum, ("row", "col"), split_axis=0, concat_axis=0, tiled=True)
    back = middle(spectrum.reshape(groups, colors, band, 2 * block), table)
    back = lax.all_to_all(back, ("row", "col"), split_axis=0, concat_axis=0, tiled=True)
    return inverse_y(back, parts)


def solution(mesh):
    in_specs = (P(None, "row", "col"), P(), P(), P(), P())
    out_specs = P(None, None, ("row", "col"), None)
    return jax.shard_map(
        per_device, mesh=mesh, in_specs=in_specs, out_specs=out_specs, check_vma=False
    )
```
